256 devices in a mesh: mp: 4 (over z_lo), dp: 4 (over z_hi, core), tensor: 16 (over x, y).
Axes of the slice: x: 4, y: 4, z: 8 (z_hi: 2, z_lo: 4; z = z_hi * 4 + z_lo), core: 2. Of those that a mesh axis runs over, the one named last changes fastest.
Arguments:
- tokens: bfloat16 [1024, 8192], P(('mp', 'tensor'), 'dp'), may hold values from -64 to 64
- norm_gain: float32 [2, 8192], replicated, may hold values from 0.5 to 1.5
- gate_weight: bfloat16 [2, 8192, 14336], P(None, 'dp', ('mp', 'tensor')), may hold values from -0.0625 to 0.0625
- up_weight: bfloat16 [2, 8192, 14336], P(None, 'dp', ('mp', 'tensor')), may hold values from -0.0625 to 0.0625
- down_weight: bfloat16 [2, 14336, 8192], P(None, 'mp', 'tensor'), may hold values from -0.046875 to 0.046875
- sketch: bfloat16 [8192, 512], P('tensor'), may hold values from -6 to 6
Outputs:
- final_basis: float32 [8192, 512], P('tensor', ('mp', 'dp'))
- projected: float32 [8192, 512], P('tensor', ('mp', 'dp'))
The draws below stay inside these ranges and needn't reach their ends.
All inputs are finite; a program needn't handle non-finite values.
Results may differ from the reference program's by a relative error of at most 0.04.
Values may be sent and summed in bfloat16 or wider, within the bound.
A program may use at most 128 MiB of HBM per device.

```python
import jax
import jax.numpy as jnp
from jax import lax

D = 8192
FFW = 14336
K = 512
TOKENS = 1024
N_DP = 4


def draw_tokens(key, part):
    first_key = jax.random.fold_in(key, 0)
    third_key = jax.random.fold_in(key, 2)
    normal_part = jnp.clip(jax.random.normal(first_key, (TOKENS, D), jnp.float32), -6.0, 6.0)
    position = jnp.arange(D, dtype=jnp.float32) / D
    jitter = jnp.exp(jax.random.uniform(third_key, (D,), jnp.float32, -0.5, 0.5))
    column_scale = jnp.exp(jnp.log(4.0) * (position - 0.5)) * jitter
    values = normal_part * column_scale[None, :]
    return values.astype(jnp.bfloat16)


def block_levels(key, dims, pieces, low, largest):
    level = 1.0
    for dim, shards_of in pieces:
        heights = jax.random.uniform(jax.random.fold_in(jax.random.fold_in(key, 6), dim), (shards_of,), jnp.float32, low / len(pieces), largest / len(pieces))
        level = level * jnp.repeat(jnp.exp(heights), dims[dim] // shards_of).reshape((-1,) + (1,) * (len(dims) - 1 - dim))
    return level


def gaussian(key, dims, spread, bound, pieces=(), kind=jnp.bfloat16):
    factor_of = block_levels(key, dims, pieces, -0.22, 0.18) if pieces else 1.0
    values = jax.random.normal(key, dims, jnp.float32) * spread * factor_of
    return jnp.minimum(jnp.maximum(values, -bound), bound).astype(kind)


def setup_inputs(seed: int = 0) -> dict:
    splits = jax.random.split(jax.random.key(seed), 7)
    tokens = draw_tokens(jax.random.fold_in(splits[6], 71), 0)
    norm_gain = jnp.clip(1.0 + 0.1 * jax.random.normal(splits[1], (2, D), jnp.float32), 0.5, 1.5)
    gate_weight = gaussian(splits[2], (2, D, FFW), D ** -0.5, 0.0625, ((1, 4), (2, 64)))
    up_weight = gaussian(splits[3], (2, D, FFW), D ** -0.5, 0.0625, ((1, 4), (2, 64)))
    down_weight = gaussian(splits[4], (2, FFW, D), FFW ** -0.5, 0.046875, ((1, 4), (2, 16)))
    sketch = gaussian(splits[5], (D, K), 1.0, 6.0, ((0, 16),))
    return dict(tokens=tokens, norm_gain=norm_gain, gate_weight=gate_weight, up_weight=up_weight, down_weight=down_weight, sketch=sketch)


EPSILON = 1e-05
HIGHEST = lax.Precision.HIGHEST

def orthonormal(matrix):
    gram_total = jnp.dot(matrix.T, matrix, precision=HIGHEST) / D
    lower_factor = jnp.linalg.cholesky(gram_total)
    return lax.linalg.triangular_solve(lower_factor, matrix, left_side=False, lower=True, transpose_a=True)

def sketch_product(left_acts, right_acts, matrix):
    inner_sums = jnp.dot(right_acts, matrix, precision=HIGHEST)
    return jnp.dot(left_acts.T, inner_sums, precision=HIGHEST) / TOKENS

def reference(tokens, norm_gain, gate_weight, up_weight, down_weight, sketch):
    values = tokens.astype(jnp.float32)
    inverse_root = lax.rsqrt(lax.optimization_barrier(jnp.sum(values * values, axis=1)) / D + EPSILON)
    normed = (values[None, :, :] * inverse_root[None, :, None] * norm_gain[:, None, :]).astype(jnp.bfloat16)
    block_width = D // N_DP

    def add_block(block_index, running):
        offset = (block_index * block_width).astype(jnp.int32)
        features_block = lax.dynamic_slice_in_dim(normed, offset, block_width, 2)
        gate_rows = lax.dynamic_slice_in_dim(gate_weight, offset, block_width, 1)
        up_rows = lax.dynamic_slice_in_dim(up_weight, offset, block_width, 1)
        outputs = []
        for copy_index in range(2):
            for weight_rows in (gate_rows, up_rows):
                product = jnp.dot(features_block[copy_index].astype(jnp.float32), weight_rows[copy_index].astype(jnp.float32), preferred_element_type=jnp.float32)
                rounded = lax.optimization_barrier(product.astype(jnp.bfloat16)).astype(jnp.float32)
                outputs.append(rounded)
        gate_sum = jnp.stack((outputs[0], outputs[2]))
        up_sum = jnp.stack((outputs[1], outputs[3]))
        return (running[0] + gate_sum, running[1] + up_sum)
    zeros_init = jnp.zeros((2, TOKENS, FFW), jnp.float32)
    gate_total, up_total = lax.fori_loop(0, N_DP, add_block, (zeros_init, zeros_init))
    hidden = (jax.nn.silu(gate_total) * up_total).astype(jnp.bfloat16)
    layer_out = [jnp.dot(hidden[copy_index].astype(jnp.float32), down_weight[copy_index].astype(jnp.float32), preferred_element_type=jnp.float32) for copy_index in range(2)]
    base_acts = layer_out[0]
    inst_acts = layer_out[1]
    first_basis = orthonormal(sketch_product(base_acts, inst_acts, sketch.astype(jnp.float32)))
    second_basis = orthonormal(sketch_product(inst_acts, base_acts, first_basis))
    final_basis = orthonormal(sketch_product(base_acts, inst_acts, second_basis))
    projected = sketch_product(inst_acts, base_acts, final_basis)
    return (final_basis, projected)
```

```python
import functools

import jax
import jax.numpy as jnp
from jax import lax
from jax.experimental import pallas as pl
from jax.experimental.pallas import tpu as pltpu
from jax.sharding import PartitionSpec as P

D = 8192
EPSILON = 1e-05
BLOCK = 128


def split(value):
    high = value.astype(jnp.bfloat16)
    return high, (value - high.astype(jnp.float32)).astype(jnp.bfloat16)


def mul(left, right, contract=((1,), (0,))):
    def dot(a, b):
        return lax.dot_general(a, b, (contract, ((), ())), preferred_element_type=jnp.float32)

    (a, a_low), (b, b_low) = left, right
    return dot(a, b) + (dot(a, b_low) + dot(a_low, b))


def inverse_factor(rows):
    lane = lax.broadcasted_iota(jnp.int32, (8, BLOCK), 1)
    sub = lax.broadcasted_iota(jnp.int32, (8, BLOCK), 0)
    rows = list(rows)
    for j in range(BLOCK):
        g, s = divmod(j, 8)
        at_j = lane == j
        below = sub > s
        row = rows[g][s : s + 1, :]
        inv = 1.0 / row[:, j : j + 1]
        scaled = jnp.where(at_j, 1.0, jnp.broadcast_to(row, (8, BLOCK))) * inv
        for h in range(g, BLOCK // 8):
            old = rows[h]
            col = jnp.broadcast_to(old[:, j : j + 1], (8, BLOCK))
            if h == g:
                new = jnp.where(at_j, 0.0, old) - col * scaled
                rows[h] = jnp.where(below, new, old)
            else:
                rows[h] = jnp.where(at_j, 0.0, old) - col * scaled
    out = []
    for g in range(BLOCK // 8):
        row_index = sub + 8 * g
        pivot = jnp.sum(jnp.where(lane == row_index, rows[g], 0.0), axis=1, keepdims=True)
        unit = jnp.where(lane == row_index, 1.0, jnp.where(lane < row_index, rows[g], 0.0))
        out.append(unit * lax.rsqrt(pivot))
    return jnp.concatenate(out, axis=0)


def orth_factor(gram, low_inv):
    n = gram.shape[0] // BLOCK
    low_inv[...] = jnp.zeros_like(low_inv)

    def step(k, carry):
        base = pl.multiple_of(k * BLOCK, BLOCK)
        here = pl.ds(base, BLOCK)
        rows = [gram[pl.ds(pl.multiple_of(base + 8 * g, 8), 8), here] for g in range(BLOCK // 8)]
        inv = inverse_factor(rows)
        inv_s = split(inv)
        panel = mul(inv_s, split(gram[here, :]))
        lane = lax.broadcasted_iota(jnp.int32, panel.shape, 1)
        panel = jnp.where(lane >= base + BLOCK, panel, 0.0)
        low_inv[here, here] = inv
        done = mul(inv_s, split(low_inv[here, :] * jnp.where(lane < base, 1.0, 0.0)))
        mine = jnp.where(lane < base, done, low_inv[here, :])
        low_inv[here, :] = mine
        panel_s = split(panel)
        gram[...] -= mul(panel_s, panel_s, ((0,), (0,)))
        low_inv[...] -= mul(panel_s, split(mine), ((0,), (0,)))
        return carry

    lax.fori_loop(0, n, step, 0)


def sketch_kernel(g0_ref, g1_ref, z_ref, out_ref, low_ref, gram, low_inv, high_z, low_z):
    tokens, rank = z_ref.shape

    def rank_step(which, g_ref):
        g_s = split(g_ref[...])
        z_s = split(z_ref[...]) if which == 0 else (high_z[...], low_z[...])
        h = mul(g_s, z_s)
        gram[...] = mul(z_s, split(h), ((0,), (0,))) * (2.0**-33)
        orth_factor(gram, low_inv)
        return h, z_s

    def advance(h):
        z = mul(split(h * (1.0 / 1024)), split(low_inv[...]), ((1,), (1,)))
        high, low = split(z)
        high_z[...] = high
        low_z[...] = low

    h, _ = rank_step(0, g0_ref)
    advance(h)
    h, _ = rank_step(1, g1_ref)
    advance(h)
    _, z_s = rank_step(2, g0_ref)
    basis = mul(z_s, split(low_inv[...]), ((1,), (1,))) * (1.0 / 1024)
    high, low = split(basis)
    out_ref[...] = high
    low_ref[...] = low


def sketch_call(gram0, gram1, z):
    tokens, rank = z.shape
    return pl.pallas_call(
        sketch_kernel,
        out_shape=(jax.ShapeDtypeStruct((tokens, rank), jnp.bfloat16),) * 2,
        in_specs=[pl.BlockSpec(memory_space=pltpu.VMEM)] * 3,
        out_specs=(pl.BlockSpec(memory_space=pltpu.VMEM),) * 2,
        scratch_shapes=[
            pltpu.VMEM((rank, rank), jnp.float32),
            pltpu.VMEM((rank, rank), jnp.float32),
            pltpu.VMEM((tokens, rank), jnp.bfloat16),
            pltpu.VMEM((tokens, rank), jnp.bfloat16),
        ],
        compiler_params=pltpu.CompilerParams(vmem_limit_bytes=56 * 2**20),
    )(gram0, gram1, z)


def project_block(block_normed, gate_weight, up_weight):
    gate_part = jnp.einsum(
        "crd,cdh->rch", block_normed, gate_weight, preferred_element_type=jnp.float32
    )
    up_part = jnp.einsum(
        "crd,cdh->rch", block_normed, up_weight, preferred_element_type=jnp.float32
    )
    return jnp.stack((gate_part, up_part), axis=2)


def on_device(tokens, norm_gain, gate_weight, up_weight, down_weight, sketch):
    feature_count = tokens.shape[1]
    offset = lax.axis_index("dp") * feature_count
    local_gain = lax.dynamic_slice_in_dim(norm_gain, offset, feature_count, 1)
    gathered = lax.all_gather(tokens, ("mp", "tensor"), axis=0, tiled=True)
    values = gathered.astype(jnp.float32)
    square_total = lax.psum(jnp.sum(values * values, axis=1), "dp")
    inverse_root = lax.rsqrt(square_total / D + EPSILON)
    normed = (values[None, :, :] * inverse_root[None, :, None] * local_gain[:, None, :]).astype(
        jnp.bfloat16
    )
    summed = lax.psum_scatter(
        project_block(normed, gate_weight, up_weight).astype(jnp.bfloat16),
        "dp",
        scatter_dimension=0,
        tiled=True,
    ).astype(jnp.float32)
    hidden = (jax.nn.silu(summed[:, :, 0]) * summed[:, :, 1]).astype(jnp.bfloat16)
    partial_out = jnp.einsum(
        "rch,chd->crd",
        lax.all_gather(hidden, "tensor", axis=2, tiled=True),
        down_weight,
        preferred_element_type=jnp.float32,
    )
    layer_out = lax.psum_scatter(partial_out, "mp", scatter_dimension=1, tiled=True)
    mine = layer_out.astype(jnp.bfloat16)
    acts = lax.all_gather(mine, ("dp", "mp"), axis=1, tiled=True)

    def against(left, right, dims):
        return lax.dot_general(left, right, (dims, ((), ())), preferred_element_type=jnp.float32)

    rows = jnp.concatenate(
        [
            against(mine[0], acts[0], ((1,), (1,))),
            against(mine[1], acts[1], ((1,), (1,))),
            against(mine[1], sketch, ((1,), (0,))),
        ],
        axis=1,
    )
    rows = lax.psum(rows, "tensor")
    full = lax.all_gather(rows, ("dp", "mp"), axis=0, tiled=True)
    count = acts.shape[1]
    gram0, gram1, z = full[:, :count], full[:, count : 2 * count], full[:, 2 * count :]
    high, low = sketch_call(gram0, gram1, z)
    share = high.shape[1] // lax.axis_size(("mp", "dp"))
    start = lax.axis_index(("mp", "dp")) * share
    high = lax.dynamic_slice_in_dim(high, start, share, 1)
    low = lax.dynamic_slice_in_dim(low, start, share, 1)
    last = mul(split(gram0), (high, low)) * (1.0 / count)
    basis_share = against(acts[0], high, ((0,), (0,))) + against(acts[0], low, ((0,), (0,)))
    last_high, last_low = split(last)
    projected = against(acts[1], last_high, ((0,), (0,))) + against(
        acts[1], last_low, ((0,), (0,))
    )
    return (basis_share, projected)


def solution(mesh):
    return jax.shard_map(
        on_device,
        mesh=mesh,
        in_specs=(
            P(("mp", "tensor"), "dp"),
            P(),
            P(None, "dp", ("mp", "tensor")),
            P(None, "dp", ("mp", "tensor")),
            P(None, "mp", "tensor"),
            P("tensor", None),
        ),
        out_specs=(P("tensor", ("mp", "dp")), P("tensor", ("mp", "dp"))),
        check_vma=False,
    )
```

```python
import functools

import jax
import jax.numpy as jnp
from jax import lax
from jax.experimental import pallas as pl
from jax.experimental.pallas import tpu as pltpu
from jax.sharding import PartitionSpec as P

D = 8192
EPSILON = 1e-05
BLOCK = 128


def split(value):
    high = value.astype(jnp.bfloat16)
    return high, (value - high.astype(jnp.float32)).astype(jnp.bfloat16)


def mul(left, right, contract=((1,), (0,))):
    def dot(a, b):
        return lax.dot_general(a, b, (contract, ((), ())), preferred_element_type=jnp.float32)

    (a, a_low), (b, b_low) = left, right
    return dot(a, b) + (dot(a, b_low) + dot(a_low, b))


def inverse_factor(rows):
    lane = lax.broadcasted_iota(jnp.int32, (8, BLOCK), 1)
    sub = lax.broadcasted_iota(jnp.int32, (8, BLOCK), 0)
    rows = list(rows)
    for j in range(BLOCK):
        g, s = divmod(j, 8)
        at_j = lane == j
        below = sub > s
        row = rows[g][s : s + 1, :]
        inv = 1.0 / row[:, j : j + 1]
        scaled = jnp.where(at_j, 1.0, jnp.broadcast_to(row, (8, BLOCK))) * inv
        for h in range(g, BLOCK // 8):
            old = rows[h]
            col = jnp.broadcast_to(old[:, j : j + 1], (8, BLOCK))
            if h == g:
                new = jnp.where(at_j, 0.0, old) - col * scaled
                rows[h] = jnp.where(below, new, old)
            else:
                rows[h] = jnp.where(at_j, 0.0, old) - col * scaled
    out = []
    for g in range(BLOCK // 8):
        row_index = sub + 8 * g
        pivot = jnp.sum(jnp.where(lane == row_index, rows[g], 0.0), axis=1, keepdims=True)
        unit = jnp.where(lane == row_index, 1.0, jnp.where(lane < row_index, rows[g], 0.0))
        out.append(unit * lax.rsqrt(pivot))
    return jnp.concatenate(out, axis=0)


def orth_factor(gram, low_inv):
    n = gram.shape[0] // BLOCK
    low_inv[...] = jnp.zeros_like(low_inv)

    def step(k, carry):
        base = pl.multiple_of(k * BLOCK, BLOCK)
        here = pl.ds(base, BLOCK)
        rows = [gram[pl.ds(pl.multiple_of(base + 8 * g, 8), 8), here] for g in range(BLOCK // 8)]
        inv = inverse_factor(rows)
        inv_s = split(inv)
        panel = mul(inv_s, split(gram[here, :]))
        lane = lax.broadcasted_iota(jnp.int32, panel.shape, 1)
        panel = jnp.where(lane >= base + BLOCK, panel, 0.0)
        low_inv[here, here] = inv
        done = mul(inv_s, split(low_inv[here, :] * jnp.where(lane < base, 1.0, 0.0)))
        mine = jnp.where(lane < base, done, low_inv[here, :])
        low_inv[here, :] = mine
        panel_s = split(panel)
        gram[...] -= mul(panel_s, panel_s, ((0,), (0,)))
        low_inv[...] -= mul(panel_s, split(mine), ((0,), (0,)))
        return carry

    lax.fori_loop(0, n, step, 0)


def sketch_kernel(g0_ref, g1_ref, z_ref, out_ref, low_ref, gram, low_inv, high_z, low_z):
    tokens, rank = z_ref.shape

    def rank_step(which, g_ref):
        g_s = split(g_ref[...])
        z_s = split(z_ref[...]) if which == 0 else (high_z[...], low_z[...])
        h = mul(g_s, z_s)
        gram[...] = mul(z_s, split(h), ((0,), (0,))) * (2.0**-33)
        orth_factor(gram, low_inv)
        return h, z_s

    def advance(h):
        z = mul(split(h * (1.0 / 1024)), split(low_inv[...]), ((1,), (1,)))
        high, low = split(z)
        high_z[...] = high
        low_z[...] = low

    h, _ = rank_step(0, g0_ref)
    advance(h)
    h, _ = rank_step(1, g1_ref)
    advance(h)
    _, z_s = rank_step(2, g0_ref)
    basis = mul(z_s, split(low_inv[...]), ((1,), (1,))) * (1.0 / 1024)
    high, low = split(basis)
    out_ref[...] = high
    low_ref[...] = low


def sketch_call(gram0, gram1, z):
    tokens, rank = z.shape
    return pl.pallas_call(
        sketch_kernel,
        out_shape=(jax.ShapeDtypeStruct((tokens, rank), jnp.bfloat16),) * 2,
        in_specs=[pl.BlockSpec(memory_space=pltpu.VMEM)] * 3,
        out_specs=(pl.BlockSpec(memory_space=pltpu.VMEM),) * 2,
        scratch_shapes=[
            pltpu.VMEM((rank, rank), jnp.float32),
            pltpu.VMEM((rank, rank), jnp.float32),
            pltpu.VMEM((tokens, rank), jnp.bfloat16),
            pltpu.VMEM((tokens, rank), jnp.bfloat16),
        ],
        compiler_params=pltpu.CompilerParams(vmem_limit_bytes=56 * 2**20),
    )(gram0, gram1, z)


MESH = pl.DeviceIdType.MESH
VMEM = pl.BlockSpec(memory_space=pltpu.VMEM)


class Sender:
    def __init__(self, send, recv):
        self.send, self.recv, self.all = send, recv, []

    def __call__(self, source, target, device):
        n = len(self.all)
        copy = pltpu.make_async_remote_copy(
            src_ref=source,
            dst_ref=target,
            send_sem=self.send.at[n],
            recv_sem=self.recv.at[n],
            device_id=device,
            device_id_type=MESH,
        )
        copy.start()
        self.all.append(copy)
        return copy

    def finish(self):
        for copy in self.all:
            copy.wait_send()


def greet(peers):
    barrier = pltpu.get_barrier_semaphore()
    for peer in peers:
        pl.semaphore_signal(barrier, inc=1, device_id=peer, device_id_type=MESH)
    pl.semaphore_wait(barrier, len(peers))


def grid_place():
    t = lax.axis_index("tensor")
    return t // 4, t % 4


def ring(send, block, upper, lower, me, toward):
    right, left = (me + 1) % 4, (me + 3) % 4
    from_left = send(block(me), block(me), toward(right))
    from_right = send(block(me), block(me), toward(left))

    def forward():
        from_left.wait_recv()
        first = send(upper(left), upper(left), toward(right))
        from_right.wait_recv()
        second = send(lower(right), lower(right), toward(left))
        return first, second

    return forward


def two_rings(send, piece_a, piece_b):
    for phase in range(2):
        a = ring(send, *piece_a(phase))
        b = ring(send, *piece_b(phase))
        pending = [*a(), *b()]
        for copy in pending:
            copy.wait_recv()


def along_x(y):
    return lambda i: {"tensor": i * 4 + y}


def along_y(x):
    return lambda i: {"tensor": x * 4 + i}


def xy_neighbours(x, y):
    return [
        {"tensor": ((x + 1) % 4) * 4 + y},
        {"tensor": ((x + 3) % 4) * 4 + y},
        {"tensor": x * 4 + (y + 1) % 4},
        {"tensor": x * 4 + (y + 3) % 4},
    ]


def tokens_kernel(x_ref, out, send_sem, recv_sem):
    x, y = grid_place()
    m = lax.axis_index("mp")
    mates = [{"mp": (m + d) % 4} for d in range(1, 4)]
    greet(mates + xy_neighbours(x, y))
    send = Sender(send_sem, recv_sem)
    rows = x_ref.shape[0]
    half = x_ref.shape[1] // 2
    mine = pl.ds(pl.multiple_of(m * rows, rows), rows)
    first = [send(x_ref, out.at[x, y, mine], mate) for mate in mates]
    out[x, y, mine] = x_ref[...]
    for copy in first:
        copy.wait_recv()
    count = 4 * rows
    a, b = pl.ds(0, half), pl.ds(half, half)
    up, down = pl.ds(0, count // 2), pl.ds(count // 2, count // 2)
    two, rest = pl.ds(0, 2), pl.ds(2, 2)

    def piece_a(phase):
        if phase == 0:
            return (
                lambda i: out.at[i, y, :, a],
                lambda i: out.at[i, y, up, a],
                lambda i: out.at[i, y, down, a],
                x,
                along_x(y),
            )
        return (
            lambda i: out.at[:, i, :, a],
            lambda i: out.at[two, i, :, a],
            lambda i: out.at[rest, i, :, a],
            y,
            along_y(x),
        )

    def piece_b(phase):
        if phase == 0:
            return (
                lambda i: out.at[x, i, :, b],
                lambda i: out.at[x, i, up, b],
                lambda i: out.at[x, i, down, b],
                y,
                along_y(x),
            )
        return (
            lambda i: out.at[i, :, :, b],
            lambda i: out.at[i, two, :, b],
            lambda i: out.at[i, rest, :, b],
            x,
            along_x(y),
        )

    two_rings(send, piece_a, piece_b)
    send.finish()


def remote_call(kernel, out_shape, copies, number, scratch=(), limit=48):
    return pl.pallas_call(
        kernel,
        out_shape=out_shape,
        out_specs=VMEM,
        scratch_shapes=[
            *scratch,
            pltpu.SemaphoreType.DMA((copies,)),
            pltpu.SemaphoreType.DMA((copies,)),
        ],
        compiler_params=pltpu.CompilerParams(
            collective_id=number, has_side_effects=True, vmem_limit_bytes=limit * 2**20
        ),
    )


def gather_tokens(tokens):
    rows, features = tokens.shape
    out = jax.ShapeDtypeStruct((4, 4, 4 * rows, features), tokens.dtype)
    return remote_call(tokens_kernel, out, 19, 0)(tokens)


def hidden_kernel(part, squares, out, near, near_sq, pair, pair_sq, far, far_sq, send_sem, recv_sem):
    x, y = grid_place()
    d = lax.axis_index("dp")
    z, core = d // 2, d % 2
    sibling, partner = {"dp": z * 2 + 1 - core}, {"dp": (1 - z) * 2 + core}
    greet([sibling, partner] + xy_neighbours(x, y))
    send = Sender(send_sem, recv_sem)
    other, mine = (1 - z) * 2, z * 2
    there = 1 - core
    first = send(part.at[other + there], near.at[1], sibling)
    first_sq = send(squares.at[other + there], near_sq.at[1], sibling)
    second = send(part.at[mine + there], near.at[0], sibling)
    second_sq = send(squares.at[mine + there], near_sq.at[0], sibling)
    units = out.shape[3]
    step = 32

    first_sq.wait_recv()
    pair_sq[...] = squares[other + core] + near_sq[1]
    across_sq = send(pair_sq, far_sq, partner)
    first.wait_recv()
    across = []
    for c in range(2):

        @pl.loop(0, 2 * units // step)
        def _(i):
            rows = pl.ds(pl.multiple_of(c * 2 * units + i * step, step), step)
            total = part[other + core, rows, :].astype(jnp.float32) + near[1, rows, :].astype(
                jnp.float32
            )
            pair[rows, :] = total.astype(jnp.bfloat16)

        rows = pl.ds(c * 2 * units, 2 * units)
        across.append(send(pair.at[rows], far.at[rows], partner))

    second_sq.wait_recv()
    across_sq.wait_recv()
    square_total = squares[mine + core] + near_sq[0] + far_sq[...]
    root = lax.rsqrt(square_total[0:1, :] / D + EPSILON)
    second.wait_recv()
    for c in range(2):
        across[c].wait_recv()

        @pl.loop(0, units // step)
        def _(i):
            def total(row):
                rows = pl.ds(pl.multiple_of(row + i * step, step), step)
                return (
                    part[mine + core, rows, :].astype(jnp.float32)
                    + near[0, rows, :].astype(jnp.float32)
                    + far[rows, :].astype(jnp.float32)
                ) * root

            gate = total(c * 2 * units)
            up = total(c * 2 * units + units)
            value = gate / (1.0 + jnp.exp(-gate)) * up
            rows = pl.ds(pl.multiple_of(i * step, step), step)
            out[c, x, y, rows, :] = value.astype(jnp.bfloat16)

    upper, lower = pl.ds(0, units // 2), pl.ds(units // 2, units // 2)
    two, rest = pl.ds(0, 2), pl.ds(2, 2)

    def piece_a(phase):
        if phase == 0:
            return (
                lambda i: out.at[0, i, y],
                lambda i: out.at[0, i, y, upper],
                lambda i: out.at[0, i, y, lower],
                x,
                along_x(y),
            )
        return (
            lambda i: out.at[0, :, i],
            lambda i: out.at[0, two, i],
            lambda i: out.at[0, rest, i],
            y,
            along_y(x),
        )

    def piece_b(phase):
        if phase == 0:
            return (
                lambda i: out.at[1, x, i],
                lambda i: out.at[1, x, i, upper],
                lambda i: out.at[1, x, i, lower],
                y,
                along_y(x),
            )
        return (
            lambda i: out.at[1, i],
            lambda i: out.at[1, i, two],
            lambda i: out.at[1, i, rest],
            x,
            along_x(y),
        )

    two_rings(send, piece_a, piece_b)
    send.finish()


def sum_and_gather_hidden(part, squares):
    _, rows, tokens = part.shape
    out = jax.ShapeDtypeStruct((2, 4, 4, rows // 4, tokens), jnp.bfloat16)
    scratch = [
        pltpu.VMEM((2, rows, tokens), jnp.bfloat16),
        pltpu.VMEM((2, 8, tokens), jnp.float32),
        pltpu.VMEM((rows, tokens), jnp.bfloat16),
        pltpu.VMEM((8, tokens), jnp.float32),
        pltpu.VMEM((rows, tokens), jnp.bfloat16),
        pltpu.VMEM((8, tokens), jnp.float32),
    ]
    return remote_call(hidden_kernel, out, 23, 1, scratch)(part, squares)


def acts_kernel(part, out, landed, send_sem, recv_sem):
    m, d = lax.axis_index("mp"), lax.axis_index("dp")
    zh, core = d // 2, d % 2
    z = zh * 4 + m
    mates = [{"mp": (m + k) % 4} for k in range(1, 4)]

    def at(chip):
        return {"mp": chip % 4, "dp": (chip // 4) * 2 + core}

    right, left = at((z + 1) % 8), at((z + 7) % 8)
    sibling = {"dp": zh * 2 + 1 - core}
    greet(mates + [right, left, sibling])
    send = Sender(send_sem, recv_sem)
    sums = [send(part.at[(m + k) % 4], landed.at[k - 1], mates[k - 1]) for k in range(1, 4)]
    for copy in sums:
        copy.wait_recv()

    for c in range(2):
        total = part[m, c].astype(jnp.float32)
        for k in range(3):
            total += landed[k, c].astype(jnp.float32)
        out[c, core * 8 + z] = total.astype(jnp.bfloat16)

    def block(chip):
        return out.at[:, core * 8 + chip]

    from_left = send(block(z), block(z), right)
    from_right = send(block(z), block(z), left)
    shared = [send(block(z), block(z), sibling)]
    for k in range(1, 4):
        before, after = (z + 8 - k) % 8, (z + k) % 8
        from_left.wait_recv()
        if k < 3:
            next_left = send(block(before), block(before), right)
        else:
            piece = out.at[0, core * 8 + before]
            next_left = send(piece, piece, right)
        from_right.wait_recv()
        if k < 3:
            next_right = send(block(after), block(after), left)
        else:
            piece = out.at[1, core * 8 + after]
            next_right = send(piece, piece, left)
        shared.append(send(block(before), block(before), sibling))
        shared.append(send(block(after), block(after), sibling))
        from_left, from_right = next_left, next_right
    from_left.wait_recv()
    from_right.wait_recv()
    far = (z + 4) % 8
    shared.append(send(block(far), block(far), sibling))
    for copy in shared:
        copy.wait_recv()
    send.finish()


def sum_and_gather_acts(part):
    _, copies, rows, features = part.shape
    out = jax.ShapeDtypeStruct((copies, 16, rows, features), jnp.bfloat16)
    scratch = [pltpu.VMEM((3, copies, rows, features), jnp.bfloat16)]
    return remote_call(acts_kernel, out, 19, 2, scratch)(part)


def rows_kernel(part, out, landed, send_sem, recv_sem):
    t = lax.axis_index("tensor")
    x, y = grid_place()
    m, d = lax.axis_index("mp"), lax.axis_index("dp")
    zh, core = d // 2, d % 2
    z = zh * 4 + m
    width = part.shape[3] // 2

    def column(index):
        return pl.ds(pl.multiple_of((index % 2) * width, 128), width)

    peers = [{"tensor": (t + k) % 16} for k in range(1, 16)]

    def at(chip):
        return {"mp": chip % 4, "dp": (chip // 4) * 2 + core}

    chips = [at((z + k) % 8) for k in range(1, 8)]
    sibling = {"dp": zh * 2 + 1 - core}
    greet(peers + chips + [sibling])
    send = Sender(send_sem, recv_sem)
    sums = []
    for k in range(1, 16):
        u = (t + k) % 16
        source = part.at[u // 4, (u % 4) // 2, :, column(u)]
        sums.append(send(source, landed.at[k - 1], peers[k - 1]))
    total = part[x, y // 2, :, column(y)]
    for k in range(15):
        sums[k].wait_recv()
        total += landed[k]
    mine = core * 8 + z
    out[mine, x, y // 2, :, column(y)] = total
    own = out.at[mine, x, y // 2, :, column(y)]
    spread = [send(own, own, chip) for chip in chips]
    for copy in spread:
        copy.wait_recv()

    low, high = pl.ds(core * 8, 4), pl.ds(core * 8 + 4, 4)
    low_a, low_b = pl.ds(core * 8, 2), pl.ds(core * 8 + 2, 2)
    high_a, high_b = pl.ds(core * 8 + 4, 2), pl.ds(core * 8 + 6, 2)
    two, rest = pl.ds(0, 2), pl.ds(2, 2)

    def cell(members, i, j):
        return out.at[members, i, j // 2, :, column(j)]

    def piece_a(phase):
        if phase == 0:
            return (
                lambda i: cell(low, i, y),
                lambda i: cell(low_a, i, y),
                lambda i: cell(low_b, i, y),
                x,
                along_x(y),
            )
        return (
            lambda j: cell(low, slice(None), j),
            lambda j: cell(low, two, j),
            lambda j: cell(low, rest, j),
            y,
            along_y(x),
        )

    def piece_b(phase):
        if phase == 0:
            return (
                lambda j: cell(high, x, j),
                lambda j: cell(high_a, x, j),
                lambda j: cell(high_b, x, j),
                y,
                along_y(x),
            )
        return (
            lambda i: out.at[high, i],
            lambda i: out.at[high_a, i],
            lambda i: out.at[high_b, i],
            x,
            along_x(y),
        )

    two_rings(send, piece_a, piece_b)
    half = out.at[pl.ds(core * 8, 8)]
    last = send(half, half, sibling)
    last.wait_recv()
    send.finish()


def sum_and_gather_rows(part):
    rows, width = part.shape
    out = jax.ShapeDtypeStruct((16, 4, 2, rows // 8, width), jnp.float32)
    scratch = [pltpu.VMEM((15, rows // 8, width // 2), jnp.float32)]
    full = remote_call(rows_kernel, out, 39, 3, scratch)(part.reshape(4, 2, rows // 8, width))
    return full.reshape(16 * rows, width)


def against(left, right, dims):
    return lax.dot_general(left, right, (dims, ((), ())), preferred_element_type=jnp.float32)


def on_device(tokens, norm_gain, gate_weight, up_weight, down_weight, sketch):
    feature_count = tokens.shape[1]
    offset = lax.axis_index("dp") * feature_count
    local_gain = lax.dynamic_slice_in_dim(norm_gain, offset, feature_count, 1)
    gathered = gather_tokens(tokens).reshape(-1, feature_count)
    count = gathered.shape[0]
    share_dp = lax.axis_size("dp")
    values = gathered.astype(jnp.float32)
    squares = jnp.sum(values * values, axis=1).reshape(share_dp, 1, count // share_dp)
    squares = jnp.broadcast_to(squares, (share_dp, 8, count // share_dp))
    parts = []
    for c in range(2):
        scaled = (values * local_gain[c]).astype(jnp.bfloat16)
        for weight in (gate_weight[c], up_weight[c]):
            parts.append(against(weight, scaled, ((0,), (1,))).astype(jnp.bfloat16))
    part = jnp.concatenate(parts, axis=0)
    part = part.reshape(part.shape[0], share_dp, -1).swapaxes(0, 1)
    hidden = sum_and_gather_hidden(part, squares)
    hidden = hidden.reshape(2, -1, hidden.shape[-1])
    partial_out = jnp.stack(
        [
            against(hidden[c], down_weight[c], ((0,), (0,))).astype(jnp.bfloat16)
            for c in range(2)
        ],
        axis=1,
    )
    share_mp = lax.axis_size("mp")
    partial_out = partial_out.reshape(share_mp, -1, 2, partial_out.shape[-1]).swapaxes(1, 2)
    blocks = sum_and_gather_acts(partial_out)
    acts = blocks.reshape(2, count, -1)
    d = lax.axis_index("dp")
    index = (d % 2) * 8 + (d // 2) * 4 + lax.axis_index("mp")
    mine = lax.dynamic_index_in_dim(blocks, index, 1, keepdims=False)
    rows = jnp.concatenate(
        [
            against(mine[0], acts[0], ((1,), (1,))),
            against(mine[1], acts[1], ((1,), (1,))),
            against(mine[1], sketch, ((1,), (0,))),
        ],
        axis=1,
    )
    full = sum_and_gather_rows(rows)
    gram0, gram1, z = full[:, :count], full[:, count : 2 * count], full[:, 2 * count :]
    high, low = sketch_call(gram0, gram1, z)
    share = high.shape[1] // lax.axis_size(("mp", "dp"))
    start = lax.axis_index(("mp", "dp")) * share
    high = lax.dynamic_slice_in_dim(high, start, share, 1)
    low = lax.dynamic_slice_in_dim(low, start, share, 1)
    last = mul(split(gram0), (high, low)) * (1.0 / count)
    basis_share = against(acts[0], high, ((0,), (0,))) + against(acts[0], low, ((0,), (0,)))
    last_high, last_low = split(last)
    projected = against(acts[1], last_high, ((0,), (0,))) + against(
        acts[1], last_low, ((0,), (0,))
    )
    return (basis_share, projected)


def solution(mesh):
    return jax.shard_map(
        on_device,
        mesh=mesh,
        in_specs=(
            P(("mp", "tensor"), "dp"),
            P(),
            P(None, "dp", ("mp", "tensor")),
            P(None, "dp", ("mp", "tensor")),
            P(None, "mp", "tensor"),
            P("tensor", None),
        ),
        out_specs=(P("tensor", ("mp", "dp")), P("tensor", ("mp", "dp"))),
        check_vma=False,
    )
```

```python
import functools

import jax
import jax.numpy as jnp
from jax import lax
from jax.experimental import pallas as pl
from jax.experimental.pallas import tpu as pltpu
from jax.sharding import PartitionSpec as P

D = 8192
EPSILON = 1e-05
BLOCK = 128


def split(value):
    high = value.astype(jnp.bfloat16)
    return high, (value - high.astype(jnp.float32)).astype(jnp.bfloat16)


def mul(left, right, contract=((1,), (0,))):
    def dot(a, b):
        return lax.dot_general(a, b, (contract, ((), ())), preferred_element_type=jnp.float32)

    (a, a_low), (b, b_low) = left, right
    return dot(a, b) + (dot(a, b_low) + dot(a_low, b))


def reciprocal(value):
    return 1.0 / value


def inverse_factor(rows):
    lane = lax.broadcasted_iota(jnp.int32, (8, BLOCK), 1)
    sub = lax.broadcasted_iota(jnp.int32, (8, BLOCK), 0)
    rows = list(rows)
    groups = BLOCK // 8

    def spread(value):
        return jnp.broadcast_to(value, (8, BLOCK))

    out = []
    for g in range(groups):
        own = (lane >= 8 * g) & (lane < 8 * g + 8)
        cols = [[spread(rows[h][:, 8 * g + k : 8 * g + k + 1]) for k in range(8)] for h in range(g, groups)]
        s = [[spread(cols[0][k][i : i + 1, :]) for k in range(i + 1)] for i in range(8)]
        lines = [
            jnp.where(own, (lane == 8 * g + k).astype(jnp.float32), spread(rows[g][k : k + 1, :]))
            for k in range(8)
        ]
        factor = [[None] * 8 for _ in range(8)]
        inv = [None] * 8
        for k in range(8):
            inv[k] = reciprocal(s[k][k])
            for i in range(k + 1, 8):
                factor[i][k] = s[i][k] * inv[k]
            for i in range(k + 1, 8):
                for n in range(k + 1, i + 1):
                    s[i][n] = s[i][n] - factor[i][k] * s[n][k]
        for k in range(8):
            for i in range(k + 1, 8):
                lines[i] = lines[i] - factor[i][k] * lines[k]
        solved = [lines[k] * inv[k] for k in range(8)]
        for i in range(7, 0, -1):
            for k in range(i):
                solved[k] = solved[k] - factor[i][k] * solved[i]
        for h in range(g + 1, groups):
            value = jnp.where(own, 0.0, rows[h])
            c = cols[h - g]
            first = (c[0] * solved[0] + c[1] * solved[1]) + (c[2] * solved[2] + c[3] * solved[3])
            second = (c[4] * solved[4] + c[5] * solved[5]) + (c[6] * solved[6] + c[7] * solved[7])
            rows[h] = value - (first + second)
        row = lines[0] * jnp.sqrt(inv[0])
        for k in range(1, 8):
            row = jnp.where(sub == k, lines[k] * jnp.sqrt(inv[k]), row)
        out.append(jnp.where(lane <= sub + 8 * g, row, 0.0))
    return jnp.concatenate(out, axis=0)


def orth_factor(gram, low_inv):
    n = gram.shape[0]
    low_inv[...] = jnp.zeros_like(low_inv)
    for base in range(0, n, BLOCK):
        end = base + BLOCK
        here, rest = pl.ds(base, BLOCK), pl.ds(end, n - end)
        inv = inverse_factor([gram[pl.ds(base + 8 * g, 8), here] for g in range(BLOCK // 8)])
        inv_s = split(inv)
        low_inv[here, here] = inv
        if base:
            before = pl.ds(0, base)
            low_inv[here, before] = mul(inv_s, split(low_inv[here, before]))
        if end < n:
            panel_s = split(mul(inv_s, split(gram[here, rest])))
            gram[rest, rest] -= mul(panel_s, panel_s, ((0,), (0,)))
            so_far = pl.ds(0, end)
            low_inv[rest, so_far] -= mul(panel_s, split(low_inv[here, so_far]), ((0,), (0,)))


def sketch_kernel(full, acts, basis_out, last_out, gram, low_inv, high_z, low_z):
    tokens = full.shape[0]
    rank = gram.shape[0]
    share = basis_out.shape[0]
    high, low = split(full[:, pl.ds(2 * tokens, rank)])
    high_z[...] = high
    low_z[...] = low

    def step(n, carry):
        g_s = split(full[:, pl.ds(pl.multiple_of((n % 2) * tokens, 128), tokens)])
        z_s = (high_z[...], low_z[...])
        h = mul(g_s, z_s)
        gram[...] = mul(z_s, split(h), ((0,), (0,))) * (2.0**-33)
        orth_factor(gram, low_inv)

        @pl.when(n < 2)
        def _():
            high, low = split(mul(split(h * (1.0 / 1024)), split(low_inv[...]), ((1,), (1,))))
            high_z[...] = high
            low_z[...] = low

        return carry

    lax.fori_loop(0, 3, step, 0)
    index = lax.axis_index("mp") * 4 + lax.axis_index("dp")
    rows = low_inv[pl.ds(pl.multiple_of(index * share, share), share), :]
    coeff = split(mul(split(rows), (high_z[...], low_z[...]), ((1,), (1,))) * (1.0 / 1024))
    last = split(mul(coeff, split(full[:, pl.ds(0, tokens)])) * (1.0 / 1024))

    def apply(pair, c):
        def dot(a):
            return jnp.dot(a, acts[c], preferred_element_type=jnp.float32)

        return dot(pair[0]) + dot(pair[1])

    basis_out[...] = apply(coeff, 0)
    last_out[...] = apply(last, 1)


def sketch_call(full, acts):
    tokens = full.shape[0]
    rank = full.shape[1] - 2 * tokens
    features = acts.shape[2]
    shape = jax.ShapeDtypeStruct((rank // 16, features), jnp.float32)
    return pl.pallas_call(
        sketch_kernel,
        out_shape=(shape, shape),
        in_specs=[pl.BlockSpec(memory_space=pltpu.VMEM)] * 2,
        out_specs=(pl.BlockSpec(memory_space=pltpu.VMEM),) * 2,
        scratch_shapes=[
            pltpu.VMEM((rank, rank), jnp.float32),
            pltpu.VMEM((rank, rank), jnp.float32),
            pltpu.VMEM((tokens, rank), jnp.bfloat16),
            pltpu.VMEM((tokens, rank), jnp.bfloat16),
        ],
        compiler_params=pltpu.CompilerParams(vmem_limit_bytes=56 * 2**20),
    )(full, acts)


MESH = pl.DeviceIdType.MESH
VMEM = pl.BlockSpec(memory_space=pltpu.VMEM)


class Sender:
    def __init__(self, send, recv):
        self.send, self.recv, self.all = send, recv, []

    def __call__(self, source, target, device):
        n = len(self.all)
        copy = pltpu.make_async_remote_copy(
            src_ref=source,
            dst_ref=target,
            send_sem=self.send.at[n],
            recv_sem=self.recv.at[n],
            device_id=device,
            device_id_type=MESH,
        )
        copy.start()
        self.all.append(copy)
        return copy

    def finish(self):
        for copy in self.all:
            copy.wait_send()


def greet(peers):
    barrier = pltpu.get_barrier_semaphore()
    for peer in peers:
        pl.semaphore_signal(barrier, inc=1, device_id=peer, device_id_type=MESH)
    pl.semaphore_wait(barrier, len(peers))


def grid_place():
    t = lax.axis_index("tensor")
    return t // 4, t % 4


def ring(send, block, upper, lower, me, toward):
    right, left = (me + 1) % 4, (me + 3) % 4
    from_left = send(block(me), block(me), toward(right))
    from_right = send(block(me), block(me), toward(left))

    def forward():
        from_left.wait_recv()
        first = send(upper(left), upper(left), toward(right))
        from_right.wait_recv()
        second = send(lower(right), lower(right), toward(left))
        return first, second

    return forward


def two_rings(send, piece_a, piece_b):
    for phase in range(2):
        a = ring(send, *piece_a(phase))
        b = ring(send, *piece_b(phase))
        pending = [*a(), *b()]
        for copy in pending:
            copy.wait_recv()


def along_x(y):
    return lambda i: {"tensor": i * 4 + y}


def along_y(x):
    return lambda i: {"tensor": x * 4 + i}


def xy_neighbours(x, y):
    return [
        {"tensor": ((x + 1) % 4) * 4 + y},
        {"tensor": ((x + 3) % 4) * 4 + y},
        {"tensor": x * 4 + (y + 1) % 4},
        {"tensor": x * 4 + (y + 3) % 4},
    ]


def tokens_kernel(x_ref, out, send_sem, recv_sem):
    x, y = grid_place()
    m = lax.axis_index("mp")
    mates = [{"mp": (m + d) % 4} for d in range(1, 4)]
    greet(mates + xy_neighbours(x, y))
    send = Sender(send_sem, recv_sem)
    rows = x_ref.shape[0]
    half = x_ref.shape[1] // 2
    mine = pl.ds(pl.multiple_of(m * rows, rows), rows)
    first = [send(x_ref, out.at[x, y, mine], mate) for mate in mates]
    out[x, y, mine] = x_ref[...]
    for copy in first:
        copy.wait_recv()
    count = 4 * rows
    a, b = pl.ds(0, half), pl.ds(half, half)
    up, down = pl.ds(0, count // 2), pl.ds(count // 2, count // 2)
    two, rest = pl.ds(0, 2), pl.ds(2, 2)

    def piece_a(phase):
        if phase == 0:
            return (
                lambda i: out.at[i, y, :, a],
                lambda i: out.at[i, y, up, a],
                lambda i: out.at[i, y, down, a],
                x,
                along_x(y),
            )
        return (
            lambda i: out.at[:, i, :, a],
            lambda i: out.at[two, i, :, a],
            lambda i: out.at[rest, i, :, a],
            y,
            along_y(x),
        )

    def piece_b(phase):
        if phase == 0:
            return (
                lambda i: out.at[x, i, :, b],
                lambda i: out.at[x, i, up, b],
                lambda i: out.at[x, i, down, b],
                y,
                along_y(x),
            )
        return (
            lambda i: out.at[i, :, :, b],
            lambda i: out.at[i, two, :, b],
            lambda i: out.at[i, rest, :, b],
            x,
            along_x(y),
        )

    two_rings(send, piece_a, piece_b)
    send.finish()


def remote_call(kernel, out_shape, copies, number, scratch=(), limit=48):
    return pl.pallas_call(
        kernel,
        out_shape=out_shape,
        out_specs=VMEM,
        scratch_shapes=[
            *scratch,
            pltpu.SemaphoreType.DMA((copies,)),
            pltpu.SemaphoreType.DMA((copies,)),
        ],
        compiler_params=pltpu.CompilerParams(
            collective_id=number, has_side_effects=True, vmem_limit_bytes=limit * 2**20
        ),
    )


def gather_tokens(tokens):
    rows, features = tokens.shape
    out = jax.ShapeDtypeStruct((4, 4, 4 * rows, features), tokens.dtype)
    return remote_call(tokens_kernel, out, 19, 0)(tokens)


def hidden_kernel(part, squares, out, near, near_sq, pair, pair_sq, far, far_sq, send_sem, recv_sem):
    x, y = grid_place()
    d = lax.axis_index("dp")
    z, core = d // 2, d % 2
    sibling, partner = {"dp": z * 2 + 1 - core}, {"dp": (1 - z) * 2 + core}
    greet([sibling, partner] + xy_neighbours(x, y))
    send = Sender(send_sem, recv_sem)
    units, tokens = out.shape[3], out.shape[4]
    step = 32

    def share(zh, side):
        return pl.ds(pl.multiple_of((zh * 2 + side) * tokens, 128), tokens)

    far_near, far_mine = share(1 - z, 1 - core), share(1 - z, core)
    own_near, own = share(z, 1 - core), share(z, core)
    first = send(part.at[:, far_near], near.at[1], sibling)
    first_sq = send(squares.at[:, far_near], near_sq.at[1], sibling)
    second = send(part.at[:, own_near], near.at[0], sibling)
    second_sq = send(squares.at[:, own_near], near_sq.at[0], sibling)

    first_sq.wait_recv()
    pair_sq[...] = squares[:, far_mine] + near_sq[1]
    across_sq = send(pair_sq, far_sq, partner)
    first.wait_recv()
    across = []
    for c in range(2):

        @pl.loop(0, 2 * units // step)
        def _(i):
            rows = pl.ds(pl.multiple_of(c * 2 * units + i * step, step), step)
            total = part[rows, far_mine].astype(jnp.float32) + near[1, rows, :].astype(
                jnp.float32
            )
            pair[rows, :] = total.astype(jnp.bfloat16)

        rows = pl.ds(c * 2 * units, 2 * units)
        across.append(send(pair.at[rows], far.at[rows], partner))

    second_sq.wait_recv()
    across_sq.wait_recv()
    square_total = squares[:, own] + near_sq[0] + far_sq[...]
    root = lax.rsqrt(square_total[0:1, :] / D + EPSILON)
    second.wait_recv()
    for c in range(2):
        across[c].wait_recv()

        @pl.loop(0, units // step)
        def _(i):
            def total(row):
                rows = pl.ds(pl.multiple_of(row + i * step, step), step)
                return (
                    part[rows, own].astype(jnp.float32)
                    + near[0, rows, :].astype(jnp.float32)
                    + far[rows, :].astype(jnp.float32)
                ) * root

            gate = total(c * 2 * units)
            up = total(c * 2 * units + units)
            value = gate / (1.0 + jnp.exp(-gate)) * up
            rows = pl.ds(pl.multiple_of(i * step, step), step)
            out[c, x, y, rows, :] = value.astype(jnp.bfloat16)

    upper, lower = pl.ds(0, units // 2), pl.ds(units // 2, units // 2)
    two, rest = pl.ds(0, 2), pl.ds(2, 2)

    def piece_a(phase):
        if phase == 0:
            return (
                lambda i: out.at[0, i, y],
                lambda i: out.at[0, i, y, upper],
                lambda i: out.at[0, i, y, lower],
                x,
                along_x(y),
            )
        return (
            lambda i: out.at[0, :, i],
            lambda i: out.at[0, two, i],
            lambda i: out.at[0, rest, i],
            y,
            along_y(x),
        )

    def piece_b(phase):
        if phase == 0:
            return (
                lambda i: out.at[1, x, i],
                lambda i: out.at[1, x, i, upper],
                lambda i: out.at[1, x, i, lower],
                y,
                along_y(x),
            )
        return (
            lambda i: out.at[1, i],
            lambda i: out.at[1, i, two],
            lambda i: out.at[1, i, rest],
            x,
            along_x(y),
        )

    two_rings(send, piece_a, piece_b)
    send.finish()


def sum_and_gather_hidden(part, squares):
    rows, tokens = part.shape[0], part.shape[1] // lax.axis_size("dp")
    out = jax.ShapeDtypeStruct((2, 4, 4, rows // 4, tokens), jnp.bfloat16)
    scratch = [
        pltpu.VMEM((2, rows, tokens), jnp.bfloat16),
        pltpu.VMEM((2, 8, tokens), jnp.float32),
        pltpu.VMEM((rows, tokens), jnp.bfloat16),
        pltpu.VMEM((8, tokens), jnp.float32),
        pltpu.VMEM((rows, tokens), jnp.bfloat16),
        pltpu.VMEM((8, tokens), jnp.float32),
    ]
    return remote_call(hidden_kernel, out, 23, 1, scratch)(part, squares)


def acts_kernel(part, out, landed, send_sem, recv_sem):
    m, d = lax.axis_index("mp"), lax.axis_index("dp")
    zh, core = d // 2, d % 2
    z = zh * 4 + m
    mates = [{"mp": (m + k) % 4} for k in range(1, 4)]

    def at(chip):
        return {"mp": chip % 4, "dp": (chip // 4) * 2 + core}

    right, left = at((z + 1) % 8), at((z + 7) % 8)
    sibling = {"dp": zh * 2 + 1 - core}
    greet(mates + [right, left, sibling])
    send = Sender(send_sem, recv_sem)
    sums = [send(part.at[(m + k) % 4], landed.at[k - 1], mates[k - 1]) for k in range(1, 4)]
    for copy in sums:
        copy.wait_recv()

    for c in range(2):
        total = part[m, c].astype(jnp.float32)
        for k in range(3):
            total += landed[k, c].astype(jnp.float32)
        out[c, core * 8 + z] = total.astype(jnp.bfloat16)

    def block(chip):
        return out.at[:, core * 8 + chip]

    from_left = send(block(z), block(z), right)
    from_right = send(block(z), block(z), left)
    shared = [send(block(z), block(z), sibling)]
    for k in range(1, 4):
        before, after = (z + 8 - k) % 8, (z + k) % 8
        from_left.wait_recv()
        if k < 3:
            next_left = send(block(before), block(before), right)
        else:
            piece = out.at[0, core * 8 + before]
            next_left = send(piece, piece, right)
        from_right.wait_recv()
        if k < 3:
            next_right = send(block(after), block(after), left)
        else:
            piece = out.at[1, core * 8 + after]
            next_right = send(piece, piece, left)
        shared.append(send(block(before), block(before), sibling))
        shared.append(send(block(after), block(after), sibling))
        from_left, from_right = next_left, next_right
    from_left.wait_recv()
    from_right.wait_recv()
    far = (z + 4) % 8
    shared.append(send(block(far), block(far), sibling))
    for copy in shared:
        copy.wait_recv()
    send.finish()


def sum_and_gather_acts(part):
    _, copies, rows, features = part.shape
    out = jax.ShapeDtypeStruct((copies, 16, rows, features), jnp.bfloat16)
    scratch = [pltpu.VMEM((3, copies, rows, features), jnp.bfloat16)]
    return remote_call(acts_kernel, out, 19, 2, scratch)(part)


def rows_kernel(part, out, landed, send_sem, recv_sem):
    t = lax.axis_index("tensor")
    x, y = grid_place()
    m, d = lax.axis_index("mp"), lax.axis_index("dp")
    zh, core = d // 2, d % 2
    z = zh * 4 + m
    width = part.shape[3] // 2

    def column(index):
        return pl.ds(pl.multiple_of((index % 2) * width, 128), width)

    peers = [{"tensor": (t + k) % 16} for k in range(1, 16)]

    def at(chip):
        return {"mp": chip % 4, "dp": (chip // 4) * 2 + core}

    chips = [at((z + k) % 8) for k in range(1, 8)]
    sibling = {"dp": zh * 2 + 1 - core}
    greet(peers + chips + [sibling])
    send = Sender(send_sem, recv_sem)
    sums = []
    for k in range(1, 16):
        u = (t + k) % 16
        source = part.at[u // 4, (u % 4) // 2, :, column(u)]
        sums.append(send(source, landed.at[k - 1], peers[k - 1]))
    total = part[x, y // 2, :, column(y)]
    for k in range(15):
        sums[k].wait_recv()
        total += landed[k]
    mine = core * 8 + z
    out[mine, x, y // 2, :, column(y)] = total
    own = out.at[mine, x, y // 2, :, column(y)]
    spread = [send(own, own, chip) for chip in chips]
    for copy in spread:
        copy.wait_recv()

    low, high = pl.ds(core * 8, 4), pl.ds(core * 8 + 4, 4)
    low_a, low_b = pl.ds(core * 8, 2), pl.ds(core * 8 + 2, 2)
    high_a, high_b = pl.ds(core * 8 + 4, 2), pl.ds(core * 8 + 6, 2)
    two, rest = pl.ds(0, 2), pl.ds(2, 2)

    def cell(members, i, j):
        return out.at[members, i, j // 2, :, column(j)]

    def piece_a(phase):
        if phase == 0:
            return (
                lambda i: cell(low, i, y),
                lambda i: cell(low_a, i, y),
                lambda i: cell(low_b, i, y),
                x,
                along_x(y),
            )
        return (
            lambda j: cell(low, slice(None), j),
            lambda j: cell(low, two, j),
            lambda j: cell(low, rest, j),
            y,
            along_y(x),
        )

    def piece_b(phase):
        if phase == 0:
            return (
                lambda j: cell(high, x, j),
                lambda j: cell(high_a, x, j),
                lambda j: cell(high_b, x, j),
                y,
                along_y(x),
            )
        return (
            lambda i: out.at[high, i],
            lambda i: out.at[high_a, i],
            lambda i: out.at[high_b, i],
            x,
            along_x(y),
        )

    two_rings(send, piece_a, piece_b)
    half = out.at[pl.ds(core * 8, 8)]
    last = send(half, half, sibling)
    last.wait_recv()
    send.finish()


def sum_and_gather_rows(part):
    rows, width = part.shape
    out = jax.ShapeDtypeStruct((16, 4, 2, rows // 8, width), jnp.float32)
    scratch = [pltpu.VMEM((15, rows // 8, width // 2), jnp.float32)]
    full = remote_call(rows_kernel, out, 39, 3, scratch)(part.reshape(4, 2, rows // 8, width))
    return full.reshape(16 * rows, width)


def against(left, right, dims):
    return lax.dot_general(left, right, (dims, ((), ())), preferred_element_type=jnp.float32)


def on_device(tokens, norm_gain, gate_weight, up_weight, down_weight, sketch):
    feature_count = tokens.shape[1]
    offset = lax.axis_index("dp") * feature_count
    local_gain = lax.dynamic_slice_in_dim(norm_gain, offset, feature_count, 1)
    gathered = gather_tokens(tokens).reshape(-1, feature_count)
    count = gathered.shape[0]
    values = gathered.astype(jnp.float32)
    squares = jnp.broadcast_to(jnp.sum(values * values, axis=1), (8, count))
    parts = []
    for c in range(2):
        scaled = (values * local_gain[c]).astype(jnp.bfloat16)
        for weight in (gate_weight[c], up_weight[c]):
            parts.append(against(weight, scaled, ((0,), (1,))).astype(jnp.bfloat16))
    part = jnp.concatenate(parts, axis=0)
    hidden = sum_and_gather_hidden(part, squares)
    hidden = hidden.reshape(2, -1, hidden.shape[-1])
    partial_out = jnp.stack(
        [
            against(hidden[c], down_weight[c], ((0,), (0,))).astype(jnp.bfloat16)
            for c in range(2)
        ],
        axis=1,
    )
    share_mp = lax.axis_size("mp")
    partial_out = partial_out.reshape(share_mp, -1, 2, partial_out.shape[-1]).swapaxes(1, 2)
    blocks = sum_and_gather_acts(partial_out)
    acts = blocks.reshape(2, count, -1)
    d = lax.axis_index("dp")
    index = (d % 2) * 8 + (d // 2) * 4 + lax.axis_index("mp")
    mine = lax.dynamic_index_in_dim(blocks, index, 1, keepdims=False)
    rows = jnp.concatenate(
        [
            against(mine[0], acts[0], ((1,), (1,))),
            against(mine[1], acts[1], ((1,), (1,))),
            against(mine[1], sketch, ((1,), (0,))),
        ],
        axis=1,
    )
    full = sum_and_gather_rows(rows)
    basis_share, projected = sketch_call(full, acts)
    return (basis_share.T, projected.T)


def solution(mesh):
    return jax.shard_map(
        on_device,
        mesh=mesh,
        in_specs=(
            P(("mp", "tensor"), "dp"),
            P(),
            P(None, "dp", ("mp", "tensor")),
            P(None, "dp", ("mp", "tensor")),
            P(None, "mp", "tensor"),
            P("tensor", None),
        ),
        out_specs=(P("tensor", ("mp", "dp")), P("tensor", ("mp", "dp"))),
        check_vma=False,
    )
```

```python
import functools

import jax
import jax.numpy as jnp
from jax import lax
from jax.experimental import pallas as pl
from jax.experimental.pallas import tpu as pltpu
from jax.sharding import PartitionSpec as P

D = 8192
EPSILON = 1e-05
BLOCK = 128


def split(value):
    high = value.astype(jnp.bfloat16)
    return high, (value - high.astype(jnp.float32)).astype(jnp.bfloat16)


def mul(left, right, contract=((1,), (0,))):
    def dot(a, b):
        return lax.dot_general(a, b, (contract, ((), ())), preferred_element_type=jnp.float32)

    (a, a_low), (b, b_low) = left, right
    return dot(a, b) + (dot(a, b_low) + dot(a_low, b))


def reciprocal(value):
    return 1.0 / value


def inverse_factor(rows):
    lane = lax.broadcasted_iota(jnp.int32, (8, BLOCK), 1)
    sub = lax.broadcasted_iota(jnp.int32, (8, BLOCK), 0)
    rows = list(rows)
    groups = BLOCK // 8

    def spread(value):
        return jnp.broadcast_to(value, (8, BLOCK))

    out = []
    for g in range(groups):
        own = (lane >= 8 * g) & (lane < 8 * g + 8)
        cols = [[spread(rows[h][:, 8 * g + k : 8 * g + k + 1]) for k in range(8)] for h in range(g + 1, min(g + 2, groups))]
        plain = [spread(rows[g][k : k + 1, :]) for k in range(8)]
        s = [
            [spread(plain[i][:, 8 * g + k : 8 * g + k + 1]) for k in range(i + 1)] for i in range(8)
        ]
        lines = [
            jnp.where(own, (lane == 8 * g + k).astype(jnp.float32), plain[k]) for k in range(8)
        ]
        factor = [[None] * 8 for _ in range(8)]
        inv = [None] * 8
        for k in range(8):
            inv[k] = reciprocal(s[k][k])
            for i in range(k + 1, 8):
                factor[i][k] = s[i][k] * inv[k]
            for i in range(k + 1, 8):
                for n in range(k + 1, i + 1):
                    s[i][n] = s[i][n] - factor[i][k] * s[n][k]
        for k in range(8):
            for i in range(k + 1, 8):
                lines[i] = lines[i] - factor[i][k] * lines[k]
        solved = [lines[k] * inv[k] for k in range(8)]
        for i in range(7, 0, -1):
            for k in range(i):
                solved[k] = solved[k] - factor[i][k] * solved[i]
        for h in range(g + 1, min(g + 2, groups)):
            value = jnp.where(own, 0.0, rows[h])
            c = cols[h - g - 1]
            first = (c[0] * solved[0] + c[1] * solved[1]) + (c[2] * solved[2] + c[3] * solved[3])
            second = (c[4] * solved[4] + c[5] * solved[5]) + (c[6] * solved[6] + c[7] * solved[7])
            rows[h] = value - (first + second)
        if g + 2 < groups:
            tight = solved[0]
            for k in range(1, 8):
                tight = jnp.where(sub == k, solved[k], tight)
            zero = jnp.zeros_like(tight)
            wide = jnp.concatenate([tight if n == g else zero for n in range(groups)], axis=0)
            tall = jnp.concatenate(rows[g + 2 :], axis=0)
            change = mul(split(tall), split(wide))
            for h in range(g + 2, groups):
                n = 8 * (h - g - 2)
                rows[h] = jnp.where(own, 0.0, rows[h]) - change[n : n + 8, :]
        row = lines[0] * jnp.sqrt(inv[0])
        for k in range(1, 8):
            row = jnp.where(sub == k, lines[k] * jnp.sqrt(inv[k]), row)
        out.append(jnp.where(lane <= sub + 8 * g, row, 0.0))
    return jnp.concatenate(out, axis=0)


def orth_factor(gram, low_inv):
    n = gram.shape[0]
    blocks = n // BLOCK
    low_inv[...] = jnp.zeros_like(low_inv)
    at = [pl.ds(k * BLOCK, BLOCK) for k in range(blocks)]

    def diagonal(k):
        return [gram[pl.ds(k * BLOCK + 8 * g, 8), at[k]] for g in range(BLOCK // 8)]

    inv = inverse_factor(diagonal(0))
    for k in range(blocks):
        inv_s = split(inv)
        low_inv[at[k], at[k]] = inv
        panel = {}
        if k + 1 < blocks:
            panel[k + 1] = split(mul(inv_s, split(gram[at[k], at[k + 1]])))
            gram[at[k + 1], at[k + 1]] -= mul(panel[k + 1], panel[k + 1], ((0,), (0,)))
            following = inverse_factor(diagonal(k + 1))
        if k:
            before = pl.ds(0, k * BLOCK)
            low_inv[at[k], before] = mul(inv_s, split(low_inv[at[k], before]))
        so_far = pl.ds(0, (k + 1) * BLOCK)
        mine = split(low_inv[at[k], so_far])
        for i in range(k + 1, blocks):
            if i not in panel:
                panel[i] = split(mul(inv_s, split(gram[at[k], at[i]])))
            low_inv[at[i], so_far] -= mul(panel[i], mine, ((0,), (0,)))
            for j in range(i, blocks):
                if j not in panel:
                    panel[j] = split(mul(inv_s, split(gram[at[k], at[j]])))
                if (i, j) != (k + 1, k + 1):
                    gram[at[i], at[j]] -= mul(panel[i], panel[j], ((0,), (0,)))
        if k + 1 < blocks:
            inv = following


def sketch_kernel(full, acts, basis_out, last_out, gram, low_inv, high_z, low_z):
    tokens = full.shape[0]
    rank = gram.shape[0]
    share = basis_out.shape[0]
    high, low = split(full[:, pl.ds(2 * tokens, rank)])
    high_z[...] = high
    low_z[...] = low

    def step(n, carry):
        g_s = split(full[:, pl.ds(pl.multiple_of((n % 2) * tokens, 128), tokens)])
        z_s = (high_z[...], low_z[...])
        h = mul(g_s, z_s)
        gram[...] = mul(z_s, split(h), ((0,), (0,))) * (2.0**-33)
        orth_factor(gram, low_inv)

        @pl.when(n < 2)
        def _():
            high, low = split(mul(split(h * (1.0 / 1024)), split(low_inv[...]), ((1,), (1,))))
            high_z[...] = high
            low_z[...] = low

        return carry

    lax.fori_loop(0, 3, step, 0)
    index = lax.axis_index("mp") * 4 + lax.axis_index("dp")
    rows = low_inv[pl.ds(pl.multiple_of(index * share, share), share), :]
    coeff = split(mul(split(rows), (high_z[...], low_z[...]), ((1,), (1,))) * (1.0 / 1024))
    last = split(mul(coeff, split(full[:, pl.ds(0, tokens)])) * (1.0 / 1024))

    def apply(pair, c):
        def dot(a):
            return jnp.dot(a, acts[c], preferred_element_type=jnp.float32)

        return dot(pair[0]) + dot(pair[1])

    basis_out[...] = apply(coeff, 0)
    last_out[...] = apply(last, 1)


def sketch_call(full, acts):
    tokens = full.shape[0]
    rank = full.shape[1] - 2 * tokens
    features = acts.shape[2]
    shape = jax.ShapeDtypeStruct((rank // 16, features), jnp.float32)
    return pl.pallas_call(
        sketch_kernel,
        out_shape=(shape, shape),
        in_specs=[pl.BlockSpec(memory_space=pltpu.VMEM)] * 2,
        out_specs=(pl.BlockSpec(memory_space=pltpu.VMEM),) * 2,
        scratch_shapes=[
            pltpu.VMEM((rank, rank), jnp.float32),
            pltpu.VMEM((rank, rank), jnp.float32),
            pltpu.VMEM((tokens, rank), jnp.bfloat16),
            pltpu.VMEM((tokens, rank), jnp.bfloat16),
        ],
        compiler_params=pltpu.CompilerParams(vmem_limit_bytes=56 * 2**20),
    )(full, acts)


MESH = pl.DeviceIdType.MESH
VMEM = pl.BlockSpec(memory_space=pltpu.VMEM)


class Sender:
    def __init__(self, send, recv):
        self.send, self.recv, self.all = send, recv, []

    def __call__(self, source, target, device):
        n = len(self.all)
        copy = pltpu.make_async_remote_copy(
            src_ref=source,
            dst_ref=target,
            send_sem=self.send.at[n],
            recv_sem=self.recv.at[n],
            device_id=device,
            device_id_type=MESH,
        )
        copy.start()
        self.all.append(copy)
        return copy

    def finish(self):
        for copy in self.all:
            copy.wait_send()


def greet(peers):
    barrier = pltpu.get_barrier_semaphore()
    for peer in peers:
        pl.semaphore_signal(barrier, inc=1, device_id=peer, device_id_type=MESH)
    pl.semaphore_wait(barrier, len(peers))


def grid_place():
    t = lax.axis_index("tensor")
    return t // 4, t % 4


def ring(send, block, upper, lower, me, toward):
    right, left = (me + 1) % 4, (me + 3) % 4
    from_left = send(block(me), block(me), toward(right))
    from_right = send(block(me), block(me), toward(left))

    def forward():
        from_left.wait_recv()
        first = send(upper(left), upper(left), toward(right))
        from_right.wait_recv()
        second = send(lower(right), lower(right), toward(left))
        return first, second

    return forward


def two_rings(send, piece_a, piece_b):
    for phase in range(2):
        a = ring(send, *piece_a(phase))
        b = ring(send, *piece_b(phase))
        pending = [*a(), *b()]
        for copy in pending:
            copy.wait_recv()


def along_x(y):
    return lambda i: {"tensor": i * 4 + y}


def along_y(x):
    return lambda i: {"tensor": x * 4 + i}


def xy_neighbours(x, y):
    return [
        {"tensor": ((x + 1) % 4) * 4 + y},
        {"tensor": ((x + 3) % 4) * 4 + y},
        {"tensor": x * 4 + (y + 1) % 4},
        {"tensor": x * 4 + (y + 3) % 4},
    ]


def tokens_kernel(x_ref, out, send_sem, recv_sem):
    x, y = grid_place()
    m = lax.axis_index("mp")
    mates = [{"mp": (m + d) % 4} for d in range(1, 4)]
    greet(mates + xy_neighbours(x, y))
    send = Sender(send_sem, recv_sem)
    rows = x_ref.shape[0]
    half = x_ref.shape[1] // 2
    mine = pl.ds(pl.multiple_of(m * rows, rows), rows)
    first = [send(x_ref, out.at[x, y, mine], mate) for mate in mates]
    out[x, y, mine] = x_ref[...]
    for copy in first:
        copy.wait_recv()
    count = 4 * rows
    a, b = pl.ds(0, half), pl.ds(half, half)
    up, down = pl.ds(0, count // 2), pl.ds(count // 2, count // 2)
    two, rest = pl.ds(0, 2), pl.ds(2, 2)

    def piece_a(phase):
        if phase == 0:
            return (
                lambda i: out.at[i, y, :, a],
                lambda i: out.at[i, y, up, a],
                lambda i: out.at[i, y, down, a],
                x,
                along_x(y),
            )
        return (
            lambda i: out.at[:, i, :, a],
            lambda i: out.at[two, i, :, a],
            lambda i: out.at[rest, i, :, a],
            y,
            along_y(x),
        )

    def piece_b(phase):
        if phase == 0:
            return (
                lambda i: out.at[x, i, :, b],
                lambda i: out.at[x, i, up, b],
                lambda i: out.at[x, i, down, b],
                y,
                along_y(x),
            )
        return (
            lambda i: out.at[i, :, :, b],
            lambda i: out.at[i, two, :, b],
            lambda i: out.at[i, rest, :, b],
            x,
            along_x(y),
        )

    two_rings(send, piece_a, piece_b)
    send.finish()


def remote_call(kernel, out_shape, copies, number, scratch=(), limit=48):
    return pl.pallas_call(
        kernel,
        out_shape=out_shape,
        out_specs=VMEM,
        scratch_shapes=[
            *scratch,
            pltpu.SemaphoreType.DMA((copies,)),
            pltpu.SemaphoreType.DMA((copies,)),
        ],
        compiler_params=pltpu.CompilerParams(
            collective_id=number, has_side_effects=True, vmem_limit_bytes=limit * 2**20
        ),
    )


def gather_tokens(tokens):
    rows, features = tokens.shape
    out = jax.ShapeDtypeStruct((4, 4, 4 * rows, features), tokens.dtype)
    return remote_call(tokens_kernel, out, 19, 0)(tokens)


def hidden_kernel(part, squares, out, near, near_sq, pair, pair_sq, far, far_sq, send_sem, recv_sem):
    x, y = grid_place()
    d = lax.axis_index("dp")
    z, core = d // 2, d % 2
    sibling, partner = {"dp": z * 2 + 1 - core}, {"dp": (1 - z) * 2 + core}
    greet([sibling, partner] + xy_neighbours(x, y))
    send = Sender(send_sem, recv_sem)
    units, tokens = out.shape[3], out.shape[4]
    chunk = tokens // 2
    step = 32

    def share(zh, side, h=None):
        start = (zh * 2 + side) * tokens
        if h is None:
            return pl.ds(pl.multiple_of(start, 128), tokens)
        return pl.ds(pl.multiple_of(start + h * chunk, 128), chunk)

    first_sq = send(squares.at[:, share(1 - z, 1 - core)], near_sq.at[1], sibling)
    first = [
        send(part.at[:, share(1 - z, 1 - core, h)], near.at[1, h], sibling) for h in range(2)
    ]
    second_sq = send(squares.at[:, share(z, 1 - core)], near_sq.at[0], sibling)
    second = [send(part.at[:, share(z, 1 - core, h)], near.at[0, h], sibling) for h in range(2)]

    first_sq.wait_recv()
    pair_sq[...] = squares[:, share(1 - z, core)] + near_sq[1]
    across_sq = send(pair_sq, far_sq, partner)
    across = []
    for h in range(2):
        first[h].wait_recv()

        @pl.loop(0, 4 * units // step)
        def _(i):
            rows = pl.ds(pl.multiple_of(i * step, step), step)
            total = part[rows, share(1 - z, core, h)].astype(jnp.float32) + near[
                1, h, rows, :
            ].astype(jnp.float32)
            pair[h, rows, :] = total.astype(jnp.bfloat16)

        across.append(send(pair.at[h], far.at[h], partner))

    second_sq.wait_recv()
    across_sq.wait_recv()
    square_total = squares[:, share(z, core)] + near_sq[0] + far_sq[...]
    root = lax.rsqrt(square_total[0:1, :] / D + EPSILON)

    def activate(h):
        second[h].wait_recv()
        across[h].wait_recv()
        lanes = pl.ds(h * chunk, chunk)
        scale = root[:, h * chunk : (h + 1) * chunk]
        for c in range(2):

            @pl.loop(0, units // step)
            def _(i):
                def total(row):
                    rows = pl.ds(pl.multiple_of(row + i * step, step), step)
                    return (
                        part[rows, share(z, core, h)].astype(jnp.float32)
                        + near[0, h, rows, :].astype(jnp.float32)
                        + far[h, rows, :].astype(jnp.float32)
                    ) * scale

                gate = total(c * 2 * units)
                up = total(c * 2 * units + units)
                value = gate / (1.0 + jnp.exp(-gate)) * up
                rows = pl.ds(pl.multiple_of(i * step, step), step)
                out[c, x, y, rows, lanes] = value.astype(jnp.bfloat16)

    upper, lower = pl.ds(0, units // 2), pl.ds(units // 2, units // 2)
    every = slice(None)
    two, rest = pl.ds(0, 2), pl.ds(2, 2)

    def start(h, phase):
        lanes = pl.ds(h * chunk, chunk)
        if phase == 0:
            return (
                ring(
                    send,
                    lambda i: out.at[0, i, y, :, lanes],
                    lambda i: out.at[0, i, y, upper, lanes],
                    lambda i: out.at[0, i, y, lower, lanes],
                    x,
                    along_x(y),
                ),
                ring(
                    send,
                    lambda i: out.at[1, x, i, :, lanes],
                    lambda i: out.at[1, x, i, upper, lanes],
                    lambda i: out.at[1, x, i, lower, lanes],
                    y,
                    along_y(x),
                ),
            )
        return (
            ring(
                send,
                lambda i: out.at[0, every, i, :, lanes],
                lambda i: out.at[0, two, i, :, lanes],
                lambda i: out.at[0, rest, i, :, lanes],
                y,
                along_y(x),
            ),
            ring(
                send,
                lambda i: out.at[1, i, every, :, lanes],
                lambda i: out.at[1, i, two, :, lanes],
                lambda i: out.at[1, i, rest, :, lanes],
                x,
                along_x(y),
            ),
        )

    def forward(pair_of_rings):
        return [copy for one in pair_of_rings for copy in one()]

    def settle(copies):
        for copy in copies:
            copy.wait_recv()

    activate(0)
    rings = start(0, 0)
    settle(forward(rings))
    early = start(0, 1)
    activate(1)
    rings = start(1, 0)
    tail = forward(early)
    settle(forward(rings))
    tail += forward(start(1, 1))
    settle(tail)
    send.finish()


def sum_and_gather_hidden(part, squares):
    rows, tokens = part.shape[0], part.shape[1] // lax.axis_size("dp")
    out = jax.ShapeDtypeStruct((2, 4, 4, rows // 4, tokens), jnp.bfloat16)
    scratch = [
        pltpu.VMEM((2, 2, rows, tokens // 2), jnp.bfloat16),
        pltpu.VMEM((2, 8, tokens), jnp.float32),
        pltpu.VMEM((2, rows, tokens // 2), jnp.bfloat16),
        pltpu.VMEM((8, tokens), jnp.float32),
        pltpu.VMEM((2, rows, tokens // 2), jnp.bfloat16),
        pltpu.VMEM((8, tokens), jnp.float32),
    ]
    return remote_call(hidden_kernel, out, 41, 1, scratch)(part, squares)


def acts_kernel(part, out, landed, send_sem, recv_sem):
    m, d = lax.axis_index("mp"), lax.axis_index("dp")
    zh, core = d // 2, d % 2
    z = zh * 4 + m
    mates = [{"mp": (m + k) % 4} for k in range(1, 4)]

    def at(chip):
        return {"mp": chip % 4, "dp": (chip // 4) * 2 + core}

    right, left = at((z + 1) % 8), at((z + 7) % 8)
    sibling = {"dp": zh * 2 + 1 - core}
    greet(mates + [right, left, sibling])
    send = Sender(send_sem, recv_sem)
    sums = [send(part.at[(m + k) % 4], landed.at[k - 1], mates[k - 1]) for k in range(1, 4)]
    for copy in sums:
        copy.wait_recv()

    for c in range(2):
        total = part[m, c].astype(jnp.float32)
        for k in range(3):
            total += landed[k, c].astype(jnp.float32)
        out[c, core * 8 + z] = total.astype(jnp.bfloat16)

    def block(chip):
        return out.at[:, core * 8 + chip]

    from_left = send(block(z), block(z), right)
    from_right = send(block(z), block(z), left)
    shared = [send(block(z), block(z), sibling)]
    for k in range(1, 4):
        before, after = (z + 8 - k) % 8, (z + k) % 8
        from_left.wait_recv()
        if k < 3:
            next_left = send(block(before), block(before), right)
        else:
            piece = out.at[0, core * 8 + before]
            next_left = send(piece, piece, right)
        from_right.wait_recv()
        if k < 3:
            next_right = send(block(after), block(after), left)
        else:
            piece = out.at[1, core * 8 + after]
            next_right = send(piece, piece, left)
        shared.append(send(block(before), block(before), sibling))
        shared.append(send(block(after), block(after), sibling))
        from_left, from_right = next_left, next_right
    from_left.wait_recv()
    from_right.wait_recv()
    far = (z + 4) % 8
    shared.append(send(block(far), block(far), sibling))
    for copy in shared:
        copy.wait_recv()
    send.finish()


def sum_and_gather_acts(part):
    _, copies, rows, features = part.shape
    out = jax.ShapeDtypeStruct((copies, 16, rows, features), jnp.bfloat16)
    scratch = [pltpu.VMEM((3, copies, rows, features), jnp.bfloat16)]
    return remote_call(acts_kernel, out, 19, 2, scratch)(part)


def rows_kernel(part, out, landed, send_sem, recv_sem):
    t = lax.axis_index("tensor")
    x, y = grid_place()
    m, d = lax.axis_index("mp"), lax.axis_index("dp")
    zh, core = d // 2, d % 2
    z = zh * 4 + m
    width = part.shape[3] // 2

    def column(index):
        return pl.ds(pl.multiple_of((index % 2) * width, 128), width)

    peers = [{"tensor": (t + k) % 16} for k in range(1, 16)]

    def at(chip):
        return {"mp": chip % 4, "dp": (chip // 4) * 2 + core}

    chips = [at((z + k) % 8) for k in range(1, 8)]
    sibling = {"dp": zh * 2 + 1 - core}
    greet(peers + chips + [sibling])
    send = Sender(send_sem, recv_sem)
    sums = []
    for k in range(1, 16):
        u = (t + k) % 16
        source = part.at[u // 4, (u % 4) // 2, :, column(u)]
        sums.append(send(source, landed.at[k - 1], peers[k - 1]))
    total = part[x, y // 2, :, column(y)]
    for k in range(15):
        sums[k].wait_recv()
        total += landed[k]
    mine = core * 8 + z
    out[mine, x, y // 2, :, column(y)] = total
    own = out.at[mine, x, y // 2, :, column(y)]
    spread = [send(own, own, chip) for chip in chips]
    for copy in spread:
        copy.wait_recv()

    low, high = pl.ds(core * 8, 4), pl.ds(core * 8 + 4, 4)
    low_a, low_b = pl.ds(core * 8, 2), pl.ds(core * 8 + 2, 2)
    high_a, high_b = pl.ds(core * 8 + 4, 2), pl.ds(core * 8 + 6, 2)
    two, rest = pl.ds(0, 2), pl.ds(2, 2)

    def cell(members, i, j):
        return out.at[members, i, j // 2, :, column(j)]

    def piece_a(phase):
        if phase == 0:
            return (
                lambda i: cell(low, i, y),
                lambda i: cell(low_a, i, y),
                lambda i: cell(low_b, i, y),
                x,
                along_x(y),
            )
        return (
            lambda j: cell(low, slice(None), j),
            lambda j: cell(low, two, j),
            lambda j: cell(low, rest, j),
            y,
            along_y(x),
        )

    def piece_b(phase):
        if phase == 0:
            return (
                lambda j: cell(high, x, j),
                lambda j: cell(high_a, x, j),
                lambda j: cell(high_b, x, j),
                y,
                along_y(x),
            )
        return (
            lambda i: out.at[high, i],
            lambda i: out.at[high_a, i],
            lambda i: out.at[high_b, i],
            x,
            along_x(y),
        )

    shared = []

    def share(source):
        shared.append(send(source, source, sibling))

    a, b = ring(send, *piece_a(0)), ring(send, *piece_b(0))
    for copy in [*a(), *b()]:
        copy.wait_recv()
    a, b = ring(send, *piece_a(1)), ring(send, *piece_b(1))
    block_a, block_b = piece_a(1)[0], piece_b(1)[0]
    share(block_a(y))
    share(block_b(x))
    pending = [*a(), *b()]
    for side in (3, 1):
        share(block_a((y + side) % 4))
        share(block_b((x + side) % 4))
    for copy in pending:
        copy.wait_recv()
    share(block_a((y + 2) % 4))
    share(block_b((x + 2) % 4))
    for copy in shared:
        copy.wait_recv()
    send.finish()


def sum_and_gather_rows(part):
    rows, width = part.shape
    out = jax.ShapeDtypeStruct((16, 4, 2, rows // 8, width), jnp.float32)
    scratch = [pltpu.VMEM((15, rows // 8, width // 2), jnp.float32)]
    full = remote_call(rows_kernel, out, 46, 3, scratch)(part.reshape(4, 2, rows // 8, width))
    return full.reshape(16 * rows, width)


def against(left, right, dims):
    return lax.dot_general(left, right, (dims, ((), ())), preferred_element_type=jnp.float32)


def on_device(tokens, norm_gain, gate_weight, up_weight, down_weight, sketch):
    feature_count = tokens.shape[1]
    offset = lax.axis_index("dp") * feature_count
    local_gain = lax.dynamic_slice_in_dim(norm_gain, offset, feature_count, 1)
    gathered = gather_tokens(tokens).reshape(-1, feature_count)
    count = gathered.shape[0]
    values = gathered.astype(jnp.float32)
    squares = jnp.broadcast_to(jnp.sum(values * values, axis=1), (8, count))
    parts = []
    for c in range(2):
        scaled = (values * local_gain[c]).astype(jnp.bfloat16)
        for weight in (gate_weight[c], up_weight[c]):
            parts.append(against(weight, scaled, ((0,), (1,))).astype(jnp.bfloat16))
    part = jnp.concatenate(parts, axis=0)
    hidden = sum_and_gather_hidden(part, squares)
    hidden = hidden.reshape(2, -1, hidden.shape[-1])
    partial_out = jnp.stack(
        [
            against(hidden[c], down_weight[c], ((0,), (0,))).astype(jnp.bfloat16)
            for c in range(2)
        ],
        axis=1,
    )
    share_mp = lax.axis_size("mp")
    partial_out = partial_out.reshape(share_mp, -1, 2, partial_out.shape[-1]).swapaxes(1, 2)
    blocks = sum_and_gather_acts(partial_out)
    acts = blocks.reshape(2, count, -1)
    d = lax.axis_index("dp")
    index = (d % 2) * 8 + (d // 2) * 4 + lax.axis_index("mp")
    mine = lax.dynamic_index_in_dim(blocks, index, 1, keepdims=False)
    rows = jnp.concatenate(
        [
            against(mine[0], acts[0], ((1,), (1,))),
            against(mine[1], acts[1], ((1,), (1,))),
            against(mine[1], sketch, ((1,), (0,))),
        ],
        axis=1,
    )
    full = sum_and_gather_rows(rows)
    basis_share, projected = sketch_call(full, acts)
    return (basis_share.T, projected.T)


def solution(mesh):
    return jax.shard_map(
        on_device,
        mesh=mesh,
        in_specs=(
            P(("mp", "tensor"), "dp"),
            P(),
            P(None, "dp", ("mp", "tensor")),
            P(None, "dp", ("mp", "tensor")),
            P(None, "mp", "tensor"),
            P("tensor", None),
        ),
        out_specs=(P("tensor", ("mp", "dp")), P("tensor", ("mp", "dp"))),
        check_vma=False,
    )
```

```python
import functools

import jax
import jax.numpy as jnp
from jax import lax
from jax.experimental import pallas as pl
from jax.experimental.pallas import tpu as pltpu
from jax.sharding import PartitionSpec as P

D = 8192
EPSILON = 1e-05
BLOCK = 128


def split(value):
    high = value.astype(jnp.bfloat16)
    return high, (value - high.astype(jnp.float32)).astype(jnp.bfloat16)


def mul(left, right, contract=((1,), (0,))):
    def dot(a, b):
        return lax.dot_general(a, b, (contract, ((), ())), preferred_element_type=jnp.float32)

    (a, a_low), (b, b_low) = left, right
    return dot(a, b) + (dot(a, b_low) + dot(a_low, b))


def reciprocal(value):
    return 1.0 / value


def inverse_factor(rows):
    lane = lax.broadcasted_iota(jnp.int32, (8, BLOCK), 1)
    sub = lax.broadcasted_iota(jnp.int32, (8, BLOCK), 0)
    rows = list(rows)
    groups = BLOCK // 8

    def spread(value):
        return jnp.broadcast_to(value, (8, BLOCK))

    out = []
    for g in range(groups):
        own = (lane >= 8 * g) & (lane < 8 * g + 8)
        cols = [[spread(rows[h][:, 8 * g + k : 8 * g + k + 1]) for k in range(8)] for h in range(g + 1, min(g + 2, groups))]
        plain = [spread(rows[g][k : k + 1, :]) for k in range(8)]
        s = [
            [spread(plain[i][:, 8 * g + k : 8 * g + k + 1]) for k in range(i + 1)] for i in range(8)
        ]
        lines = [
            jnp.where(own, (lane == 8 * g + k).astype(jnp.float32), plain[k]) for k in range(8)
        ]
        factor = [[None] * 8 for _ in range(8)]
        inv = [None] * 8
        for k in range(8):
            inv[k] = reciprocal(s[k][k])
            for i in range(k + 1, 8):
                factor[i][k] = s[i][k] * inv[k]
            for i in range(k + 1, 8):
                for n in range(k + 1, i + 1):
                    s[i][n] = s[i][n] - factor[i][k] * s[n][k]
        for k in range(8):
            for i in range(k + 1, 8):
                lines[i] = lines[i] - factor[i][k] * lines[k]
        solved = [lines[k] * inv[k] for k in range(8)]
        for i in range(7, 0, -1):
            for k in range(i):
                solved[k] = solved[k] - factor[i][k] * solved[i]
        for h in range(g + 1, min(g + 2, groups)):
            value = jnp.where(own, 0.0, rows[h])
            c = cols[h - g - 1]
            first = (c[0] * solved[0] + c[1] * solved[1]) + (c[2] * solved[2] + c[3] * solved[3])
            second = (c[4] * solved[4] + c[5] * solved[5]) + (c[6] * solved[6] + c[7] * solved[7])
            rows[h] = value - (first + second)
        if g + 2 < groups:
            tight = solved[0]
            for k in range(1, 8):
                tight = jnp.where(sub == k, solved[k], tight)
            zero = jnp.zeros_like(tight)
            wide = jnp.concatenate([tight if n == g else zero for n in range(groups)], axis=0)
            tall = jnp.concatenate(rows[g + 2 :], axis=0)
            change = mul(split(tall), split(wide))
            for h in range(g + 2, groups):
                n = 8 * (h - g - 2)
                rows[h] = jnp.where(own, 0.0, rows[h]) - change[n : n + 8, :]
        row = lines[0] * jnp.sqrt(inv[0])
        for k in range(1, 8):
            row = jnp.where(sub == k, lines[k] * jnp.sqrt(inv[k]), row)
        out.append(jnp.where(lane <= sub + 8 * g, row, 0.0))
    return jnp.concatenate(out, axis=0)


def orth_factor(gram, low_inv):
    n = gram.shape[0]
    blocks = n // BLOCK
    low_inv[...] = jnp.zeros_like(low_inv)
    at = [pl.ds(k * BLOCK, BLOCK) for k in range(blocks)]

    def diagonal(k):
        return [gram[pl.ds(k * BLOCK + 8 * g, 8), at[k]] for g in range(BLOCK // 8)]

    inv = inverse_factor(diagonal(0))
    for k in range(blocks):
        inv_s = split(inv)
        low_inv[at[k], at[k]] = inv
        panel = {}
        if k + 1 < blocks:
            panel[k + 1] = split(mul(inv_s, split(gram[at[k], at[k + 1]])))
            gram[at[k + 1], at[k + 1]] -= mul(panel[k + 1], panel[k + 1], ((0,), (0,)))
            following = inverse_factor(diagonal(k + 1))
        if k:
            before = pl.ds(0, k * BLOCK)
            low_inv[at[k], before] = mul(inv_s, split(low_inv[at[k], before]))
        so_far = pl.ds(0, (k + 1) * BLOCK)
        mine = split(low_inv[at[k], so_far])
        for i in range(k + 1, blocks):
            if i not in panel:
                panel[i] = split(mul(inv_s, split(gram[at[k], at[i]])))
            low_inv[at[i], so_far] -= mul(panel[i], mine, ((0,), (0,)))
            for j in range(i, blocks):
                if j not in panel:
                    panel[j] = split(mul(inv_s, split(gram[at[k], at[j]])))
                if (i, j) != (k + 1, k + 1):
                    gram[at[i], at[j]] -= mul(panel[i], panel[j], ((0,), (0,)))
        if k + 1 < blocks:
            inv = following


def sketch_kernel(full, acts, basis_out, last_out, gram, low_inv, high_z, low_z):
    tokens = full.shape[0]
    rank = gram.shape[0]
    share = basis_out.shape[0]
    high, low = split(full[:, pl.ds(2 * tokens, rank)])
    high_z[...] = high
    low_z[...] = low

    def step(n, carry):
        g_s = split(full[:, pl.ds(pl.multiple_of((n % 2) * tokens, 128), tokens)])
        z_s = (high_z[...], low_z[...])
        h = mul(g_s, z_s)
        gram[...] = mul(z_s, split(h), ((0,), (0,))) * (2.0**-33)
        orth_factor(gram, low_inv)

        @pl.when(n < 2)
        def _():
            high, low = split(mul(split(h * (1.0 / 1024)), split(low_inv[...]), ((1,), (1,))))
            high_z[...] = high
            low_z[...] = low

        return carry

    lax.fori_loop(0, 3, step, 0)
    index = lax.axis_index("mp") * 4 + lax.axis_index("dp")
    rows = low_inv[pl.ds(pl.multiple_of(index * share, share), share), :]
    coeff = split(mul(split(rows), (high_z[...], low_z[...]), ((1,), (1,))) * (1.0 / 1024))
    last = split(mul(coeff, split(full[:, pl.ds(0, tokens)])) * (1.0 / 1024))

    def apply(pair, c):
        def dot(a):
            return jnp.dot(a, acts[c], preferred_element_type=jnp.float32)

        return dot(pair[0]) + dot(pair[1])

    basis_out[...] = apply(coeff, 0)
    last_out[...] = apply(last, 1)


def sketch_call(full, acts):
    tokens = full.shape[0]
    rank = full.shape[1] - 2 * tokens
    features = acts.shape[2]
    shape = jax.ShapeDtypeStruct((rank // 16, features), jnp.float32)
    return pl.pallas_call(
        sketch_kernel,
        out_shape=(shape, shape),
        in_specs=[pl.BlockSpec(memory_space=pltpu.VMEM)] * 2,
        out_specs=(pl.BlockSpec(memory_space=pltpu.VMEM),) * 2,
        scratch_shapes=[
            pltpu.VMEM((rank, rank), jnp.float32),
            pltpu.VMEM((rank, rank), jnp.float32),
            pltpu.VMEM((tokens, rank), jnp.bfloat16),
            pltpu.VMEM((tokens, rank), jnp.bfloat16),
        ],
        compiler_params=pltpu.CompilerParams(vmem_limit_bytes=36 * 2**20),
    )(full, acts)


MESH = pl.DeviceIdType.MESH
VMEM = pl.BlockSpec(memory_space=pltpu.VMEM)


class Sender:
    def __init__(self, send, recv):
        self.send, self.recv, self.all = send, recv, []

    def __call__(self, source, target, device):
        n = len(self.all)
        copy = pltpu.make_async_remote_copy(
            src_ref=source,
            dst_ref=target,
            send_sem=self.send.at[n],
            recv_sem=self.recv.at[n],
            device_id=device,
            device_id_type=MESH,
        )
        copy.start()
        self.all.append(copy)
        return copy

    def finish(self):
        for copy in self.all:
            copy.wait_send()


def greet(peers):
    barrier = pltpu.get_barrier_semaphore()
    for peer in peers:
        pl.semaphore_signal(barrier, inc=1, device_id=peer, device_id_type=MESH)
    pl.semaphore_wait(barrier, len(peers))


def grid_place():
    t = lax.axis_index("tensor")
    return t // 4, t % 4


def ring(send, block, upper, lower, me, toward):
    right, left = (me + 1) % 4, (me + 3) % 4
    from_left = send(block(me), block(me), toward(right))
    from_right = send(block(me), block(me), toward(left))

    def forward():
        from_left.wait_recv()
        first = send(upper(left), upper(left), toward(right))
        from_right.wait_recv()
        second = send(lower(right), lower(right), toward(left))
        return first, second

    return forward


def two_rings(send, piece_a, piece_b):
    for phase in range(2):
        a = ring(send, *piece_a(phase))
        b = ring(send, *piece_b(phase))
        pending = [*a(), *b()]
        for copy in pending:
            copy.wait_recv()


def along_x(y):
    return lambda i: {"tensor": i * 4 + y}


def along_y(x):
    return lambda i: {"tensor": x * 4 + i}


def xy_neighbours(x, y):
    return [
        {"tensor": ((x + 1) % 4) * 4 + y},
        {"tensor": ((x + 3) % 4) * 4 + y},
        {"tensor": x * 4 + (y + 1) % 4},
        {"tensor": x * 4 + (y + 3) % 4},
    ]


def tokens_kernel(x_ref, out, send_sem, recv_sem):
    x, y = grid_place()
    m = lax.axis_index("mp")
    mates = [{"mp": (m + d) % 4} for d in range(1, 4)]
    greet(mates + xy_neighbours(x, y))
    send = Sender(send_sem, recv_sem)
    rows = x_ref.shape[0]
    half = x_ref.shape[1] // 2
    mine = pl.ds(pl.multiple_of(m * rows, rows), rows)
    first = [send(x_ref, out.at[x, y, mine], mate) for mate in mates]
    out[x, y, mine] = x_ref[...]
    for copy in first:
        copy.wait_recv()
    count = 4 * rows
    a, b = pl.ds(0, half), pl.ds(half, half)
    up, down = pl.ds(0, count // 2), pl.ds(count // 2, count // 2)
    two, rest = pl.ds(0, 2), pl.ds(2, 2)

    def piece_a(phase):
        if phase == 0:
            return (
                lambda i: out.at[i, y, :, a],
                lambda i: out.at[i, y, up, a],
                lambda i: out.at[i, y, down, a],
                x,
                along_x(y),
            )
        return (
            lambda i: out.at[:, i, :, a],
            lambda i: out.at[two, i, :, a],
            lambda i: out.at[rest, i, :, a],
            y,
            along_y(x),
        )

    def piece_b(phase):
        if phase == 0:
            return (
                lambda i: out.at[x, i, :, b],
                lambda i: out.at[x, i, up, b],
                lambda i: out.at[x, i, down, b],
                y,
                along_y(x),
            )
        return (
            lambda i: out.at[i, :, :, b],
            lambda i: out.at[i, two, :, b],
            lambda i: out.at[i, rest, :, b],
            x,
            along_x(y),
        )

    two_rings(send, piece_a, piece_b)
    send.finish()


def remote_call(kernel, out_shape, copies, number, limit, scratch=()):
    return pl.pallas_call(
        kernel,
        out_shape=out_shape,
        out_specs=VMEM,
        scratch_shapes=[
            *scratch,
            pltpu.SemaphoreType.DMA((copies,)),
            pltpu.SemaphoreType.DMA((copies,)),
        ],
        compiler_params=pltpu.CompilerParams(
            collective_id=number, has_side_effects=True, vmem_limit_bytes=limit * 2**20
        ),
    )


def gather_tokens(tokens):
    rows, features = tokens.shape
    out = jax.ShapeDtypeStruct((4, 4, 4 * rows, features), tokens.dtype)
    return remote_call(tokens_kernel, out, 19, 0, 12)(tokens)


def project_kernel(x_ref, gain_ref, gate_ref, up_ref, part, squares):
    def dot(a, b):
        return lax.dot_general(a, b, (((1,), (1,)), ((), ())), preferred_element_type=jnp.float32)

    features = x_ref.shape[1]
    units = gate_ref.shape[1]
    values = x_ref[...].astype(jnp.float32)
    high, low = split(values * values)
    ones = jnp.ones((8, features), jnp.bfloat16)
    squares[...] = dot(ones, high) + dot(ones, low)
    lanes = pl.ds(pl.multiple_of(lax.axis_index("dp") * features, 128), features)
    for c in range(2):
        scaled = (values * gain_ref[c : c + 1, lanes]).astype(jnp.bfloat16)
        row = 2 * c * units
        part[pl.ds(row, units), :] = dot(gate_ref[c], scaled).astype(jnp.bfloat16)
        part[pl.ds(row + units, units), :] = dot(up_ref[c], scaled).astype(jnp.bfloat16)


def project(tokens, norm_gain, gate_weight, up_weight):
    count, features = tokens.shape
    units = gate_weight.shape[2]
    step = 256
    whole = pl.BlockSpec((2, units, features), lambda i: (0, 0, 0))
    return pl.pallas_call(
        project_kernel,
        grid=(count // step,),
        out_shape=(
            jax.ShapeDtypeStruct((4 * units, count), jnp.bfloat16),
            jax.ShapeDtypeStruct((8, count), jnp.float32),
        ),
        in_specs=[
            pl.BlockSpec((step, features), lambda i: (i, 0)),
            pl.BlockSpec(norm_gain.shape, lambda i: (0, 0)),
            whole,
            whole,
        ],
        out_specs=(
            pl.BlockSpec((4 * units, step), lambda i: (0, i)),
            pl.BlockSpec((8, step), lambda i: (0, i)),
        ),
        compiler_params=pltpu.CompilerParams(vmem_limit_bytes=40 * 2**20),
    )(tokens, norm_gain, gate_weight.swapaxes(1, 2), up_weight.swapaxes(1, 2))


def hidden_kernel(part, squares, out, near, near_sq, pair, pair_sq, far, far_sq, send_sem, recv_sem):
    x, y = grid_place()
    d = lax.axis_index("dp")
    z, core = d // 2, d % 2
    sibling, partner = {"dp": z * 2 + 1 - core}, {"dp": (1 - z) * 2 + core}
    greet([sibling, partner] + xy_neighbours(x, y))
    send = Sender(send_sem, recv_sem)
    units, tokens = out.shape[3], out.shape[4]
    chunk = tokens // 2
    step = 32

    def share(zh, side, h=None):
        start = (zh * 2 + side) * tokens
        if h is None:
            return pl.ds(pl.multiple_of(start, 128), tokens)
        return pl.ds(pl.multiple_of(start + h * chunk, 128), chunk)

    first_sq = send(squares.at[:, share(1 - z, 1 - core)], near_sq.at[1], sibling)
    first = [
        send(part.at[:, share(1 - z, 1 - core, h)], near.at[1, h], sibling) for h in range(2)
    ]
    second_sq = send(squares.at[:, share(z, 1 - core)], near_sq.at[0], sibling)
    second = [send(part.at[:, share(z, 1 - core, h)], near.at[0, h], sibling) for h in range(2)]

    first_sq.wait_recv()
    pair_sq[...] = squares[:, share(1 - z, core)] + near_sq[1]
    across_sq = send(pair_sq, far_sq, partner)
    across = []
    for h in range(2):
        first[h].wait_recv()

        @pl.loop(0, 4 * units // step)
        def _(i):
            rows = pl.ds(pl.multiple_of(i * step, step), step)
            total = part[rows, share(1 - z, core, h)].astype(jnp.float32) + near[
                1, h, rows, :
            ].astype(jnp.float32)
            pair[h, rows, :] = total.astype(jnp.bfloat16)

        across.append(send(pair.at[h], far.at[h], partner))

    second_sq.wait_recv()
    across_sq.wait_recv()
    square_total = squares[:, share(z, core)] + near_sq[0] + far_sq[...]
    root = lax.rsqrt(square_total[0:1, :] / D + EPSILON)

    def activate(h):
        second[h].wait_recv()
        across[h].wait_recv()
        lanes = pl.ds(h * chunk, chunk)
        scale = root[:, h * chunk : (h + 1) * chunk]
        for c in range(2):

            @pl.loop(0, units // step)
            def _(i):
                def total(row):
                    rows = pl.ds(pl.multiple_of(row + i * step, step), step)
                    return (
                        part[rows, share(z, core, h)].astype(jnp.float32)
                        + near[0, h, rows, :].astype(jnp.float32)
                        + far[h, rows, :].astype(jnp.float32)
                    ) * scale

                gate = total(c * 2 * units)
                up = total(c * 2 * units + units)
                value = gate / (1.0 + jnp.exp(-gate)) * up
                rows = pl.ds(pl.multiple_of(i * step, step), step)
                out[c, x, y, rows, lanes] = value.astype(jnp.bfloat16)

    upper, lower = pl.ds(0, units // 2), pl.ds(units // 2, units // 2)
    every = slice(None)
    two, rest = pl.ds(0, 2), pl.ds(2, 2)

    def start(h, phase):
        lanes = pl.ds(h * chunk, chunk)
        if phase == 0:
            return (
                ring(
                    send,
                    lambda i: out.at[0, i, y, :, lanes],
                    lambda i: out.at[0, i, y, upper, lanes],
                    lambda i: out.at[0, i, y, lower, lanes],
                    x,
                    along_x(y),
                ),
                ring(
                    send,
                    lambda i: out.at[1, x, i, :, lanes],
                    lambda i: out.at[1, x, i, upper, lanes],
                    lambda i: out.at[1, x, i, lower, lanes],
                    y,
                    along_y(x),
                ),
            )
        return (
            ring(
                send,
                lambda i: out.at[0, every, i, :, lanes],
                lambda i: out.at[0, two, i, :, lanes],
                lambda i: out.at[0, rest, i, :, lanes],
                y,
                along_y(x),
            ),
            ring(
                send,
                lambda i: out.at[1, i, every, :, lanes],
                lambda i: out.at[1, i, two, :, lanes],
                lambda i: out.at[1, i, rest, :, lanes],
                x,
                along_x(y),
            ),
        )

    def forward(pair_of_rings):
        return [copy for one in pair_of_rings for copy in one()]

    def settle(copies):
        for copy in copies:
            copy.wait_recv()

    activate(0)
    rings = start(0, 0)
    settle(forward(rings))
    early = start(0, 1)
    activate(1)
    rings = start(1, 0)
    tail = forward(early)
    settle(forward(rings))
    tail += forward(start(1, 1))
    settle(tail)
    send.finish()


def sum_and_gather_hidden(part, squares):
    rows, tokens = part.shape[0], part.shape[1] // lax.axis_size("dp")
    out = jax.ShapeDtypeStruct((2, 4, 4, rows // 4, tokens), jnp.bfloat16)
    scratch = [
        pltpu.VMEM((2, 2, rows, tokens // 2), jnp.bfloat16),
        pltpu.VMEM((2, 8, tokens), jnp.float32),
        pltpu.VMEM((2, rows, tokens // 2), jnp.bfloat16),
        pltpu.VMEM((8, tokens), jnp.float32),
        pltpu.VMEM((2, rows, tokens // 2), jnp.bfloat16),
        pltpu.VMEM((8, tokens), jnp.float32),
    ]
    return remote_call(hidden_kernel, out, 41, 1, 24, scratch)(part, squares)


def acts_kernel(part, out, landed, send_sem, recv_sem):
    m, d = lax.axis_index("mp"), lax.axis_index("dp")
    zh, core = d // 2, d % 2
    z = zh * 4 + m
    mates = [{"mp": (m + k) % 4} for k in range(1, 4)]

    def at(chip):
        return {"mp": chip % 4, "dp": (chip // 4) * 2 + core}

    right, left = at((z + 1) % 8), at((z + 7) % 8)
    sibling = {"dp": zh * 2 + 1 - core}
    greet(mates + [right, left, sibling])
    send = Sender(send_sem, recv_sem)
    sums = [
        [
            send(part.at[(m + k) % 4, c], landed.at[k - 1, c], mates[k - 1])
            for k in (2, 1, 3)
        ]
        for c in range(2)
    ]
    half = part.shape[2] // 2
    halves = pl.ds(0, half), pl.ds(half, half)

    def block(c, chip):
        return out.at[c, core * 8 + chip]

    shared = []
    waiting = []
    for c in range(2):
        for copy in sums[c]:
            copy.wait_recv()
        total = part[m, c].astype(jnp.float32)
        for k in range(3):
            total += landed[k, c].astype(jnp.float32)
        out[c, core * 8 + z] = total.astype(jnp.bfloat16)
        here = block(c, z)
        waiting.append((send(here, here, right), send(here, here, left)))
        shared.append(send(here, here, sibling))
    for k in range(1, 4):
        before, after = (z + 8 - k) % 8, (z + k) % 8
        for c in range(2):
            from_left, from_right = waiting[c]
            near, next_near = block(c, before), block(c, after)
            on, back = near, next_near
            if k == 3:
                on = out.at[c, core * 8 + before, halves[0]]
                back = out.at[c, core * 8 + after, halves[1]]
            from_left.wait_recv()
            next_left = send(on, on, right)
            from_right.wait_recv()
            next_right = send(back, back, left)
            shared.append(send(near, near, sibling))
            shared.append(send(next_near, next_near, sibling))
            waiting[c] = (next_left, next_right)
    far = (z + 4) % 8
    for c in range(2):
        for copy in waiting[c]:
            copy.wait_recv()
        shared.append(send(block(c, far), block(c, far), sibling))
    for copy in shared:
        copy.wait_recv()
    send.finish()


def sum_and_gather_acts(part):
    _, copies, rows, features = part.shape
    out = jax.ShapeDtypeStruct((copies, 16, rows, features), jnp.bfloat16)
    scratch = [pltpu.VMEM((3, copies, rows, features), jnp.bfloat16)]
    return remote_call(acts_kernel, out, 38, 2, 12, scratch)(part)


def rows_kernel(part, out, landed, send_sem, recv_sem):
    t = lax.axis_index("tensor")
    x, y = grid_place()
    m, d = lax.axis_index("mp"), lax.axis_index("dp")
    zh, core = d // 2, d % 2
    z = zh * 4 + m
    width = part.shape[3] // 2

    def column(index):
        return pl.ds(pl.multiple_of((index % 2) * width, 128), width)

    peers = [{"tensor": (t + k) % 16} for k in range(1, 16)]

    def at(chip):
        return {"mp": chip % 4, "dp": (chip // 4) * 2 + core}

    chips = [at((z + k) % 8) for k in range(1, 8)]
    sibling = {"dp": zh * 2 + 1 - core}
    greet(peers + chips + [sibling])
    send = Sender(send_sem, recv_sem)
    sums = []
    for k in range(1, 16):
        u = (t + k) % 16
        source = part.at[u // 4, (u % 4) // 2, :, column(u)]
        sums.append(send(source, landed.at[k - 1], peers[k - 1]))
    total = part[x, y // 2, :, column(y)]
    for k in range(15):
        sums[k].wait_recv()
        total += landed[k]
    mine = core * 8 + z
    out[mine, x, y // 2, :, column(y)] = total
    own = out.at[mine, x, y // 2, :, column(y)]
    spread = [send(own, own, chip) for chip in chips]
    for copy in spread:
        copy.wait_recv()

    low, high = pl.ds(core * 8, 4), pl.ds(core * 8 + 4, 4)
    low_a, low_b = pl.ds(core * 8, 2), pl.ds(core * 8 + 2, 2)
    high_a, high_b = pl.ds(core * 8 + 4, 2), pl.ds(core * 8 + 6, 2)
    two, rest = pl.ds(0, 2), pl.ds(2, 2)

    def cell(members, i, j):
        return out.at[members, i, j // 2, :, column(j)]

    def piece_a(phase):
        if phase == 0:
            return (
                lambda i: cell(low, i, y),
                lambda i: cell(low_a, i, y),
                lambda i: cell(low_b, i, y),
                x,
                along_x(y),
            )
        return (
            lambda j: cell(low, slice(None), j),
            lambda j: cell(low, two, j),
            lambda j: cell(low, rest, j),
            y,
            along_y(x),
        )

    def piece_b(phase):
        if phase == 0:
            return (
                lambda j: cell(high, x, j),
                lambda j: cell(high_a, x, j),
                lambda j: cell(high_b, x, j),
                y,
                along_y(x),
            )
        return (
            lambda i: out.at[high, i],
            lambda i: out.at[high_a, i],
            lambda i: out.at[high_b, i],
            x,
            along_x(y),
        )

    shared = []

    def share(source):
        shared.append(send(source, source, sibling))

    a, b = ring(send, *piece_a(0)), ring(send, *piece_b(0))
    for copy in [*a(), *b()]:
        copy.wait_recv()
    a, b = ring(send, *piece_a(1)), ring(send, *piece_b(1))
    block_a, block_b = piece_a(1)[0], piece_b(1)[0]
    share(block_a(y))
    share(block_b(x))
    pending = [*a(), *b()]
    for side in (3, 1):
        share(block_a((y + side) % 4))
        share(block_b((x + side) % 4))
    for copy in pending:
        copy.wait_recv()
    share(block_a((y + 2) % 4))
    share(block_b((x + 2) % 4))
    for copy in shared:
        copy.wait_recv()
    send.finish()


def sum_and_gather_rows(part):
    rows, width = part.shape
    out = jax.ShapeDtypeStruct((16, 4, 2, rows // 8, width), jnp.float32)
    scratch = [pltpu.VMEM((15, rows // 8, width // 2), jnp.float32)]
    full = remote_call(rows_kernel, out, 46, 3, 24, scratch)(part.reshape(4, 2, rows // 8, width))
    return full.reshape(16 * rows, width)


def against(left, right, dims):
    return lax.dot_general(left, right, (dims, ((), ())), preferred_element_type=jnp.float32)


def on_device(tokens, norm_gain, gate_weight, up_weight, down_weight, sketch):
    feature_count = tokens.shape[1]
    gathered = gather_tokens(tokens).reshape(-1, feature_count)
    count = gathered.shape[0]
    part, squares = project(gathered, norm_gain, gate_weight, up_weight)
    hidden = sum_and_gather_hidden(part, squares)
    hidden = hidden.reshape(2, -1, hidden.shape[-1])
    partial_out = jnp.stack(
        [
            against(hidden[c], down_weight[c], ((0,), (0,))).astype(jnp.bfloat16)
            for c in range(2)
        ],
        axis=1,
    )
    share_mp = lax.axis_size("mp")
    partial_out = partial_out.reshape(share_mp, -1, 2, partial_out.shape[-1]).swapaxes(1, 2)
    blocks = sum_and_gather_acts(partial_out)
    acts = blocks.reshape(2, count, -1)
    d = lax.axis_index("dp")
    index = (d % 2) * 8 + (d // 2) * 4 + lax.axis_index("mp")
    mine = lax.dynamic_index_in_dim(blocks, index, 1, keepdims=False)
    rows = jnp.concatenate(
        [
            against(mine[0], acts[0], ((1,), (1,))),
            against(mine[1], acts[1], ((1,), (1,))),
            against(mine[1], sketch, ((1,), (0,))),
        ],
        axis=1,
    )
    full = sum_and_gather_rows(rows)
    basis_share, projected = sketch_call(full, acts)
    return (basis_share.T, projected.T)


def solution(mesh):
    return jax.shard_map(
        on_device,
        mesh=mesh,
        in_specs=(
            P(("mp", "tensor"), "dp"),
            P(),
            P(None, "dp", ("mp", "tensor")),
            P(None, "dp", ("mp", "tensor")),
            P(None, "mp", "tensor"),
            P("tensor", None),
        ),
        out_specs=(P("tensor", ("mp", "dp")), P("tensor", ("mp", "dp"))),
        check_vma=False,
    )
```

```python
import functools

import jax
import jax.numpy as jnp
from jax import lax
from jax.experimental import pallas as pl
from jax.experimental.pallas import tpu as pltpu
from jax.sharding import PartitionSpec as P

D = 8192
EPSILON = 1e-05
BLOCK = 128
HALF = 4


def split(value):
    high = value.astype(jnp.bfloat16)
    return high, (value - high.astype(jnp.float32)).astype(jnp.bfloat16)


def mul(left, right, contract=((1,), (0,))):
    def dot(a, b):
        return lax.dot_general(a, b, (contract, ((), ())), preferred_element_type=jnp.float32)

    (a, a_low), (b, b_low) = left, right
    return dot(a, b) + (dot(a, b_low) + dot(a_low, b))


def reciprocal(value):
    return 1.0 / value


def inverse_factor(rows):
    lane = lax.broadcasted_iota(jnp.int32, (8, BLOCK), 1)
    sub = lax.broadcasted_iota(jnp.int32, (8, BLOCK), 0)
    rows = list(rows)
    groups = BLOCK // 8

    def spread(value):
        return jnp.broadcast_to(value, (8, BLOCK))

    out = []
    for g in range(groups):
        own = (lane >= 8 * g) & (lane < 8 * g + 8)
        cols = [[spread(rows[h][:, 8 * g + k : 8 * g + k + 1]) for k in range(8)] for h in range(g + 1, min(g + 2, groups))]
        plain = [spread(rows[g][k : k + 1, :]) for k in range(8)]
        s = [
            [spread(plain[i][:, 8 * g + k : 8 * g + k + 1]) for k in range(i + 1)] for i in range(8)
        ]
        lines = [
            jnp.where(own, (lane == 8 * g + k).astype(jnp.float32), plain[k]) for k in range(8)
        ]
        factor = [[None] * 8 for _ in range(8)]
        inv = [None] * 8
        for k in range(8):
            inv[k] = reciprocal(s[k][k])
            for i in range(k + 1, 8):
                factor[i][k] = s[i][k] * inv[k]
            for i in range(k + 1, 8):
                for n in range(k + 1, i + 1):
                    s[i][n] = s[i][n] - factor[i][k] * s[n][k]
        for k in range(8):
            for i in range(k + 1, 8):
                lines[i] = lines[i] - factor[i][k] * lines[k]
        solved = [lines[k] * inv[k] for k in range(8)]
        for i in range(7, 0, -1):
            for k in range(i):
                solved[k] = solved[k] - factor[i][k] * solved[i]
        for h in range(g + 1, min(g + 2, groups)):
            value = jnp.where(own, 0.0, rows[h])
            c = cols[h - g - 1]
            first = (c[0] * solved[0] + c[1] * solved[1]) + (c[2] * solved[2] + c[3] * solved[3])
            second = (c[4] * solved[4] + c[5] * solved[5]) + (c[6] * solved[6] + c[7] * solved[7])
            rows[h] = value - (first + second)
        if g + 2 < groups:
            tight = solved[0]
            for k in range(1, 8):
                tight = jnp.where(sub == k, solved[k], tight)
            zero = jnp.zeros_like(tight)
            wide = jnp.concatenate([tight if n == g else zero for n in range(groups)], axis=0)
            tall = jnp.concatenate(rows[g + 2 :], axis=0)
            change = mul(split(tall), split(wide))
            for h in range(g + 2, groups):
                n = 8 * (h - g - 2)
                rows[h] = jnp.where(own, 0.0, rows[h]) - change[n : n + 8, :]
        row = lines[0] * jnp.sqrt(inv[0])
        for k in range(1, 8):
            row = jnp.where(sub == k, lines[k] * jnp.sqrt(inv[k]), row)
        out.append(jnp.where(lane <= sub + 8 * g, row, 0.0))
    return jnp.concatenate(out, axis=0)


def orth_factor(gram, low_inv):
    n = gram.shape[0]
    blocks = n // BLOCK
    low_inv[...] = jnp.zeros_like(low_inv)
    at = [pl.ds(k * BLOCK, BLOCK) for k in range(blocks)]

    def diagonal(k):
        return [gram[pl.ds(k * BLOCK + 8 * g, 8), at[k]] for g in range(BLOCK // 8)]

    inv = inverse_factor(diagonal(0))
    for k in range(blocks):
        inv_s = split(inv)
        low_inv[at[k], at[k]] = inv
        panel = {}
        if k + 1 < blocks:
            panel[k + 1] = split(mul(inv_s, split(gram[at[k], at[k + 1]])))
            gram[at[k + 1], at[k + 1]] -= mul(panel[k + 1], panel[k + 1], ((0,), (0,)))
            following = inverse_factor(diagonal(k + 1))
        if k:
            before = pl.ds(0, k * BLOCK)
            low_inv[at[k], before] = mul(inv_s, split(low_inv[at[k], before]))
        so_far = pl.ds(0, (k + 1) * BLOCK)
        mine = split(low_inv[at[k], so_far])
        for i in range(k + 1, blocks):
            if i not in panel:
                panel[i] = split(mul(inv_s, split(gram[at[k], at[i]])))
            low_inv[at[i], so_far] -= mul(panel[i], mine, ((0,), (0,)))
            for j in range(i, blocks):
                if j not in panel:
                    panel[j] = split(mul(inv_s, split(gram[at[k], at[j]])))
                if (i, j) != (k + 1, k + 1):
                    gram[at[i], at[j]] -= mul(panel[i], panel[j], ((0,), (0,)))
        if k + 1 < blocks:
            inv = following


def fill_grams(full, g_high, g_low):
    @pl.loop(0, 2 * HALF)
    def _(z):
        here = pl.ds(pl.multiple_of(z * BLOCK, BLOCK), BLOCK)
        for c in range(2):
            for k in range(HALF + 1):
                there = pl.ds(pl.multiple_of(((z + k) % 8) * BLOCK, BLOCK), BLOCK)
                value = full[here, pl.ds((c * (HALF + 1) + k) * BLOCK, BLOCK)]
                g_high[c, here, there], g_low[c, here, there] = split(value)
                if 0 < k < HALF:
                    g_high[c, there, here], g_low[c, there, here] = split(value.T)


def sketch_kernel(full, acts, basis_out, last_out, gram, low_inv, high_z, low_z, g_high, g_low):
    tokens = full.shape[0]
    rank = gram.shape[0]
    share = basis_out.shape[0]
    high, low = split(full[:, pl.ds(2 * (HALF + 1) * BLOCK, rank)])
    high_z[...] = high
    low_z[...] = low
    fill_grams(full, g_high, g_low)

    def step(n, carry):
        z_s = (high_z[...], low_z[...])
        h = mul((g_high[n % 2], g_low[n % 2]), z_s)
        gram[...] = mul(z_s, split(h), ((0,), (0,))) * (2.0**-33)
        orth_factor(gram, low_inv)

        @pl.when(n < 2)
        def _():
            high, low = split(mul(split(h * (1.0 / 1024)), split(low_inv[...]), ((1,), (1,))))
            high_z[...] = high
            low_z[...] = low

        return carry

    lax.fori_loop(0, 3, step, 0)
    index = lax.axis_index("mp") * 4 + lax.axis_index("dp")
    rows = low_inv[pl.ds(pl.multiple_of(index * share, share), share), :]
    coeff = split(mul(split(rows), (high_z[...], low_z[...]), ((1,), (1,))) * (1.0 / 1024))
    last = split(mul(coeff, (g_high[0], g_low[0])) * (1.0 / 1024))

    def apply(pair, c):
        def dot(a):
            return jnp.dot(a, acts[c], preferred_element_type=jnp.float32)

        return dot(pair[0]) + dot(pair[1])

    basis_out[...] = apply(coeff, 0)
    last_out[...] = apply(last, 1)


def sketch_call(full, acts):
    tokens = full.shape[0]
    rank = full.shape[1] - 2 * (HALF + 1) * BLOCK
    features = acts.shape[2]
    shape = jax.ShapeDtypeStruct((rank // 16, features), jnp.float32)
    return pl.pallas_call(
        sketch_kernel,
        out_shape=(shape, shape),
        in_specs=[pl.BlockSpec(memory_space=pltpu.VMEM)] * 2,
        out_specs=(pl.BlockSpec(memory_space=pltpu.VMEM),) * 2,
        scratch_shapes=[
            pltpu.VMEM((rank, rank), jnp.float32),
            pltpu.VMEM((rank, rank), jnp.float32),
            pltpu.VMEM((tokens, rank), jnp.bfloat16),
            pltpu.VMEM((tokens, rank), jnp.bfloat16),
            pltpu.VMEM((2, tokens, tokens), jnp.bfloat16),
            pltpu.VMEM((2, tokens, tokens), jnp.bfloat16),
        ],
        compiler_params=pltpu.CompilerParams(vmem_limit_bytes=36 * 2**20),
    )(full, acts)


MESH = pl.DeviceIdType.MESH
VMEM = pl.BlockSpec(memory_space=pltpu.VMEM)


class Sender:
    def __init__(self, send, recv):
        self.send, self.recv, self.all = send, recv, []

    def __call__(self, source, target, device):
        n = len(self.all)
        copy = pltpu.make_async_remote_copy(
            src_ref=source,
            dst_ref=target,
            send_sem=self.send.at[n],
            recv_sem=self.recv.at[n],
            device_id=device,
            device_id_type=MESH,
        )
        copy.start()
        self.all.append(copy)
        return copy

    def finish(self):
        for copy in self.all:
            copy.wait_send()


def greet(peers):
    barrier = pltpu.get_barrier_semaphore()
    for peer in peers:
        pl.semaphore_signal(barrier, inc=1, device_id=peer, device_id_type=MESH)
    pl.semaphore_wait(barrier, len(peers))


def grid_place():
    t = lax.axis_index("tensor")
    return t // 4, t % 4


def ring(send, block, upper, lower, me, toward):
    right, left = (me + 1) % 4, (me + 3) % 4
    from_left = send(block(me), block(me), toward(right))
    from_right = send(block(me), block(me), toward(left))

    def forward():
        from_left.wait_recv()
        first = send(upper(left), upper(left), toward(right))
        from_right.wait_recv()
        second = send(lower(right), lower(right), toward(left))
        return first, second

    return forward


def two_rings(send, piece_a, piece_b):
    for phase in range(2):
        a = ring(send, *piece_a(phase))
        b = ring(send, *piece_b(phase))
        pending = [*a(), *b()]
        for copy in pending:
            copy.wait_recv()


def along_x(y):
    return lambda i: {"tensor": i * 4 + y}


def along_y(x):
    return lambda i: {"tensor": x * 4 + i}


def xy_neighbours(x, y):
    return [
        {"tensor": ((x + 1) % 4) * 4 + y},
        {"tensor": ((x + 3) % 4) * 4 + y},
        {"tensor": x * 4 + (y + 1) % 4},
        {"tensor": x * 4 + (y + 3) % 4},
    ]


def tokens_kernel(x_ref, out, send_sem, recv_sem):
    x, y = grid_place()
    m = lax.axis_index("mp")
    mates = [{"mp": (m + d) % 4} for d in range(1, 4)]
    greet(mates + xy_neighbours(x, y))
    send = Sender(send_sem, recv_sem)
    rows = x_ref.shape[0]
    half = x_ref.shape[1] // 2
    mine = pl.ds(pl.multiple_of(m * rows, rows), rows)
    first = [send(x_ref, out.at[x, y, mine], mate) for mate in mates]
    out[x, y, mine] = x_ref[...]
    for copy in first:
        copy.wait_recv()
    count = 4 * rows
    a, b = pl.ds(0, half), pl.ds(half, half)
    up, down = pl.ds(0, count // 2), pl.ds(count // 2, count // 2)
    two, rest = pl.ds(0, 2), pl.ds(2, 2)

    def piece_a(phase):
        if phase == 0:
            return (
                lambda i: out.at[i, y, :, a],
                lambda i: out.at[i, y, up, a],
                lambda i: out.at[i, y, down, a],
                x,
                along_x(y),
            )
        return (
            lambda i: out.at[:, i, :, a],
            lambda i: out.at[two, i, :, a],
            lambda i: out.at[rest, i, :, a],
            y,
            along_y(x),
        )

    def piece_b(phase):
        if phase == 0:
            return (
                lambda i: out.at[x, i, :, b],
                lambda i: out.at[x, i, up, b],
                lambda i: out.at[x, i, down, b],
                y,
                along_y(x),
            )
        return (
            lambda i: out.at[i, :, :, b],
            lambda i: out.at[i, two, :, b],
            lambda i: out.at[i, rest, :, b],
            x,
            along_x(y),
        )

    two_rings(send, piece_a, piece_b)
    send.finish()


def remote_call(kernel, out_shape, copies, number, limit, scratch=()):
    return pl.pallas_call(
        kernel,
        out_shape=out_shape,
        out_specs=VMEM,
        scratch_shapes=[
            *scratch,
            pltpu.SemaphoreType.DMA((copies,)),
            pltpu.SemaphoreType.DMA((copies,)),
        ],
        compiler_params=pltpu.CompilerParams(
            collective_id=number, has_side_effects=True, vmem_limit_bytes=limit * 2**20
        ),
    )


def gather_tokens(tokens):
    rows, features = tokens.shape
    out = jax.ShapeDtypeStruct((4, 4, 4 * rows, features), tokens.dtype)
    return remote_call(tokens_kernel, out, 19, 0, 12)(tokens)


def project_kernel(x_ref, gain_ref, gate_ref, up_ref, part, squares):
    def dot(a, b):
        return lax.dot_general(a, b, (((1,), (1,)), ((), ())), preferred_element_type=jnp.float32)

    features = x_ref.shape[1]
    units = gate_ref.shape[1]
    values = x_ref[...].astype(jnp.float32)
    high, low = split(values * values)
    ones = jnp.ones((8, features), jnp.bfloat16)
    squares[...] = dot(ones, high) + dot(ones, low)
    lanes = pl.ds(pl.multiple_of(lax.axis_index("dp") * features, 128), features)
    for c in range(2):
        scaled = (values * gain_ref[c : c + 1, lanes]).astype(jnp.bfloat16)
        row = 2 * c * units
        part[pl.ds(row, units), :] = dot(gate_ref[c], scaled).astype(jnp.bfloat16)
        part[pl.ds(row + units, units), :] = dot(up_ref[c], scaled).astype(jnp.bfloat16)


def project(tokens, norm_gain, gate_weight, up_weight):
    count, features = tokens.shape
    units = gate_weight.shape[2]
    step = 256
    whole = pl.BlockSpec((2, units, features), lambda i: (0, 0, 0))
    return pl.pallas_call(
        project_kernel,
        grid=(count // step,),
        out_shape=(
            jax.ShapeDtypeStruct((4 * units, count), jnp.bfloat16),
            jax.ShapeDtypeStruct((8, count), jnp.float32),
        ),
        in_specs=[
            pl.BlockSpec((step, features), lambda i: (i, 0)),
            pl.BlockSpec(norm_gain.shape, lambda i: (0, 0)),
            whole,
            whole,
        ],
        out_specs=(
            pl.BlockSpec((4 * units, step), lambda i: (0, i)),
            pl.BlockSpec((8, step), lambda i: (0, i)),
        ),
        compiler_params=pltpu.CompilerParams(vmem_limit_bytes=40 * 2**20),
    )(tokens, norm_gain, gate_weight.swapaxes(1, 2), up_weight.swapaxes(1, 2))


def hidden_kernel(part, squares, out, near, near_sq, pair, pair_sq, far, far_sq, send_sem, recv_sem):
    x, y = grid_place()
    d = lax.axis_index("dp")
    z, core = d // 2, d % 2
    sibling, partner = {"dp": z * 2 + 1 - core}, {"dp": (1 - z) * 2 + core}
    greet([sibling, partner] + xy_neighbours(x, y))
    send = Sender(send_sem, recv_sem)
    units, tokens = out.shape[3], out.shape[4]
    chunk = tokens // 2
    step = 32

    def share(zh, side, h=None):
        start = (zh * 2 + side) * tokens
        if h is None:
            return pl.ds(pl.multiple_of(start, 128), tokens)
        return pl.ds(pl.multiple_of(start + h * chunk, 128), chunk)

    first_sq = send(squares.at[:, share(1 - z, 1 - core)], near_sq.at[1], sibling)
    first = [
        send(part.at[:, share(1 - z, 1 - core, h)], near.at[1, h], sibling) for h in range(2)
    ]
    second_sq = send(squares.at[:, share(z, 1 - core)], near_sq.at[0], sibling)
    second = [send(part.at[:, share(z, 1 - core, h)], near.at[0, h], sibling) for h in range(2)]

    first_sq.wait_recv()
    pair_sq[...] = squares[:, share(1 - z, core)] + near_sq[1]
    across_sq = send(pair_sq, far_sq, partner)
    across = []
    for h in range(2):
        first[h].wait_recv()

        @pl.loop(0, 4 * units // step)
        def _(i):
            rows = pl.ds(pl.multiple_of(i * step, step), step)
            total = part[rows, share(1 - z, core, h)].astype(jnp.float32) + near[
                1, h, rows, :
            ].astype(jnp.float32)
            pair[h, rows, :] = total.astype(jnp.bfloat16)

        across.append(send(pair.at[h], far.at[h], partner))

    second_sq.wait_recv()
    across_sq.wait_recv()
    square_total = squares[:, share(z, core)] + near_sq[0] + far_sq[...]
    root = lax.rsqrt(square_total[0:1, :] / D + EPSILON)

    def activate(h):
        second[h].wait_recv()
        across[h].wait_recv()
        lanes = pl.ds(h * chunk, chunk)
        scale = root[:, h * chunk : (h + 1) * chunk]
        for c in range(2):

            @pl.loop(0, units // step)
            def _(i):
                def total(row):
                    rows = pl.ds(pl.multiple_of(row + i * step, step), step)
                    return (
                        part[rows, share(z, core, h)].astype(jnp.float32)
                        + near[0, h, rows, :].astype(jnp.float32)
                        + far[h, rows, :].astype(jnp.float32)
                    ) * scale

                gate = total(c * 2 * units)
                up = total(c * 2 * units + units)
                value = gate / (1.0 + jnp.exp(-gate)) * up
                rows = pl.ds(pl.multiple_of(i * step, step), step)
                out[c, x, y, rows, lanes] = value.astype(jnp.bfloat16)

    upper, lower = pl.ds(0, units // 2), pl.ds(units // 2, units // 2)
    every = slice(None)
    two, rest = pl.ds(0, 2), pl.ds(2, 2)

    def start(h, phase):
        lanes = pl.ds(h * chunk, chunk)
        if phase == 0:
            return (
                ring(
                    send,
                    lambda i: out.at[0, i, y, :, lanes],
                    lambda i: out.at[0, i, y, upper, lanes],
                    lambda i: out.at[0, i, y, lower, lanes],
                    x,
                    along_x(y),
                ),
                ring(
                    send,
                    lambda i: out.at[1, x, i, :, lanes],
                    lambda i: out.at[1, x, i, upper, lanes],
                    lambda i: out.at[1, x, i, lower, lanes],
                    y,
                    along_y(x),
                ),
            )
        return (
            ring(
                send,
                lambda i: out.at[0, every, i, :, lanes],
                lambda i: out.at[0, two, i, :, lanes],
                lambda i: out.at[0, rest, i, :, lanes],
                y,
                along_y(x),
            ),
            ring(
                send,
                lambda i: out.at[1, i, every, :, lanes],
                lambda i: out.at[1, i, two, :, lanes],
                lambda i: out.at[1, i, rest, :, lanes],
                x,
                along_x(y),
            ),
        )

    def forward(pair_of_rings):
        return [copy for one in pair_of_rings for copy in one()]

    def settle(copies):
        for copy in copies:
            copy.wait_recv()

    activate(0)
    rings = start(0, 0)
    settle(forward(rings))
    early = start(0, 1)
    activate(1)
    rings = start(1, 0)
    tail = forward(early)
    settle(forward(rings))
    tail += forward(start(1, 1))
    settle(tail)
    send.finish()


def sum_and_gather_hidden(part, squares):
    rows, tokens = part.shape[0], part.shape[1] // lax.axis_size("dp")
    out = jax.ShapeDtypeStruct((2, 4, 4, rows // 4, tokens), jnp.bfloat16)
    scratch = [
        pltpu.VMEM((2, 2, rows, tokens // 2), jnp.bfloat16),
        pltpu.VMEM((2, 8, tokens), jnp.float32),
        pltpu.VMEM((2, rows, tokens // 2), jnp.bfloat16),
        pltpu.VMEM((8, tokens), jnp.float32),
        pltpu.VMEM((2, rows, tokens // 2), jnp.bfloat16),
        pltpu.VMEM((8, tokens), jnp.float32),
    ]
    return remote_call(hidden_kernel, out, 41, 1, 24, scratch)(part, squares)


def acts_kernel(part, out, landed, send_sem, recv_sem):
    m, d = lax.axis_index("mp"), lax.axis_index("dp")
    zh, core = d // 2, d % 2
    z = zh * 4 + m
    mates = [{"mp": (m + k) % 4} for k in range(1, 4)]

    def at(chip):
        return {"mp": chip % 4, "dp": (chip // 4) * 2 + core}

    right, left = at((z + 1) % 8), at((z + 7) % 8)
    sibling = {"dp": zh * 2 + 1 - core}
    greet(mates + [right, left, sibling])
    send = Sender(send_sem, recv_sem)
    sums = [
        [
            send(part.at[(m + k) % 4, c], landed.at[k - 1, c], mates[k - 1])
            for k in (2, 1, 3)
        ]
        for c in range(2)
    ]
    half = part.shape[2] // 2
    halves = pl.ds(0, half), pl.ds(half, half)

    def block(c, chip):
        return out.at[c, chip * 2 + core]

    shared = []
    waiting = []
    for c in range(2):
        for copy in sums[c]:
            copy.wait_recv()
        total = part[m, c].astype(jnp.float32)
        for k in range(3):
            total += landed[k, c].astype(jnp.float32)
        out[c, z * 2 + core] = total.astype(jnp.bfloat16)
        here = block(c, z)
        waiting.append((send(here, here, right), send(here, here, left)))
        shared.append(send(here, here, sibling))
    for k in range(1, 4):
        before, after = (z + 8 - k) % 8, (z + k) % 8
        for c in range(2):
            from_left, from_right = waiting[c]
            near, next_near = block(c, before), block(c, after)
            on, back = near, next_near
            if k == 3:
                on = out.at[c, before * 2 + core, halves[0]]
                back = out.at[c, after * 2 + core, halves[1]]
            from_left.wait_recv()
            next_left = send(on, on, right)
            from_right.wait_recv()
            next_right = send(back, back, left)
            shared.append(send(near, near, sibling))
            shared.append(send(next_near, next_near, sibling))
            waiting[c] = (next_left, next_right)
    far = (z + 4) % 8
    for c in range(2):
        for copy in waiting[c]:
            copy.wait_recv()
        shared.append(send(block(c, far), block(c, far), sibling))
    for copy in shared:
        copy.wait_recv()
    send.finish()


def sum_and_gather_acts(part):
    _, copies, rows, features = part.shape
    out = jax.ShapeDtypeStruct((copies, 16, rows, features), jnp.bfloat16)
    scratch = [pltpu.VMEM((3, copies, rows, features), jnp.bfloat16)]
    return remote_call(acts_kernel, out, 38, 2, 12, scratch)(part)


def rows_kernel(part, out, landed, send_sem, recv_sem):
    t = lax.axis_index("tensor")
    x, y = grid_place()
    m, d = lax.axis_index("mp"), lax.axis_index("dp")
    zh, core = d // 2, d % 2
    z = zh * 4 + m
    width = part.shape[3] // 2

    def column(index):
        return pl.ds(pl.multiple_of((index % 2) * width, 128), width)

    peers = [{"tensor": (t + k) % 16} for k in range(1, 16)]

    def at(chip):
        return {"mp": chip % 4, "dp": (chip // 4) * 2 + core}

    chips = [at((z + k) % 8) for k in range(1, 8)]
    sibling = {"dp": zh * 2 + 1 - core}
    greet(peers + chips + [sibling])
    send = Sender(send_sem, recv_sem)
    sums = []
    for k in range(1, 16):
        u = (t + k) % 16
        source = part.at[u // 4, (u % 4) // 2, :, column(u)]
        sums.append(send(source, landed.at[k - 1], peers[k - 1]))
    total = part[x, y // 2, :, column(y)]
    for k in range(15):
        sums[k].wait_recv()
        total += landed[k]
    out[z, core, x, y // 2, :, column(y)] = total
    own = out.at[z, core, x, y // 2, :, column(y)]
    spread = [send(own, own, chip) for chip in chips]
    for copy in spread:
        copy.wait_recv()

    low, high = pl.ds(0, 4), pl.ds(4, 4)
    low_a, low_b = pl.ds(0, 2), pl.ds(2, 2)
    high_a, high_b = pl.ds(4, 2), pl.ds(6, 2)
    two, rest = pl.ds(0, 2), pl.ds(2, 2)

    def cell(members, i, j):
        return out.at[members, core, i, j // 2, :, column(j)]

    def piece_a(phase):
        if phase == 0:
            return (
                lambda i: cell(low, i, y),
                lambda i: cell(low_a, i, y),
                lambda i: cell(low_b, i, y),
                x,
                along_x(y),
            )
        return (
            lambda j: cell(low, slice(None), j),
            lambda j: cell(low, two, j),
            lambda j: cell(low, rest, j),
            y,
            along_y(x),
        )

    def piece_b(phase):
        if phase == 0:
            return (
                lambda j: cell(high, x, j),
                lambda j: cell(high_a, x, j),
                lambda j: cell(high_b, x, j),
                y,
                along_y(x),
            )
        return (
            lambda i: out.at[high, core, i],
            lambda i: out.at[high_a, core, i],
            lambda i: out.at[high_b, core, i],
            x,
            along_x(y),
        )

    shared = []

    def share(source):
        shared.append(send(source, source, sibling))

    a, b = ring(send, *piece_a(0)), ring(send, *piece_b(0))
    for copy in [*a(), *b()]:
        copy.wait_recv()
    a, b = ring(send, *piece_a(1)), ring(send, *piece_b(1))
    block_a, block_b = piece_a(1)[0], piece_b(1)[0]
    share(block_a(y))
    share(block_b(x))
    pending = [*a(), *b()]
    for side in (3, 1):
        share(block_a((y + side) % 4))
        share(block_b((x + side) % 4))
    for copy in pending:
        copy.wait_recv()
    share(block_a((y + 2) % 4))
    share(block_b((x + 2) % 4))
    for copy in shared:
        copy.wait_recv()
    send.finish()


def sum_and_gather_rows(part):
    rows, width = part.shape
    out = jax.ShapeDtypeStruct((8, 2, 4, 2, rows // 8, width), jnp.float32)
    scratch = [pltpu.VMEM((15, rows // 8, width // 2), jnp.float32)]
    full = remote_call(rows_kernel, out, 46, 3, 24, scratch)(part.reshape(4, 2, rows // 8, width))
    return full.reshape(16 * rows, width)


def products_kernel(acts, sketch, out):
    d = lax.axis_index("dp")
    core = d % 2
    z = (d // 2) * 4 + lax.axis_index("mp")
    rows = out.shape[0]
    for c in range(2):
        mine = acts[c, z, pl.ds(pl.multiple_of(core * rows, rows), rows)]
        for k in range(HALF + 1):
            other = acts[c, lax.rem(z + k, 8)]
            lanes = pl.ds((c * (HALF + 1) + k) * BLOCK, BLOCK)
            out[:, lanes] = lax.dot_general(
                mine, other, (((1,), (1,)), ((), ())), preferred_element_type=jnp.float32
            )
    lanes = pl.ds(2 * (HALF + 1) * BLOCK, sketch.shape[1])
    out[:, lanes] = jnp.dot(mine, sketch[...], preferred_element_type=jnp.float32)


def row_products(acts, sketch):
    rows = acts.shape[2] // 2
    width = 2 * (HALF + 1) * BLOCK + sketch.shape[1]
    return pl.pallas_call(
        products_kernel,
        out_shape=jax.ShapeDtypeStruct((rows, width), jnp.float32),
        in_specs=[VMEM, VMEM],
        out_specs=VMEM,
        compiler_params=pltpu.CompilerParams(vmem_limit_bytes=12 * 2**20),
    )(acts, sketch)


def against(left, right, dims):
    return lax.dot_general(left, right, (dims, ((), ())), preferred_element_type=jnp.float32)


def on_device(tokens, norm_gain, gate_weight, up_weight, down_weight, sketch):
    feature_count = tokens.shape[1]
    gathered = gather_tokens(tokens).reshape(-1, feature_count)
    count = gathered.shape[0]
    part, squares = project(gathered, norm_gain, gate_weight, up_weight)
    hidden = sum_and_gather_hidden(part, squares)
    hidden = hidden.reshape(2, -1, hidden.shape[-1])
    partial_out = jnp.stack(
        [
            against(hidden[c], down_weight[c], ((0,), (0,))).astype(jnp.bfloat16)
            for c in range(2)
        ],
        axis=1,
    )
    share_mp = lax.axis_size("mp")
    partial_out = partial_out.reshape(share_mp, -1, 2, partial_out.shape[-1]).swapaxes(1, 2)
    blocks = sum_and_gather_acts(partial_out)
    acts = blocks.reshape(2, count, -1)
    rows = row_products(blocks.reshape(2, 8, count // 8, -1), sketch)
    full = sum_and_gather_rows(rows)
    basis_share, projected = sketch_call(full, acts)
    return (basis_share.T, projected.T)


def solution(mesh):
    return jax.shard_map(
        on_device,
        mesh=mesh,
        in_specs=(
            P(("mp", "tensor"), "dp"),
            P(),
            P(None, "dp", ("mp", "tensor")),
            P(None, "dp", ("mp", "tensor")),
            P(None, "mp", "tensor"),
            P("tensor", None),
        ),
        out_specs=(P("tensor", ("mp", "dp")), P("tensor", ("mp", "dp"))),
        check_vma=False,
    )
```

```python
import functools

import jax
import jax.numpy as jnp
from jax import lax
from jax.experimental import pallas as pl
from jax.experimental.pallas import tpu as pltpu
from jax.sharding import PartitionSpec as P

D = 8192
EPSILON = 1e-05
BLOCK = 128
HALF = 4


def split(value):
    high = value.astype(jnp.bfloat16)
    return high, (value - high.astype(jnp.float32)).astype(jnp.bfloat16)


def mul(left, right, contract=((1,), (0,))):
    def dot(a, b):
        return lax.dot_general(a, b, (contract, ((), ())), preferred_element_type=jnp.float32)

    (a, a_low), (b, b_low) = left, right
    return dot(a, b) + (dot(a, b_low) + dot(a_low, b))


def reciprocal(value):
    return 1.0 / value


def inverse_factor(rows):
    lane = lax.broadcasted_iota(jnp.int32, (8, BLOCK), 1)
    sub = lax.broadcasted_iota(jnp.int32, (8, BLOCK), 0)
    rows = list(rows)
    groups = BLOCK // 8

    def spread(value):
        return jnp.broadcast_to(value, (8, BLOCK))

    out = []
    for g in range(groups):
        own = (lane >= 8 * g) & (lane < 8 * g + 8)
        cols = [[spread(rows[h][:, 8 * g + k : 8 * g + k + 1]) for k in range(8)] for h in range(g + 1, min(g + 2, groups))]
        plain = [spread(rows[g][k : k + 1, :]) for k in range(8)]
        s = [
            [spread(plain[i][:, 8 * g + k : 8 * g + k + 1]) for k in range(i + 1)] for i in range(8)
        ]
        lines = [
            jnp.where(own, (lane == 8 * g + k).astype(jnp.float32), plain[k]) for k in range(8)
        ]
        factor = [[None] * 8 for _ in range(8)]
        inv = [None] * 8
        for k in range(8):
            inv[k] = reciprocal(s[k][k])
            for i in range(k + 1, 8):
                factor[i][k] = s[i][k] * inv[k]
            for i in range(k + 1, 8):
                for n in range(k + 1, i + 1):
                    s[i][n] = s[i][n] - factor[i][k] * s[n][k]
        for k in range(8):
            for i in range(k + 1, 8):
                lines[i] = lines[i] - factor[i][k] * lines[k]
        solved = [lines[k] * inv[k] for k in range(8)]
        for i in range(7, 0, -1):
            for k in range(i):
                solved[k] = solved[k] - factor[i][k] * solved[i]
        for h in range(g + 1, min(g + 2, groups)):
            value = jnp.where(own, 0.0, rows[h])
            c = cols[h - g - 1]
            first = (c[0] * solved[0] + c[1] * solved[1]) + (c[2] * solved[2] + c[3] * solved[3])
            second = (c[4] * solved[4] + c[5] * solved[5]) + (c[6] * solved[6] + c[7] * solved[7])
            rows[h] = value - (first + second)
        if g + 2 < groups:
            tight = solved[0]
            for k in range(1, 8):
                tight = jnp.where(sub == k, solved[k], tight)
            zero = jnp.zeros_like(tight)
            wide = jnp.concatenate([tight if n == g else zero for n in range(groups)], axis=0)
            tall = jnp.concatenate(rows[g + 2 :], axis=0)
            change = mul(split(tall), split(wide))
            for h in range(g + 2, groups):
                n = 8 * (h - g - 2)
                rows[h] = jnp.where(own, 0.0, rows[h]) - change[n : n + 8, :]
        row = lines[0] * jnp.sqrt(inv[0])
        for k in range(1, 8):
            row = jnp.where(sub == k, lines[k] * jnp.sqrt(inv[k]), row)
        out.append(jnp.where(lane <= sub + 8 * g, row, 0.0))
    return jnp.concatenate(out, axis=0)


def orth_factor(gram, low_inv):
    n = gram.shape[0]
    blocks = n // BLOCK
    low_inv[...] = jnp.zeros_like(low_inv)
    at = [pl.ds(k * BLOCK, BLOCK) for k in range(blocks)]

    def diagonal(k):
        return [gram[pl.ds(k * BLOCK + 8 * g, 8), at[k]] for g in range(BLOCK // 8)]

    inv = inverse_factor(diagonal(0))
    for k in range(blocks):
        inv_s = split(inv)
        low_inv[at[k], at[k]] = inv
        panel = {}
        if k + 1 < blocks:
            panel[k + 1] = split(mul(inv_s, split(gram[at[k], at[k + 1]])))
            gram[at[k + 1], at[k + 1]] -= mul(panel[k + 1], panel[k + 1], ((0,), (0,)))
            following = inverse_factor(diagonal(k + 1))
        if k:
            before = pl.ds(0, k * BLOCK)
            low_inv[at[k], before] = mul(inv_s, split(low_inv[at[k], before]))
        so_far = pl.ds(0, (k + 1) * BLOCK)
        mine = split(low_inv[at[k], so_far])
        for i in range(k + 1, blocks):
            if i not in panel:
                panel[i] = split(mul(inv_s, split(gram[at[k], at[i]])))
            low_inv[at[i], so_far] -= mul(panel[i], mine, ((0,), (0,)))
            for j in range(i, blocks):
                if j not in panel:
                    panel[j] = split(mul(inv_s, split(gram[at[k], at[j]])))
                if (i, j) != (k + 1, k + 1):
                    gram[at[i], at[j]] -= mul(panel[i], panel[j], ((0,), (0,)))
        if k + 1 < blocks:
            inv = following


def fill_grams(full, g_high, g_low):
    @pl.loop(0, 2 * HALF)
    def _(z):
        here = pl.ds(pl.multiple_of(z * BLOCK, BLOCK), BLOCK)
        for c in range(2):
            for k in range(HALF + 1):
                there = pl.ds(pl.multiple_of(((z + k) % 8) * BLOCK, BLOCK), BLOCK)
                value = full[here, pl.ds((c * (HALF + 1) + k) * BLOCK, BLOCK)]
                g_high[c, here, there], g_low[c, here, there] = split(value)
                if 0 < k < HALF:
                    g_high[c, there, here], g_low[c, there, here] = split(value.T)


def sketch_kernel(full, acts, basis_out, last_out, gram, low_inv, high_z, low_z, g_high, g_low):
    tokens = full.shape[0]
    rank = gram.shape[0]
    share = basis_out.shape[0]
    high, low = split(full[:, pl.ds(2 * (HALF + 1) * BLOCK, rank)])
    high_z[...] = high
    low_z[...] = low
    fill_grams(full, g_high, g_low)

    def step(n, carry):
        z_s = (high_z[...], low_z[...])
        h = mul((g_high[n % 2], g_low[n % 2]), z_s)
        gram[...] = mul(z_s, split(h), ((0,), (0,))) * (2.0**-33)
        orth_factor(gram, low_inv)

        @pl.when(n < 2)
        def _():
            high, low = split(mul(split(h * (1.0 / 1024)), split(low_inv[...]), ((1,), (1,))))
            high_z[...] = high
            low_z[...] = low

        return carry

    lax.fori_loop(0, 3, step, 0)
    index = lax.axis_index("mp") * 4 + lax.axis_index("dp")
    rows = low_inv[pl.ds(pl.multiple_of(index * share, share), share), :]
    coeff = split(mul(split(rows), (high_z[...], low_z[...]), ((1,), (1,))) * (1.0 / 1024))
    last = split(mul(coeff, (g_high[0], g_low[0])) * (1.0 / 1024))

    def apply(pair, c):
        def dot(a):
            return jnp.dot(a, acts[c], preferred_element_type=jnp.float32)

        return dot(pair[0]) + dot(pair[1])

    basis_out[...] = apply(coeff, 0)
    last_out[...] = apply(last, 1)


def sketch_call(full, acts):
    tokens = full.shape[0]
    rank = full.shape[1] - 2 * (HALF + 1) * BLOCK
    features = acts.shape[2]
    shape = jax.ShapeDtypeStruct((rank // 16, features), jnp.float32)
    return pl.pallas_call(
        sketch_kernel,
        out_shape=(shape, shape),
        in_specs=[pl.BlockSpec(memory_space=pltpu.VMEM)] * 2,
        out_specs=(pl.BlockSpec(memory_space=pltpu.VMEM),) * 2,
        scratch_shapes=[
            pltpu.VMEM((rank, rank), jnp.float32),
            pltpu.VMEM((rank, rank), jnp.float32),
            pltpu.VMEM((tokens, rank), jnp.bfloat16),
            pltpu.VMEM((tokens, rank), jnp.bfloat16),
            pltpu.VMEM((2, tokens, tokens), jnp.bfloat16),
            pltpu.VMEM((2, tokens, tokens), jnp.bfloat16),
        ],
        compiler_params=pltpu.CompilerParams(vmem_limit_bytes=36 * 2**20),
    )(full, acts)


MESH = pl.DeviceIdType.MESH
VMEM = pl.BlockSpec(memory_space=pltpu.VMEM)


class Sender:
    def __init__(self, send, recv):
        self.send, self.recv, self.all = send, recv, []

    def __call__(self, source, target, device):
        n = len(self.all)
        copy = pltpu.make_async_remote_copy(
            src_ref=source,
            dst_ref=target,
            send_sem=self.send.at[n],
            recv_sem=self.recv.at[n],
            device_id=device,
            device_id_type=MESH,
        )
        copy.start()
        self.all.append(copy)
        return copy

    def finish(self):
        for copy in self.all:
            copy.wait_send()


def greet(peers):
    barrier = pltpu.get_barrier_semaphore()
    for peer in peers:
        pl.semaphore_signal(barrier, inc=1, device_id=peer, device_id_type=MESH)
    pl.semaphore_wait(barrier, len(peers))


def grid_place():
    t = lax.axis_index("tensor")
    return t // 4, t % 4


def ring(send, block, upper, lower, me, toward):
    right, left = (me + 1) % 4, (me + 3) % 4
    from_left = send(block(me), block(me), toward(right))
    from_right = send(block(me), block(me), toward(left))

    def forward():
        from_left.wait_recv()
        first = send(upper(left), upper(left), toward(right))
        from_right.wait_recv()
        second = send(lower(right), lower(right), toward(left))
        return first, second

    return forward


def crossed_rings(send, plans, middle=None):
    def along_first(plan):
        cell, me, toward, me_next, _ = plan
        return ring(send, *(lambda i, p=p: cell(i, me_next, p) for p in range(3)), me, toward)

    def along_second(plan, shift):
        cell, me, _, me_next, toward_next = plan
        i = (me + shift) % 4
        return ring(send, *(lambda j, p=p: cell(i, j, p) for p in range(3)), me_next, toward_next)

    first = [along_first(plan) for plan in plans]
    own = [along_second(plan, 0) for plan in plans]
    last = [copy for forward in first for copy in forward()]
    sides = [along_second(plan, shift) for shift in (3, 1) for plan in plans]
    pending = [copy for forward in own for copy in forward()]
    for copy in last:
        copy.wait_recv()
    opposite = [along_second(plan, 2) for plan in plans]
    if middle is not None:
        middle()
    for forward in sides + opposite:
        pending += forward()
    return pending


def along_x(y):
    return lambda i: {"tensor": i * 4 + y}


def along_y(x):
    return lambda i: {"tensor": x * 4 + i}


def xy_neighbours(x, y):
    return [
        {"tensor": ((x + 1) % 4) * 4 + y},
        {"tensor": ((x + 3) % 4) * 4 + y},
        {"tensor": x * 4 + (y + 1) % 4},
        {"tensor": x * 4 + (y + 3) % 4},
    ]


def tokens_kernel(x_ref, out, send_sem, recv_sem):
    x, y = grid_place()
    m = lax.axis_index("mp")
    mates = [{"mp": (m + d) % 4} for d in range(1, 4)]
    greet(mates + xy_neighbours(x, y))
    send = Sender(send_sem, recv_sem)
    rows = x_ref.shape[0]
    half = x_ref.shape[1] // 2
    mine = pl.ds(pl.multiple_of(m * rows, rows), rows)
    first = [send(x_ref, out.at[x, y, mine], mate) for mate in mates]
    out[x, y, mine] = x_ref[...]
    for copy in first:
        copy.wait_recv()
    count = 4 * rows
    a, b = pl.ds(0, half), pl.ds(half, half)
    up, down = pl.ds(0, count // 2), pl.ds(count // 2, count // 2)
    part = slice(None), up, down
    plan_a = (lambda i, j, p: out.at[i, j, part[p], a], x, along_x(y), y, along_y(x))
    plan_b = (lambda i, j, p: out.at[j, i, part[p], b], y, along_y(x), x, along_x(y))
    for copy in crossed_rings(send, (plan_a, plan_b)):
        copy.wait_recv()
    send.finish()


def remote_call(kernel, out_shape, copies, number, limit, scratch=()):
    return pl.pallas_call(
        kernel,
        out_shape=out_shape,
        out_specs=VMEM,
        scratch_shapes=[
            *scratch,
            pltpu.SemaphoreType.DMA((copies,)),
            pltpu.SemaphoreType.DMA((copies,)),
        ],
        compiler_params=pltpu.CompilerParams(
            collective_id=number, has_side_effects=True, vmem_limit_bytes=limit * 2**20
        ),
    )


def gather_tokens(tokens):
    rows, features = tokens.shape
    out = jax.ShapeDtypeStruct((4, 4, 4 * rows, features), tokens.dtype)
    return remote_call(tokens_kernel, out, 43, 0, 12)(tokens)


def project_kernel(x_ref, gain_ref, gate_ref, up_ref, part, squares):
    def dot(a, b):
        return lax.dot_general(a, b, (((1,), (1,)), ((), ())), preferred_element_type=jnp.float32)

    features = x_ref.shape[1]
    units = gate_ref.shape[1]
    values = x_ref[...].astype(jnp.float32)
    high, low = split(values * values)
    ones = jnp.ones((8, features), jnp.bfloat16)
    squares[...] = dot(ones, high) + dot(ones, low)
    lanes = pl.ds(pl.multiple_of(lax.axis_index("dp") * features, 128), features)
    for c in range(2):
        scaled = (values * gain_ref[c : c + 1, lanes]).astype(jnp.bfloat16)
        row = 2 * c * units
        part[pl.ds(row, units), :] = dot(gate_ref[c], scaled).astype(jnp.bfloat16)
        part[pl.ds(row + units, units), :] = dot(up_ref[c], scaled).astype(jnp.bfloat16)


def project(tokens, norm_gain, gate_weight, up_weight):
    count, features = tokens.shape
    units = gate_weight.shape[2]
    step = 256
    whole = pl.BlockSpec((2, units, features), lambda i: (0, 0, 0))
    return pl.pallas_call(
        project_kernel,
        grid=(count // step,),
        out_shape=(
            jax.ShapeDtypeStruct((4 * units, count), jnp.bfloat16),
            jax.ShapeDtypeStruct((8, count), jnp.float32),
        ),
        in_specs=[
            pl.BlockSpec((step, features), lambda i: (i, 0)),
            pl.BlockSpec(norm_gain.shape, lambda i: (0, 0)),
            whole,
            whole,
        ],
        out_specs=(
            pl.BlockSpec((4 * units, step), lambda i: (0, i)),
            pl.BlockSpec((8, step), lambda i: (0, i)),
        ),
        compiler_params=pltpu.CompilerParams(vmem_limit_bytes=40 * 2**20),
    )(tokens, norm_gain, gate_weight.swapaxes(1, 2), up_weight.swapaxes(1, 2))


def hidden_kernel(part, squares, out, near, near_sq, pair, pair_sq, far, far_sq, send_sem, recv_sem):
    x, y = grid_place()
    d = lax.axis_index("dp")
    z, core = d // 2, d % 2
    sibling, partner = {"dp": z * 2 + 1 - core}, {"dp": (1 - z) * 2 + core}
    greet([sibling, partner] + xy_neighbours(x, y))
    send = Sender(send_sem, recv_sem)
    units, tokens = out.shape[3], out.shape[4]
    chunk = tokens // 2
    step = 32

    def share(zh, side, h=None):
        start = (zh * 2 + side) * tokens
        if h is None:
            return pl.ds(pl.multiple_of(start, 128), tokens)
        return pl.ds(pl.multiple_of(start + h * chunk, 128), chunk)

    first_sq = send(squares.at[:, share(1 - z, 1 - core)], near_sq.at[1], sibling)
    first = [
        send(part.at[:, share(1 - z, 1 - core, h)], near.at[1, h], sibling) for h in range(2)
    ]
    second_sq = send(squares.at[:, share(z, 1 - core)], near_sq.at[0], sibling)
    second = [send(part.at[:, share(z, 1 - core, h)], near.at[0, h], sibling) for h in range(2)]

    first_sq.wait_recv()
    pair_sq[...] = squares[:, share(1 - z, core)] + near_sq[1]
    across_sq = send(pair_sq, far_sq, partner)
    across = []
    for h in range(2):
        first[h].wait_recv()

        @pl.loop(0, 4 * units // step)
        def _(i):
            rows = pl.ds(pl.multiple_of(i * step, step), step)
            total = part[rows, share(1 - z, core, h)].astype(jnp.float32) + near[
                1, h, rows, :
            ].astype(jnp.float32)
            pair[h, rows, :] = total.astype(jnp.bfloat16)

        across.append(send(pair.at[h], far.at[h], partner))

    second_sq.wait_recv()
    across_sq.wait_recv()
    square_total = squares[:, share(z, core)] + near_sq[0] + far_sq[...]
    root = lax.rsqrt(square_total[0:1, :] / D + EPSILON)

    def activate(h):
        second[h].wait_recv()
        across[h].wait_recv()
        lanes = pl.ds(h * chunk, chunk)
        scale = root[:, h * chunk : (h + 1) * chunk]
        for c in range(2):

            @pl.loop(0, units // step)
            def _(i):
                def total(row):
                    rows = pl.ds(pl.multiple_of(row + i * step, step), step)
                    return (
                        part[rows, share(z, core, h)].astype(jnp.float32)
                        + near[0, h, rows, :].astype(jnp.float32)
                        + far[h, rows, :].astype(jnp.float32)
                    ) * scale

                gate = total(c * 2 * units)
                up = total(c * 2 * units + units)
                value = gate / (1.0 + jnp.exp(-gate)) * up
                rows = pl.ds(pl.multiple_of(i * step, step), step)
                out[c, x, y, rows, lanes] = value.astype(jnp.bfloat16)

    upper, lower = pl.ds(0, units // 2), pl.ds(units // 2, units // 2)
    every = slice(None)
    two, rest = pl.ds(0, 2), pl.ds(2, 2)

    def start(h, phase):
        lanes = pl.ds(h * chunk, chunk)
        if phase == 0:
            return (
                ring(
                    send,
                    lambda i: out.at[0, i, y, :, lanes],
                    lambda i: out.at[0, i, y, upper, lanes],
                    lambda i: out.at[0, i, y, lower, lanes],
                    x,
                    along_x(y),
                ),
                ring(
                    send,
                    lambda i: out.at[1, x, i, :, lanes],
                    lambda i: out.at[1, x, i, upper, lanes],
                    lambda i: out.at[1, x, i, lower, lanes],
                    y,
                    along_y(x),
                ),
            )
        return (
            ring(
                send,
                lambda i: out.at[0, every, i, :, lanes],
                lambda i: out.at[0, two, i, :, lanes],
                lambda i: out.at[0, rest, i, :, lanes],
                y,
                along_y(x),
            ),
            ring(
                send,
                lambda i: out.at[1, i, every, :, lanes],
                lambda i: out.at[1, i, two, :, lanes],
                lambda i: out.at[1, i, rest, :, lanes],
                x,
                along_x(y),
            ),
        )

    def forward(pair_of_rings):
        return [copy for one in pair_of_rings for copy in one()]

    def settle(copies):
        for copy in copies:
            copy.wait_recv()

    activate(0)
    rings = start(0, 0)
    settle(forward(rings))
    early = start(0, 1)
    activate(1)
    rings = start(1, 0)
    tail = forward(early)
    settle(forward(rings))
    tail += forward(start(1, 1))
    settle(tail)
    send.finish()


def sum_and_gather_hidden(part, squares):
    rows, tokens = part.shape[0], part.shape[1] // lax.axis_size("dp")
    out = jax.ShapeDtypeStruct((2, 4, 4, rows // 4, tokens), jnp.bfloat16)
    scratch = [
        pltpu.VMEM((2, 2, rows, tokens // 2), jnp.bfloat16),
        pltpu.VMEM((2, 8, tokens), jnp.float32),
        pltpu.VMEM((2, rows, tokens // 2), jnp.bfloat16),
        pltpu.VMEM((8, tokens), jnp.float32),
        pltpu.VMEM((2, rows, tokens // 2), jnp.bfloat16),
        pltpu.VMEM((8, tokens), jnp.float32),
    ]
    return remote_call(hidden_kernel, out, 41, 1, 24, scratch)(part, squares)


def acts_kernel(part, out, landed, send_sem, recv_sem):
    m, d = lax.axis_index("mp"), lax.axis_index("dp")
    zh, core = d // 2, d % 2
    z = zh * 4 + m
    mates = [{"mp": (m + k) % 4} for k in range(1, 4)]

    def at(chip):
        return {"mp": chip % 4, "dp": (chip // 4) * 2 + core}

    right, left = at((z + 1) % 8), at((z + 7) % 8)
    sibling = {"dp": zh * 2 + 1 - core}
    greet(mates + [right, left, sibling])
    send = Sender(send_sem, recv_sem)
    sums = [
        [
            send(part.at[(m + k) % 4, c], landed.at[k - 1, c], mates[k - 1])
            for k in (2, 1, 3)
        ]
        for c in range(2)
    ]
    half = part.shape[2] // 2
    halves = pl.ds(0, half), pl.ds(half, half)

    def block(c, chip):
        return out.at[c, chip * 2 + core]

    shared = []
    waiting = []
    for c in range(2):
        for copy in sums[c]:
            copy.wait_recv()
        total = part[m, c].astype(jnp.float32)
        for k in range(3):
            total += landed[k, c].astype(jnp.float32)
        out[c, z * 2 + core] = total.astype(jnp.bfloat16)
        here = block(c, z)
        waiting.append((send(here, here, right), send(here, here, left)))
        shared.append(send(here, here, sibling))
    for k in range(1, 4):
        before, after = (z + 8 - k) % 8, (z + k) % 8
        for c in range(2):
            from_left, from_right = waiting[c]
            near, next_near = block(c, before), block(c, after)
            on, back = near, next_near
            if k == 3:
                on = out.at[c, before * 2 + core, halves[0]]
                back = out.at[c, after * 2 + core, halves[1]]
            from_left.wait_recv()
            next_left = send(on, on, right)
            from_right.wait_recv()
            next_right = send(back, back, left)
            shared.append(send(near, near, sibling))
            shared.append(send(next_near, next_near, sibling))
            waiting[c] = (next_left, next_right)
    far = (z + 4) % 8
    for c in range(2):
        for copy in waiting[c]:
            copy.wait_recv()
        shared.append(send(block(c, far), block(c, far), sibling))
    for copy in shared:
        copy.wait_recv()
    send.finish()


def sum_and_gather_acts(part):
    _, copies, rows, features = part.shape
    out = jax.ShapeDtypeStruct((copies, 16, rows, features), jnp.bfloat16)
    scratch = [pltpu.VMEM((3, copies, rows, features), jnp.bfloat16)]
    return remote_call(acts_kernel, out, 38, 2, 12, scratch)(part)


def rows_kernel(part, out, landed, send_sem, recv_sem):
    t = lax.axis_index("tensor")
    x, y = grid_place()
    m, d = lax.axis_index("mp"), lax.axis_index("dp")
    zh, core = d // 2, d % 2
    z = zh * 4 + m
    width = part.shape[3] // 2

    def column(index):
        return pl.ds(pl.multiple_of((index % 2) * width, 128), width)

    peers = [{"tensor": (t + k) % 16} for k in range(1, 16)]

    def at(chip):
        return {"mp": chip % 4, "dp": (chip // 4) * 2 + core}

    chips = [at((z + k) % 8) for k in range(1, 8)]
    sibling = {"dp": zh * 2 + 1 - core}
    greet(peers + chips + [sibling])
    send = Sender(send_sem, recv_sem)
    sums = []
    for k in range(1, 16):
        u = (t + k) % 16
        source = part.at[u // 4, (u % 4) // 2, :, column(u)]
        sums.append(send(source, landed.at[k - 1], peers[k - 1]))
    total = part[x, y // 2, :, column(y)]
    for k in range(15):
        sums[k].wait_recv()
        total += landed[k]
    out[z, core, x, y // 2, :, column(y)] = total
    own = out.at[z, core, x, y // 2, :, column(y)]
    spread = [send(own, own, chip) for chip in chips]
    for copy in spread:
        copy.wait_recv()

    low = pl.ds(0, 4), pl.ds(0, 2), pl.ds(2, 2)
    high = pl.ds(4, 4), pl.ds(4, 2), pl.ds(6, 2)

    def cell(members, i, j):
        return out.at[members, core, i, j // 2, :, column(j)]

    plan_a = (lambda i, j, p: cell(low[p], i, j), x, along_x(y), y, along_y(x))
    plan_b = (lambda i, j, p: cell(high[p], j, i), y, along_y(x), x, along_x(y))
    shared = []

    def share(shift):
        across_a = cell(low[0], slice(None), (y + shift) % 4)
        across_b = out.at[high[0], core, (x + shift) % 4]
        shared.append(send(across_a, across_a, sibling))
        shared.append(send(across_b, across_b, sibling))

    pending = crossed_rings(send, (plan_a, plan_b), lambda: share(0))
    share(3)
    share(1)
    for copy in pending:
        copy.wait_recv()
    share(2)
    for copy in shared:
        copy.wait_recv()
    send.finish()


def sum_and_gather_rows(part):
    rows, width = part.shape
    out = jax.ShapeDtypeStruct((8, 2, 4, 2, rows // 8, width), jnp.float32)
    scratch = [pltpu.VMEM((15, rows // 8, width // 2), jnp.float32)]
    full = remote_call(rows_kernel, out, 70, 3, 24, scratch)(part.reshape(4, 2, rows // 8, width))
    return full.reshape(16 * rows, width)


def products_kernel(acts, sketch, out):
    d = lax.axis_index("dp")
    core = d % 2
    z = (d // 2) * 4 + lax.axis_index("mp")
    rows = out.shape[0]
    for c in range(2):
        mine = acts[c, z, pl.ds(pl.multiple_of(core * rows, rows), rows)]
        for k in range(HALF + 1):
            other = acts[c, lax.rem(z + k, 8)]
            lanes = pl.ds((c * (HALF + 1) + k) * BLOCK, BLOCK)
            out[:, lanes] = lax.dot_general(
                mine, other, (((1,), (1,)), ((), ())), preferred_element_type=jnp.float32
            )
    lanes = pl.ds(2 * (HALF + 1) * BLOCK, sketch.shape[1])
    out[:, lanes] = jnp.dot(mine, sketch[...], preferred_element_type=jnp.float32)


def row_products(acts, sketch):
    rows = acts.shape[2] // 2
    width = 2 * (HALF + 1) * BLOCK + sketch.shape[1]
    return pl.pallas_call(
        products_kernel,
        out_shape=jax.ShapeDtypeStruct((rows, width), jnp.float32),
        in_specs=[VMEM, VMEM],
        out_specs=VMEM,
        compiler_params=pltpu.CompilerParams(vmem_limit_bytes=12 * 2**20),
    )(acts, sketch)


def against(left, right, dims):
    return lax.dot_general(left, right, (dims, ((), ())), preferred_element_type=jnp.float32)


def on_device(tokens, norm_gain, gate_weight, up_weight, down_weight, sketch):
    feature_count = tokens.shape[1]
    gathered = gather_tokens(tokens).reshape(-1, feature_count)
    count = gathered.shape[0]
    part, squares = project(gathered, norm_gain, gate_weight, up_weight)
    hidden = sum_and_gather_hidden(part, squares)
    hidden = hidden.reshape(2, -1, hidden.shape[-1])
    partial_out = jnp.stack(
        [
            against(hidden[c], down_weight[c], ((0,), (0,))).astype(jnp.bfloat16)
            for c in range(2)
        ],
        axis=1,
    )
    share_mp = lax.axis_size("mp")
    partial_out = partial_out.reshape(share_mp, -1, 2, partial_out.shape[-1]).swapaxes(1, 2)
    blocks = sum_and_gather_acts(partial_out)
    acts = blocks.reshape(2, count, -1)
    rows = row_products(blocks.reshape(2, 8, count // 8, -1), sketch)
    full = sum_and_gather_rows(rows)
    basis_share, projected = sketch_call(full, acts)
    return (basis_share.T, projected.T)


def solution(mesh):
    return jax.shard_map(
        on_device,
        mesh=mesh,
        in_specs=(
            P(("mp", "tensor"), "dp"),
            P(),
            P(None, "dp", ("mp", "tensor")),
            P(None, "dp", ("mp", "tensor")),
            P(None, "mp", "tensor"),
            P("tensor", None),
        ),
        out_specs=(P("tensor", ("mp", "dp")), P("tensor", ("mp", "dp"))),
        check_vma=False,
    )
```

```python
import functools

import jax
import jax.numpy as jnp
from jax import lax
from jax.experimental import pallas as pl
from jax.experimental.pallas import tpu as pltpu
from jax.sharding import PartitionSpec as P

D = 8192
EPSILON = 1e-05
BLOCK = 128
HALF = 4


def split(value):
    high = value.astype(jnp.bfloat16)
    return high, (value - high.astype(jnp.float32)).astype(jnp.bfloat16)


def mul(left, right, contract=((1,), (0,))):
    def dot(a, b):
        return lax.dot_general(a, b, (contract, ((), ())), preferred_element_type=jnp.float32)

    (a, a_low), (b, b_low) = left, right
    return dot(a, b) + (dot(a, b_low) + dot(a_low, b))


def reciprocal(value):
    return 1.0 / value


def inverse_factor(rows):
    lane = lax.broadcasted_iota(jnp.int32, (8, BLOCK), 1)
    sub = lax.broadcasted_iota(jnp.int32, (8, BLOCK), 0)
    rows = list(rows)
    groups = BLOCK // 8

    def spread(value):
        return jnp.broadcast_to(value, (8, BLOCK))

    out = []
    for g in range(groups):
        own = (lane >= 8 * g) & (lane < 8 * g + 8)
        cols = [[spread(rows[h][:, 8 * g + k : 8 * g + k + 1]) for k in range(8)] for h in range(g + 1, min(g + 2, groups))]
        plain = [spread(rows[g][k : k + 1, :]) for k in range(8)]
        s = [
            [spread(plain[i][:, 8 * g + k : 8 * g + k + 1]) for k in range(i + 1)] for i in range(8)
        ]
        lines = [
            jnp.where(own, (lane == 8 * g + k).astype(jnp.float32), plain[k]) for k in range(8)
        ]
        factor = [[None] * 8 for _ in range(8)]
        inv = [None] * 8
        for k in range(8):
            inv[k] = reciprocal(s[k][k])
            for i in range(k + 1, 8):
                factor[i][k] = s[i][k] * inv[k]
            for i in range(k + 1, 8):
                for n in range(k + 1, i + 1):
                    s[i][n] = s[i][n] - factor[i][k] * s[n][k]
        for k in range(8):
            for i in range(k + 1, 8):
                lines[i] = lines[i] - factor[i][k] * lines[k]
        solved = [lines[k] * inv[k] for k in range(8)]
        for i in range(7, 0, -1):
            for k in range(i):
                solved[k] = solved[k] - factor[i][k] * solved[i]
        for h in range(g + 1, min(g + 2, groups)):
            value = jnp.where(own, 0.0, rows[h])
            c = cols[h - g - 1]
            first = (c[0] * solved[0] + c[1] * solved[1]) + (c[2] * solved[2] + c[3] * solved[3])
            second = (c[4] * solved[4] + c[5] * solved[5]) + (c[6] * solved[6] + c[7] * solved[7])
            rows[h] = value - (first + second)
        if g + 2 < groups:
            tight = solved[0]
            for k in range(1, 8):
                tight = jnp.where(sub == k, solved[k], tight)
            zero = jnp.zeros_like(tight)
            wide = jnp.concatenate([tight if n == g else zero for n in range(groups)], axis=0)
            tall = jnp.concatenate(rows[g + 2 :], axis=0)
            change = mul(split(tall), split(wide))
            for h in range(g + 2, groups):
                n = 8 * (h - g - 2)
                rows[h] = jnp.where(own, 0.0, rows[h]) - change[n : n + 8, :]
        row = lines[0] * jnp.sqrt(inv[0])
        for k in range(1, 8):
            row = jnp.where(sub == k, lines[k] * jnp.sqrt(inv[k]), row)
        out.append(jnp.where(lane <= sub + 8 * g, row, 0.0))
    return jnp.concatenate(out, axis=0)


def orth_factor(gram, low_inv):
    n = gram.shape[0]
    blocks = n // BLOCK
    low_inv[...] = jnp.zeros_like(low_inv)
    at = [pl.ds(k * BLOCK, BLOCK) for k in range(blocks)]

    def diagonal(k):
        return [gram[pl.ds(k * BLOCK + 8 * g, 8), at[k]] for g in range(BLOCK // 8)]

    inv = inverse_factor(diagonal(0))
    for k in range(blocks):
        inv_s = split(inv)
        low_inv[at[k], at[k]] = inv
        panel = {}
        if k + 1 < blocks:
            panel[k + 1] = split(mul(inv_s, split(gram[at[k], at[k + 1]])))
            gram[at[k + 1], at[k + 1]] -= mul(panel[k + 1], panel[k + 1], ((0,), (0,)))
            following = inverse_factor(diagonal(k + 1))
        if k:
            before = pl.ds(0, k * BLOCK)
            low_inv[at[k], before] = mul(inv_s, split(low_inv[at[k], before]))
        so_far = pl.ds(0, (k + 1) * BLOCK)
        mine = split(low_inv[at[k], so_far])
        for i in range(k + 1, blocks):
            if i not in panel:
                panel[i] = split(mul(inv_s, split(gram[at[k], at[i]])))
            low_inv[at[i], so_far] -= mul(panel[i], mine, ((0,), (0,)))
            for j in range(i, blocks):
                if j not in panel:
                    panel[j] = split(mul(inv_s, split(gram[at[k], at[j]])))
                if (i, j) != (k + 1, k + 1):
                    gram[at[i], at[j]] -= mul(panel[i], panel[j], ((0,), (0,)))
        if k + 1 < blocks:
            inv = following


def fill_grams(full, g_high, g_low):
    @pl.loop(0, 2 * HALF)
    def _(z):
        here = pl.ds(pl.multiple_of(z * BLOCK, BLOCK), BLOCK)
        for c in range(2):
            for k in range(HALF + 1):
                there = pl.ds(pl.multiple_of(((z + k) % 8) * BLOCK, BLOCK), BLOCK)
                value = full[here, pl.ds((c * (HALF + 1) + k) * BLOCK, BLOCK)]
                g_high[c, here, there], g_low[c, here, there] = split(value)
                if 0 < k < HALF:
                    g_high[c, there, here], g_low[c, there, here] = split(value.T)


def sketch_kernel(full, acts, basis_out, last_out, gram, low_inv, high_z, low_z, g_high, g_low):
    tokens = full.shape[0]
    rank = gram.shape[0]
    share = basis_out.shape[0]
    high, low = split(full[:, pl.ds(2 * (HALF + 1) * BLOCK, rank)])
    high_z[...] = high
    low_z[...] = low
    fill_grams(full, g_high, g_low)

    def step(n, carry):
        z_s = (high_z[...], low_z[...])
        h = mul((g_high[n % 2], g_low[n % 2]), z_s)
        gram[...] = mul(z_s, split(h), ((0,), (0,))) * (2.0**-33)
        orth_factor(gram, low_inv)

        @pl.when(n < 2)
        def _():
            high, low = split(mul(split(h * (1.0 / 1024)), split(low_inv[...]), ((1,), (1,))))
            high_z[...] = high
            low_z[...] = low

        return carry

    lax.fori_loop(0, 3, step, 0)
    index = lax.axis_index("mp") * 4 + lax.axis_index("dp")
    rows = low_inv[pl.ds(pl.multiple_of(index * share, share), share), :]
    coeff = split(mul(split(rows), (high_z[...], low_z[...]), ((1,), (1,))) * (1.0 / 1024))
    last = split(mul(coeff, (g_high[0], g_low[0])) * (1.0 / 1024))

    def apply(pair, c):
        def dot(a):
            return jnp.dot(a, acts[c], preferred_element_type=jnp.float32)

        return dot(pair[0]) + dot(pair[1])

    basis_out[...] = apply(coeff, 0)
    last_out[...] = apply(last, 1)


def sketch_call(full, acts):
    tokens = full.shape[0]
    rank = full.shape[1] - 2 * (HALF + 1) * BLOCK
    features = acts.shape[2]
    shape = jax.ShapeDtypeStruct((rank // 16, features), jnp.float32)
    return pl.pallas_call(
        sketch_kernel,
        out_shape=(shape, shape),
        in_specs=[pl.BlockSpec(memory_space=pltpu.VMEM)] * 2,
        out_specs=(pl.BlockSpec(memory_space=pltpu.VMEM),) * 2,
        scratch_shapes=[
            pltpu.VMEM((rank, rank), jnp.float32),
            pltpu.VMEM((rank, rank), jnp.float32),
            pltpu.VMEM((tokens, rank), jnp.bfloat16),
            pltpu.VMEM((tokens, rank), jnp.bfloat16),
            pltpu.VMEM((2, tokens, tokens), jnp.bfloat16),
            pltpu.VMEM((2, tokens, tokens), jnp.bfloat16),
        ],
        compiler_params=pltpu.CompilerParams(vmem_limit_bytes=36 * 2**20),
    )(full, acts)


MESH = pl.DeviceIdType.MESH
VMEM = pl.BlockSpec(memory_space=pltpu.VMEM)


class Sender:
    def __init__(self, send, recv):
        self.send, self.recv, self.all = send, recv, []

    def __call__(self, source, target, device):
        n = len(self.all)
        copy = pltpu.make_async_remote_copy(
            src_ref=source,
            dst_ref=target,
            send_sem=self.send.at[n],
            recv_sem=self.recv.at[n],
            device_id=device,
            device_id_type=MESH,
        )
        copy.start()
        self.all.append(copy)
        return copy

    def finish(self):
        for copy in self.all:
            copy.wait_send()


def greet(peers):
    barrier = pltpu.get_barrier_semaphore()
    for peer in peers:
        pl.semaphore_signal(barrier, inc=1, device_id=peer, device_id_type=MESH)
    pl.semaphore_wait(barrier, len(peers))


def grid_place():
    t = lax.axis_index("tensor")
    return t // 4, t % 4


def ring(send, block, upper, lower, me, toward):
    right, left = (me + 1) % 4, (me + 3) % 4
    from_left = send(block(me), block(me), toward(right))
    from_right = send(block(me), block(me), toward(left))

    def forward():
        from_left.wait_recv()
        first = send(upper(left), upper(left), toward(right))
        from_right.wait_recv()
        second = send(lower(right), lower(right), toward(left))
        return first, second

    return forward


def crossed_rings(send, plans, middle=None):
    def along_first(plan):
        cell, me, toward, me_next, _ = plan
        return ring(send, *(lambda i, p=p: cell(i, me_next, p) for p in range(3)), me, toward)

    def along_second(plan, shift):
        cell, me, _, me_next, toward_next = plan
        i = (me + shift) % 4
        return ring(send, *(lambda j, p=p: cell(i, j, p) for p in range(3)), me_next, toward_next)

    first = [along_first(plan) for plan in plans]
    own = [along_second(plan, 0) for plan in plans]
    last = [copy for forward in first for copy in forward()]
    sides = [along_second(plan, shift) for shift in (3, 1) for plan in plans]
    pending = [copy for forward in own for copy in forward()]
    for copy in last:
        copy.wait_recv()
    opposite = [along_second(plan, 2) for plan in plans]
    if middle is not None:
        middle()
    for forward in sides + opposite:
        pending += forward()
    return pending


def along_x(y):
    return lambda i: {"tensor": i * 4 + y}


def along_y(x):
    return lambda i: {"tensor": x * 4 + i}


def xy_neighbours(x, y):
    return [
        {"tensor": ((x + 1) % 4) * 4 + y},
        {"tensor": ((x + 3) % 4) * 4 + y},
        {"tensor": x * 4 + (y + 1) % 4},
        {"tensor": x * 4 + (y + 3) % 4},
    ]


def tokens_kernel(x_ref, out, send_sem, recv_sem):
    x, y = grid_place()
    m = lax.axis_index("mp")
    mates = [{"mp": (m + d) % 4} for d in range(1, 4)]
    greet(mates + xy_neighbours(x, y))
    send = Sender(send_sem, recv_sem)
    rows = x_ref.shape[0]
    half = x_ref.shape[1] // 2
    mine = pl.ds(pl.multiple_of(m * rows, rows), rows)
    first = [send(x_ref, out.at[x, y, mine], mate) for mate in mates]
    out[x, y, mine] = x_ref[...]
    for copy in first:
        copy.wait_recv()
    count = 4 * rows
    a, b = pl.ds(0, half), pl.ds(half, half)
    up, down = pl.ds(0, count // 2), pl.ds(count // 2, count // 2)
    part = slice(None), up, down
    plan_a = (lambda i, j, p: out.at[i, j, part[p], a], x, along_x(y), y, along_y(x))
    plan_b = (lambda i, j, p: out.at[j, i, part[p], b], y, along_y(x), x, along_x(y))
    for copy in crossed_rings(send, (plan_a, plan_b)):
        copy.wait_recv()
    send.finish()


def remote_call(kernel, out_shape, copies, number, limit, scratch=()):
    return pl.pallas_call(
        kernel,
        out_shape=out_shape,
        out_specs=VMEM,
        scratch_shapes=[
            *scratch,
            pltpu.SemaphoreType.DMA((copies,)),
            pltpu.SemaphoreType.DMA((copies,)),
        ],
        compiler_params=pltpu.CompilerParams(
            collective_id=number, has_side_effects=True, vmem_limit_bytes=limit * 2**20
        ),
    )


def gather_tokens(tokens):
    rows, features = tokens.shape
    out = jax.ShapeDtypeStruct((4, 4, 4 * rows, features), tokens.dtype)
    return remote_call(tokens_kernel, out, 43, 0, 12)(tokens)


def project_kernel(x_ref, gain_ref, gate_ref, up_ref, part, squares):
    def dot(a, b):
        return lax.dot_general(a, b, (((1,), (1,)), ((), ())), preferred_element_type=jnp.float32)

    features = x_ref.shape[1]
    units = gate_ref.shape[1]
    values = x_ref[...].astype(jnp.float32)
    high, low = split(values * values)
    ones = jnp.ones((8, features), jnp.bfloat16)
    squares[...] = dot(ones, high) + dot(ones, low)
    lanes = pl.ds(pl.multiple_of(lax.axis_index("dp") * features, 128), features)
    for c in range(2):
        scaled = (values * gain_ref[c : c + 1, lanes]).astype(jnp.bfloat16)
        row = 2 * c * units
        part[pl.ds(row, units), :] = dot(gate_ref[c], scaled).astype(jnp.bfloat16)
        part[pl.ds(row + units, units), :] = dot(up_ref[c], scaled).astype(jnp.bfloat16)


def project(tokens, norm_gain, gate_weight, up_weight):
    count, features = tokens.shape
    units = gate_weight.shape[2]
    step = 256
    whole = pl.BlockSpec((2, units, features), lambda i: (0, 0, 0))
    return pl.pallas_call(
        project_kernel,
        grid=(count // step,),
        out_shape=(
            jax.ShapeDtypeStruct((4 * units, count), jnp.bfloat16),
            jax.ShapeDtypeStruct((8, count), jnp.float32),
        ),
        in_specs=[
            pl.BlockSpec((step, features), lambda i: (i, 0)),
            pl.BlockSpec(norm_gain.shape, lambda i: (0, 0)),
            whole,
            whole,
        ],
        out_specs=(
            pl.BlockSpec((4 * units, step), lambda i: (0, i)),
            pl.BlockSpec((8, step), lambda i: (0, i)),
        ),
        compiler_params=pltpu.CompilerParams(vmem_limit_bytes=40 * 2**20),
    )(tokens, norm_gain, gate_weight.swapaxes(1, 2), up_weight.swapaxes(1, 2))


def hidden_kernel(part, squares, out, near, near_sq, pair, pair_sq, far, far_sq, send_sem, recv_sem):
    x, y = grid_place()
    d = lax.axis_index("dp")
    z, core = d // 2, d % 2
    sibling, partner = {"dp": z * 2 + 1 - core}, {"dp": (1 - z) * 2 + core}
    greet([sibling, partner] + xy_neighbours(x, y))
    send = Sender(send_sem, recv_sem)
    units, tokens = out.shape[3], out.shape[4]
    chunk = tokens // 2
    step = 32

    def share(zh, side, h=None):
        start = (zh * 2 + side) * tokens
        if h is None:
            return pl.ds(pl.multiple_of(start, 128), tokens)
        return pl.ds(pl.multiple_of(start + h * chunk, 128), chunk)

    first_sq = send(squares.at[:, share(1 - z, 1 - core)], near_sq.at[1], sibling)
    first = [
        send(part.at[:, share(1 - z, 1 - core, h)], near.at[1, h], sibling) for h in range(2)
    ]
    second_sq = send(squares.at[:, share(z, 1 - core)], near_sq.at[0], sibling)
    second = [send(part.at[:, share(z, 1 - core, h)], near.at[0, h], sibling) for h in range(2)]

    first_sq.wait_recv()
    pair_sq[...] = squares[:, share(1 - z, core)] + near_sq[1]
    across_sq = send(pair_sq, far_sq, partner)
    across = []
    for h in range(2):
        first[h].wait_recv()

        @pl.loop(0, 4 * units // step)
        def _(i):
            rows = pl.ds(pl.multiple_of(i * step, step), step)
            total = part[rows, share(1 - z, core, h)].astype(jnp.float32) + near[
                1, h, rows, :
            ].astype(jnp.float32)
            pair[h, rows, :] = total.astype(jnp.bfloat16)

        across.append(send(pair.at[h], far.at[h], partner))

    second_sq.wait_recv()
    across_sq.wait_recv()
    square_total = squares[:, share(z, core)] + near_sq[0] + far_sq[...]
    root = lax.rsqrt(square_total[0:1, :] / D + EPSILON)

    def activate(h):
        second[h].wait_recv()
        across[h].wait_recv()
        lanes = pl.ds(h * chunk, chunk)
        scale = root[:, h * chunk : (h + 1) * chunk]
        for c in range(2):

            @pl.loop(0, units // step)
            def _(i):
                def total(row):
                    rows = pl.ds(pl.multiple_of(row + i * step, step), step)
                    return (
                        part[rows, share(z, core, h)].astype(jnp.float32)
                        + near[0, h, rows, :].astype(jnp.float32)
                        + far[h, rows, :].astype(jnp.float32)
                    ) * scale

                gate = total(c * 2 * units)
                up = total(c * 2 * units + units)
                value = gate / (1.0 + jnp.exp(-gate)) * up
                rows = pl.ds(pl.multiple_of(i * step, step), step)
                out[c, x, y, rows, lanes] = value.astype(jnp.bfloat16)

    part_rows = slice(None), pl.ds(0, units // 2), pl.ds(units // 2, units // 2)
    pending = []
    for h in range(2):
        activate(h)
        lanes = pl.ds(h * chunk, chunk)

        def base(i, j, p, lanes=lanes):
            return out.at[0, i, j, part_rows[p], lanes]

        def instruct(i, j, p, lanes=lanes):
            return out.at[1, j, i, part_rows[p], lanes]

        plan_a = (base, x, along_x(y), y, along_y(x))
        plan_b = (instruct, y, along_y(x), x, along_x(y))
        pending += crossed_rings(send, (plan_a, plan_b))
    for copy in pending:
        copy.wait_recv()
    send.finish()


def sum_and_gather_hidden(part, squares):
    rows, tokens = part.shape[0], part.shape[1] // lax.axis_size("dp")
    out = jax.ShapeDtypeStruct((2, 4, 4, rows // 4, tokens), jnp.bfloat16)
    scratch = [
        pltpu.VMEM((2, 2, rows, tokens // 2), jnp.bfloat16),
        pltpu.VMEM((2, 8, tokens), jnp.float32),
        pltpu.VMEM((2, rows, tokens // 2), jnp.bfloat16),
        pltpu.VMEM((8, tokens), jnp.float32),
        pltpu.VMEM((2, rows, tokens // 2), jnp.bfloat16),
        pltpu.VMEM((8, tokens), jnp.float32),
    ]
    return remote_call(hidden_kernel, out, 89, 1, 24, scratch)(part, squares)


def acts_kernel(part, out, landed, send_sem, recv_sem):
    m, d = lax.axis_index("mp"), lax.axis_index("dp")
    zh, core = d // 2, d % 2
    z = zh * 4 + m
    mates = [{"mp": (m + k) % 4} for k in range(1, 4)]

    def at(chip):
        return {"mp": chip % 4, "dp": (chip // 4) * 2 + core}

    right, left = at((z + 1) % 8), at((z + 7) % 8)
    sibling = {"dp": zh * 2 + 1 - core}
    greet(mates + [right, left, sibling])
    send = Sender(send_sem, recv_sem)
    sums = [
        [
            send(part.at[(m + k) % 4, c], landed.at[k - 1, c], mates[k - 1])
            for k in (2, 1, 3)
        ]
        for c in range(2)
    ]
    half = part.shape[2] // 2
    halves = pl.ds(0, half), pl.ds(half, half)

    def block(c, chip):
        return out.at[c, chip * 2 + core]

    shared = []
    waiting = []
    for c in range(2):
        for copy in sums[c]:
            copy.wait_recv()
        total = part[m, c].astype(jnp.float32)
        for k in range(3):
            total += landed[k, c].astype(jnp.float32)
        out[c, z * 2 + core] = total.astype(jnp.bfloat16)
        here = block(c, z)
        waiting.append((send(here, here, right), send(here, here, left)))
        shared.append(send(here, here, sibling))
    for k in range(1, 4):
        before, after = (z + 8 - k) % 8, (z + k) % 8
        for c in range(2):
            from_left, from_right = waiting[c]
            near, next_near = block(c, before), block(c, after)
            on, back = near, next_near
            if k == 3:
                on = out.at[c, before * 2 + core, halves[0]]
                back = out.at[c, after * 2 + core, halves[1]]
            from_left.wait_recv()
            next_left = send(on, on, right)
            from_right.wait_recv()
            next_right = send(back, back, left)
            shared.append(send(near, near, sibling))
            shared.append(send(next_near, next_near, sibling))
            waiting[c] = (next_left, next_right)
    far = (z + 4) % 8
    for c in range(2):
        for copy in waiting[c]:
            copy.wait_recv()
        shared.append(send(block(c, far), block(c, far), sibling))
    for copy in shared:
        copy.wait_recv()
    send.finish()


def sum_and_gather_acts(part):
    _, copies, rows, features = part.shape
    out = jax.ShapeDtypeStruct((copies, 16, rows, features), jnp.bfloat16)
    scratch = [pltpu.VMEM((3, copies, rows, features), jnp.bfloat16)]
    return remote_call(acts_kernel, out, 38, 2, 12, scratch)(part)


def rows_kernel(part, out, landed, send_sem, recv_sem):
    t = lax.axis_index("tensor")
    x, y = grid_place()
    m, d = lax.axis_index("mp"), lax.axis_index("dp")
    zh, core = d // 2, d % 2
    z = zh * 4 + m
    width = part.shape[3] // 2

    def column(index):
        return pl.ds(pl.multiple_of((index % 2) * width, 128), width)

    peers = [{"tensor": (t + k) % 16} for k in range(1, 16)]

    def at(chip):
        return {"mp": chip % 4, "dp": (chip // 4) * 2 + core}

    chips = [at((z + k) % 8) for k in range(1, 8)]
    sibling = {"dp": zh * 2 + 1 - core}
    greet(peers + chips + [sibling])
    send = Sender(send_sem, recv_sem)
    sums = []
    for k in range(1, 16):
        u = (t + k) % 16
        source = part.at[u // 4, (u % 4) // 2, :, column(u)]
        sums.append(send(source, landed.at[k - 1], peers[k - 1]))
    total = part[x, y // 2, :, column(y)]
    for k in range(15):
        sums[k].wait_recv()
        total += landed[k]
    out[z, core, x, y // 2, :, column(y)] = total
    own = out.at[z, core, x, y // 2, :, column(y)]
    spread = [send(own, own, chip) for chip in chips]
    for copy in spread:
        copy.wait_recv()

    low = pl.ds(0, 4), pl.ds(0, 2), pl.ds(2, 2)
    high = pl.ds(4, 4), pl.ds(4, 2), pl.ds(6, 2)

    def cell(members, i, j):
        return out.at[members, core, i, j // 2, :, column(j)]

    plan_a = (lambda i, j, p: cell(low[p], i, j), x, along_x(y), y, along_y(x))
    plan_b = (lambda i, j, p: cell(high[p], j, i), y, along_y(x), x, along_x(y))
    shared = []

    def share(shift):
        across_a = cell(low[0], slice(None), (y + shift) % 4)
        across_b = out.at[high[0], core, (x + shift) % 4]
        shared.append(send(across_a, across_a, sibling))
        shared.append(send(across_b, across_b, sibling))

    pending = crossed_rings(send, (plan_a, plan_b), lambda: share(0))
    share(3)
    share(1)
    for copy in pending:
        copy.wait_recv()
    share(2)
    for copy in shared:
        copy.wait_recv()
    send.finish()


def sum_and_gather_rows(part):
    rows, width = part.shape
    out = jax.ShapeDtypeStruct((8, 2, 4, 2, rows // 8, width), jnp.float32)
    scratch = [pltpu.VMEM((15, rows // 8, width // 2), jnp.float32)]
    full = remote_call(rows_kernel, out, 70, 3, 24, scratch)(part.reshape(4, 2, rows // 8, width))
    return full.reshape(16 * rows, width)


def products_kernel(acts, sketch, out):
    d = lax.axis_index("dp")
    core = d % 2
    z = (d // 2) * 4 + lax.axis_index("mp")
    rows = out.shape[0]
    for c in range(2):
        mine = acts[c, z, pl.ds(pl.multiple_of(core * rows, rows), rows)]
        for k in range(HALF + 1):
            other = acts[c, lax.rem(z + k, 8)]
            lanes = pl.ds((c * (HALF + 1) + k) * BLOCK, BLOCK)
            out[:, lanes] = lax.dot_general(
                mine, other, (((1,), (1,)), ((), ())), preferred_element_type=jnp.float32
            )
    lanes = pl.ds(2 * (HALF + 1) * BLOCK, sketch.shape[1])
    out[:, lanes] = jnp.dot(mine, sketch[...], preferred_element_type=jnp.float32)


def row_products(acts, sketch):
    rows = acts.shape[2] // 2
    width = 2 * (HALF + 1) * BLOCK + sketch.shape[1]
    return pl.pallas_call(
        products_kernel,
        out_shape=jax.ShapeDtypeStruct((rows, width), jnp.float32),
        in_specs=[VMEM, VMEM],
        out_specs=VMEM,
        compiler_params=pltpu.CompilerParams(vmem_limit_bytes=12 * 2**20),
    )(acts, sketch)


def against(left, right, dims):
    return lax.dot_general(left, right, (dims, ((), ())), preferred_element_type=jnp.float32)


def on_device(tokens, norm_gain, gate_weight, up_weight, down_weight, sketch):
    feature_count = tokens.shape[1]
    gathered = gather_tokens(tokens).reshape(-1, feature_count)
    count = gathered.shape[0]
    part, squares = project(gathered, norm_gain, gate_weight, up_weight)
    hidden = sum_and_gather_hidden(part, squares)
    hidden = hidden.reshape(2, -1, hidden.shape[-1])
    partial_out = jnp.stack(
        [
            against(hidden[c], down_weight[c], ((0,), (0,))).astype(jnp.bfloat16)
            for c in range(2)
        ],
        axis=1,
    )
    share_mp = lax.axis_size("mp")
    partial_out = partial_out.reshape(share_mp, -1, 2, partial_out.shape[-1]).swapaxes(1, 2)
    blocks = sum_and_gather_acts(partial_out)
    acts = blocks.reshape(2, count, -1)
    rows = row_products(blocks.reshape(2, 8, count // 8, -1), sketch)
    full = sum_and_gather_rows(rows)
    basis_share, projected = sketch_call(full, acts)
    return (basis_share.T, projected.T)


def solution(mesh):
    return jax.shard_map(
        on_device,
        mesh=mesh,
        in_specs=(
            P(("mp", "tensor"), "dp"),
            P(),
            P(None, "dp", ("mp", "tensor")),
            P(None, "dp", ("mp", "tensor")),
            P(None, "mp", "tensor"),
            P("tensor", None),
        ),
        out_specs=(P("tensor", ("mp", "dp")), P("tensor", ("mp", "dp"))),
        check_vma=False,
    )
```

```python
import functools

import jax
import jax.numpy as jnp
from jax import lax
from jax.experimental import pallas as pl
from jax.experimental.pallas import tpu as pltpu
from jax.sharding import PartitionSpec as P

D = 8192
EPSILON = 1e-05
BLOCK = 128
HALF = 4


def split(value):
    high = value.astype(jnp.bfloat16)
    return high, (value - high.astype(jnp.float32)).astype(jnp.bfloat16)


def mul(left, right, contract=((1,), (0,))):
    def dot(a, b):
        return lax.dot_general(a, b, (contract, ((), ())), preferred_element_type=jnp.float32)

    (a, a_low), (b, b_low) = left, right
    return dot(a, b) + (dot(a, b_low) + dot(a_low, b))


def reciprocal(value):
    return 1.0 / value


def inverse_factor(rows):
    lane = lax.broadcasted_iota(jnp.int32, (8, BLOCK), 1)
    sub = lax.broadcasted_iota(jnp.int32, (8, BLOCK), 0)
    rows = list(rows)
    groups = BLOCK // 8

    def spread(value):
        return jnp.broadcast_to(value, (8, BLOCK))

    out = []
    for g in range(groups):
        own = (lane >= 8 * g) & (lane < 8 * g + 8)
        cols = [[spread(rows[h][:, 8 * g + k : 8 * g + k + 1]) for k in range(8)] for h in range(g + 1, min(g + 2, groups))]
        plain = [spread(rows[g][k : k + 1, :]) for k in range(8)]
        s = [
            [spread(plain[i][:, 8 * g + k : 8 * g + k + 1]) for k in range(i + 1)] for i in range(8)
        ]
        lines = [
            jnp.where(own, (lane == 8 * g + k).astype(jnp.float32), plain[k]) for k in range(8)
        ]
        factor = [[None] * 8 for _ in range(8)]
        inv = [None] * 8
        for k in range(8):
            inv[k] = reciprocal(s[k][k])
            for i in range(k + 1, 8):
                factor[i][k] = s[i][k] * inv[k]
            for i in range(k + 1, 8):
                for n in range(k + 1, i + 1):
                    s[i][n] = s[i][n] - factor[i][k] * s[n][k]
        for k in range(8):
            for i in range(k + 1, 8):
                lines[i] = lines[i] - factor[i][k] * lines[k]
        solved = [lines[k] * inv[k] for k in range(8)]
        for i in range(7, 0, -1):
            for k in range(i):
                solved[k] = solved[k] - factor[i][k] * solved[i]
        for h in range(g + 1, min(g + 2, groups)):
            value = jnp.where(own, 0.0, rows[h])
            c = cols[h - g - 1]
            first = (c[0] * solved[0] + c[1] * solved[1]) + (c[2] * solved[2] + c[3] * solved[3])
            second = (c[4] * solved[4] + c[5] * solved[5]) + (c[6] * solved[6] + c[7] * solved[7])
            rows[h] = value - (first + second)
        if g + 2 < groups:
            tight = solved[0]
            for k in range(1, 8):
                tight = jnp.where(sub == k, solved[k], tight)
            zero = jnp.zeros_like(tight)
            wide = jnp.concatenate([tight if n == g else zero for n in range(groups)], axis=0)
            tall = jnp.concatenate(rows[g + 2 :], axis=0)
            change = mul(split(tall), split(wide))
            for h in range(g + 2, groups):
                n = 8 * (h - g - 2)
                rows[h] = jnp.where(own, 0.0, rows[h]) - change[n : n + 8, :]
        row = lines[0] * jnp.sqrt(inv[0])
        for k in range(1, 8):
            row = jnp.where(sub == k, lines[k] * jnp.sqrt(inv[k]), row)
        out.append(jnp.where(lane <= sub + 8 * g, row, 0.0))
    return jnp.concatenate(out, axis=0)


def orth_factor(gram, low_inv):
    n = gram.shape[0]
    blocks = n // BLOCK
    low_inv[...] = jnp.zeros_like(low_inv)
    at = [pl.ds(k * BLOCK, BLOCK) for k in range(blocks)]

    def diagonal(k):
        return [gram[pl.ds(k * BLOCK + 8 * g, 8), at[k]] for g in range(BLOCK // 8)]

    inv = inverse_factor(diagonal(0))
    for k in range(blocks):
        inv_s = split(inv)
        low_inv[at[k], at[k]] = inv
        panel = {}
        if k + 1 < blocks:
            panel[k + 1] = split(mul(inv_s, split(gram[at[k], at[k + 1]])))
            gram[at[k + 1], at[k + 1]] -= mul(panel[k + 1], panel[k + 1], ((0,), (0,)))
            following = inverse_factor(diagonal(k + 1))
        if k:
            before = pl.ds(0, k * BLOCK)
            low_inv[at[k], before] = mul(inv_s, split(low_inv[at[k], before]))
        so_far = pl.ds(0, (k + 1) * BLOCK)
        mine = split(low_inv[at[k], so_far])
        for i in range(k + 1, blocks):
            if i not in panel:
                panel[i] = split(mul(inv_s, split(gram[at[k], at[i]])))
            low_inv[at[i], so_far] -= mul(panel[i], mine, ((0,), (0,)))
            for j in range(i, blocks):
                if j not in panel:
                    panel[j] = split(mul(inv_s, split(gram[at[k], at[j]])))
                if (i, j) != (k + 1, k + 1):
                    gram[at[i], at[j]] -= mul(panel[i], panel[j], ((0,), (0,)))
        if k + 1 < blocks:
            inv = following


def fill_grams(full, g_high, g_low):
    @pl.loop(0, 2 * HALF)
    def _(z):
        here = pl.ds(pl.multiple_of(z * BLOCK, BLOCK), BLOCK)
        for c in range(2):
            for k in range(HALF + 1):
                there = pl.ds(pl.multiple_of(((z + k) % 8) * BLOCK, BLOCK), BLOCK)
                value = full[here, pl.ds((c * (HALF + 1) + k) * BLOCK, BLOCK)]
                g_high[c, here, there], g_low[c, here, there] = split(value)
                if 0 < k < HALF:
                    g_high[c, there, here], g_low[c, there, here] = split(value.T)


def sketch_kernel(full, acts, basis_out, last_out, gram, low_inv, high_z, low_z, g_high, g_low):
    tokens = full.shape[0]
    rank = gram.shape[0]
    share = basis_out.shape[0]
    high, low = split(full[:, pl.ds(2 * (HALF + 1) * BLOCK, rank)])
    high_z[...] = high
    low_z[...] = low
    fill_grams(full, g_high, g_low)

    def step(n, carry):
        z_s = (high_z[...], low_z[...])
        h = mul((g_high[n % 2], g_low[n % 2]), z_s)
        gram[...] = mul(z_s, split(h), ((0,), (0,))) * (2.0**-33)
        orth_factor(gram, low_inv)

        @pl.when(n < 2)
        def _():
            high, low = split(mul(split(h * (1.0 / 1024)), split(low_inv[...]), ((1,), (1,))))
            high_z[...] = high
            low_z[...] = low

        return carry

    lax.fori_loop(0, 3, step, 0)
    index = lax.axis_index("mp") * 4 + lax.axis_index("dp")
    rows = low_inv[pl.ds(pl.multiple_of(index * share, share), share), :]
    coeff = split(mul(split(rows), (high_z[...], low_z[...]), ((1,), (1,))) * (1.0 / 1024))
    last = split(mul(coeff, (g_high[0], g_low[0])) * (1.0 / 1024))

    def apply(pair, c):
        def dot(a):
            return jnp.dot(a, acts[c], preferred_element_type=jnp.float32)

        return dot(pair[0]) + dot(pair[1])

    basis_out[...] = apply(coeff, 0)
    last_out[...] = apply(last, 1)


def sketch_call(full, acts):
    tokens = full.shape[0]
    rank = full.shape[1] - 2 * (HALF + 1) * BLOCK
    features = acts.shape[2]
    shape = jax.ShapeDtypeStruct((rank // 16, features), jnp.float32)
    return pl.pallas_call(
        sketch_kernel,
        out_shape=(shape, shape),
        in_specs=[pl.BlockSpec(memory_space=pltpu.VMEM)] * 2,
        out_specs=(pl.BlockSpec(memory_space=pltpu.VMEM),) * 2,
        scratch_shapes=[
            pltpu.VMEM((rank, rank), jnp.float32),
            pltpu.VMEM((rank, rank), jnp.float32),
            pltpu.VMEM((tokens, rank), jnp.bfloat16),
            pltpu.VMEM((tokens, rank), jnp.bfloat16),
            pltpu.VMEM((2, tokens, tokens), jnp.bfloat16),
            pltpu.VMEM((2, tokens, tokens), jnp.bfloat16),
        ],
        compiler_params=pltpu.CompilerParams(vmem_limit_bytes=36 * 2**20),
    )(full, acts)


MESH = pl.DeviceIdType.MESH
VMEM = pl.BlockSpec(memory_space=pltpu.VMEM)


class Sender:
    def __init__(self, send, recv):
        self.send, self.recv, self.all = send, recv, []

    def __call__(self, source, target, device):
        n = len(self.all)
        copy = pltpu.make_async_remote_copy(
            src_ref=source,
            dst_ref=target,
            send_sem=self.send.at[n],
            recv_sem=self.recv.at[n],
            device_id=device,
            device_id_type=MESH,
        )
        copy.start()
        self.all.append(copy)
        return copy

    def finish(self):
        for copy in self.all:
            copy.wait_send()


def greet(peers):
    barrier = pltpu.get_barrier_semaphore()
    for peer in peers:
        pl.semaphore_signal(barrier, inc=1, device_id=peer, device_id_type=MESH)
    pl.semaphore_wait(barrier, len(peers))


def grid_place():
    t = lax.axis_index("tensor")
    return t // 4, t % 4


def ring(send, block, upper, lower, me, toward):
    right, left = (me + 1) % 4, (me + 3) % 4
    from_left = send(block(me), block(me), toward(right))
    from_right = send(block(me), block(me), toward(left))

    def forward():
        from_left.wait_recv()
        first = send(upper(left), upper(left), toward(right))
        from_right.wait_recv()
        second = send(lower(right), lower(right), toward(left))
        return first, second

    return forward


def crossed_rings(send, plans, middle=None):
    def along_first(plan):
        cell, me, toward, me_next, _ = plan
        return ring(send, *(lambda i, p=p: cell(i, me_next, p) for p in range(3)), me, toward)

    def along_second(plan, shift):
        cell, me, _, me_next, toward_next = plan
        i = (me + shift) % 4
        return ring(send, *(lambda j, p=p: cell(i, j, p) for p in range(3)), me_next, toward_next)

    first = [along_first(plan) for plan in plans]
    own = [along_second(plan, 0) for plan in plans]
    last = [copy for forward in first for copy in forward()]
    sides = [along_second(plan, shift) for shift in (3, 1) for plan in plans]
    pending = [copy for forward in own for copy in forward()]
    for copy in last:
        copy.wait_recv()
    opposite = [along_second(plan, 2) for plan in plans]
    if middle is not None:
        middle()
    for forward in sides + opposite:
        pending += forward()
    return pending


def along_x(y):
    return lambda i: {"tensor": i * 4 + y}


def along_y(x):
    return lambda i: {"tensor": x * 4 + i}


def xy_neighbours(x, y):
    return [
        {"tensor": ((x + 1) % 4) * 4 + y},
        {"tensor": ((x + 3) % 4) * 4 + y},
        {"tensor": x * 4 + (y + 1) % 4},
        {"tensor": x * 4 + (y + 3) % 4},
    ]


def tokens_kernel(x_ref, out, send_sem, recv_sem):
    x, y = grid_place()
    m = lax.axis_index("mp")
    mates = [{"mp": (m + d) % 4} for d in range(1, 4)]
    greet(mates + xy_neighbours(x, y))
    send = Sender(send_sem, recv_sem)
    rows = x_ref.shape[0]
    half = x_ref.shape[1] // 2
    mine = pl.ds(pl.multiple_of(m * rows, rows), rows)
    first = [send(x_ref, out.at[x, y, mine], mate) for mate in mates]
    out[x, y, mine] = x_ref[...]
    for copy in first:
        copy.wait_recv()
    count = 4 * rows
    a, b = pl.ds(0, half), pl.ds(half, half)
    up, down = pl.ds(0, count // 2), pl.ds(count // 2, count // 2)
    part = slice(None), up, down
    plan_a = (lambda i, j, p: out.at[i, j, part[p], a], x, along_x(y), y, along_y(x))
    plan_b = (lambda i, j, p: out.at[j, i, part[p], b], y, along_y(x), x, along_x(y))
    for copy in crossed_rings(send, (plan_a, plan_b)):
        copy.wait_recv()
    send.finish()


def remote_call(kernel, out_shape, copies, number, limit, scratch=()):
    return pl.pallas_call(
        kernel,
        out_shape=out_shape,
        out_specs=VMEM,
        scratch_shapes=[
            *scratch,
            pltpu.SemaphoreType.DMA((copies,)),
            pltpu.SemaphoreType.DMA((copies,)),
        ],
        compiler_params=pltpu.CompilerParams(
            collective_id=number, has_side_effects=True, vmem_limit_bytes=limit * 2**20
        ),
    )


def gather_tokens(tokens):
    rows, features = tokens.shape
    out = jax.ShapeDtypeStruct((4, 4, 4 * rows, features), tokens.dtype)
    return remote_call(tokens_kernel, out, 43, 0, 12)(tokens)


def project_kernel(x_ref, gain_ref, gate_ref, up_ref, part, squares):
    def dot(a, b):
        return lax.dot_general(a, b, (((1,), (1,)), ((), ())), preferred_element_type=jnp.float32)

    features = x_ref.shape[1]
    units = gate_ref.shape[1]
    values = x_ref[...].astype(jnp.float32)
    high, low = split(values * values)
    ones = jnp.ones((8, features), jnp.bfloat16)
    squares[...] = dot(ones, high) + dot(ones, low)
    lanes = pl.ds(pl.multiple_of(lax.axis_index("dp") * features, 128), features)
    for c in range(2):
        scaled = (values * gain_ref[c : c + 1, lanes]).astype(jnp.bfloat16)
        row = 2 * c * units
        part[pl.ds(row, units), :] = dot(gate_ref[c], scaled).astype(jnp.bfloat16)
        part[pl.ds(row + units, units), :] = dot(up_ref[c], scaled).astype(jnp.bfloat16)


def project(tokens, norm_gain, gate_weight, up_weight):
    count, features = tokens.shape
    units = gate_weight.shape[2]
    step = 256
    whole = pl.BlockSpec((2, units, features), lambda i: (0, 0, 0))
    return pl.pallas_call(
        project_kernel,
        grid=(count // step,),
        out_shape=(
            jax.ShapeDtypeStruct((4 * units, count), jnp.bfloat16),
            jax.ShapeDtypeStruct((8, count), jnp.float32),
        ),
        in_specs=[
            pl.BlockSpec((step, features), lambda i: (i, 0)),
            pl.BlockSpec(norm_gain.shape, lambda i: (0, 0)),
            whole,
            whole,
        ],
        out_specs=(
            pl.BlockSpec((4 * units, step), lambda i: (0, i)),
            pl.BlockSpec((8, step), lambda i: (0, i)),
        ),
        compiler_params=pltpu.CompilerParams(vmem_limit_bytes=40 * 2**20),
    )(tokens, norm_gain, gate_weight.swapaxes(1, 2), up_weight.swapaxes(1, 2))


def hidden_kernel(part, squares, out, near, near_sq, pair, pair_sq, far, far_sq, send_sem, recv_sem):
    x, y = grid_place()
    d = lax.axis_index("dp")
    z, core = d // 2, d % 2
    sibling, partner = {"dp": z * 2 + 1 - core}, {"dp": (1 - z) * 2 + core}
    greet([sibling, partner] + xy_neighbours(x, y))
    send = Sender(send_sem, recv_sem)
    units, tokens = out.shape[3], out.shape[4]
    chunk = tokens // 2
    step = 32

    def share(zh, side, h=None):
        start = (zh * 2 + side) * tokens
        if h is None:
            return pl.ds(pl.multiple_of(start, 128), tokens)
        return pl.ds(pl.multiple_of(start + h * chunk, 128), chunk)

    first_sq = send(squares.at[:, share(1 - z, 1 - core)], near_sq.at[1], sibling)
    first = [
        send(part.at[:, share(1 - z, 1 - core, h)], near.at[1, h], sibling) for h in range(2)
    ]
    second_sq = send(squares.at[:, share(z, 1 - core)], near_sq.at[0], sibling)
    second = [send(part.at[:, share(z, 1 - core, h)], near.at[0, h], sibling) for h in range(2)]

    first_sq.wait_recv()
    pair_sq[...] = squares[:, share(1 - z, core)] + near_sq[1]
    across_sq = send(pair_sq, far_sq, partner)
    across = []
    for h in range(2):
        first[h].wait_recv()

        @pl.loop(0, 4 * units // step)
        def _(i):
            rows = pl.ds(pl.multiple_of(i * step, step), step)
            total = part[rows, share(1 - z, core, h)].astype(jnp.float32) + near[
                1, h, rows, :
            ].astype(jnp.float32)
            pair[h, rows, :] = total.astype(jnp.bfloat16)

        across.append(send(pair.at[h], far.at[h], partner))

    second_sq.wait_recv()
    across_sq.wait_recv()
    square_total = squares[:, share(z, core)] + near_sq[0] + far_sq[...]
    root = lax.rsqrt(square_total[0:1, :] / D + EPSILON)

    def activate(h):
        second[h].wait_recv()
        across[h].wait_recv()
        lanes = pl.ds(h * chunk, chunk)
        scale = root[:, h * chunk : (h + 1) * chunk]
        for c in range(2):

            @pl.loop(0, units // step)
            def _(i):
                def total(row):
                    rows = pl.ds(pl.multiple_of(row + i * step, step), step)
                    return (
                        part[rows, share(z, core, h)].astype(jnp.float32)
                        + near[0, h, rows, :].astype(jnp.float32)
                        + far[h, rows, :].astype(jnp.float32)
                    ) * scale

                gate = total(c * 2 * units)
                up = total(c * 2 * units + units)
                value = gate / (1.0 + jnp.exp(-gate)) * up
                rows = pl.ds(pl.multiple_of(i * step, step), step)
                out[c, x, y, rows, lanes] = value.astype(jnp.bfloat16)

    part_rows = slice(None), pl.ds(0, units // 2), pl.ds(units // 2, units // 2)
    pending = []
    for h in range(2):
        activate(h)
        lanes = pl.ds(h * chunk, chunk)

        def base(i, j, p, lanes=lanes):
            return out.at[0, i, j, part_rows[p], lanes]

        def instruct(i, j, p, lanes=lanes):
            return out.at[1, j, i, part_rows[p], lanes]

        plan_a = (base, x, along_x(y), y, along_y(x))
        plan_b = (instruct, y, along_y(x), x, along_x(y))
        pending += crossed_rings(send, (plan_a, plan_b))
    for copy in pending:
        copy.wait_recv()
    send.finish()


def sum_and_gather_hidden(part, squares):
    rows, tokens = part.shape[0], part.shape[1] // lax.axis_size("dp")
    out = jax.ShapeDtypeStruct((2, 4, 4, rows // 4, tokens), jnp.bfloat16)
    scratch = [
        pltpu.VMEM((2, 2, rows, tokens // 2), jnp.bfloat16),
        pltpu.VMEM((2, 8, tokens), jnp.float32),
        pltpu.VMEM((2, rows, tokens // 2), jnp.bfloat16),
        pltpu.VMEM((8, tokens), jnp.float32),
        pltpu.VMEM((2, rows, tokens // 2), jnp.bfloat16),
        pltpu.VMEM((8, tokens), jnp.float32),
    ]
    return remote_call(hidden_kernel, out, 89, 1, 24, scratch)(part, squares)


def acts_kernel(part, out, landed, send_sem, recv_sem):
    m, d = lax.axis_index("mp"), lax.axis_index("dp")
    zh, core = d // 2, d % 2
    z = zh * 4 + m
    mates = [{"mp": (m + k) % 4} for k in range(1, 4)]

    def at(chip):
        return {"mp": chip % 4, "dp": (chip // 4) * 2 + core}

    right, left = at((z + 1) % 8), at((z + 7) % 8)
    sibling = {"dp": zh * 2 + 1 - core}
    greet(mates + [right, left, sibling])
    send = Sender(send_sem, recv_sem)
    sums = [
        [
            send(part.at[(m + k) % 4, c], landed.at[k - 1, c], mates[k - 1])
            for k in (2, 1, 3)
        ]
        for c in range(2)
    ]
    half = part.shape[2] // 2
    halves = pl.ds(0, half), pl.ds(half, half)

    def block(c, chip):
        return out.at[c, chip * 2 + core]

    shared = []
    waiting = [None, None]

    def begin(c):
        for copy in sums[c]:
            copy.wait_recv()
        total = part[m, c].astype(jnp.float32)
        for k in range(3):
            total += landed[k, c].astype(jnp.float32)
        out[c, z * 2 + core] = total.astype(jnp.bfloat16)
        here = block(c, z)
        waiting[c] = (send(here, here, right), send(here, here, left))
        shared.append(send(here, here, sibling))

    def advance(c, k):
        before, after = (z + 8 - k) % 8, (z + k) % 8
        from_left, from_right = waiting[c]
        near, next_near = block(c, before), block(c, after)
        on, back = near, next_near
        if k == 3:
            on = out.at[c, before * 2 + core, halves[0]]
            back = out.at[c, after * 2 + core, halves[1]]
        from_left.wait_recv()
        next_left = send(on, on, right)
        from_right.wait_recv()
        next_right = send(back, back, left)
        shared.append(send(near, near, sibling))
        shared.append(send(next_near, next_near, sibling))
        waiting[c] = (next_left, next_right)

    begin(0)
    advance(0, 1)
    begin(1)
    for k in range(1, 4):
        if k < 3:
            advance(0, k + 1)
        advance(1, k)
    far = (z + 4) % 8
    for c in range(2):
        for copy in waiting[c]:
            copy.wait_recv()
        shared.append(send(block(c, far), block(c, far), sibling))
    for copy in shared:
        copy.wait_recv()
    send.finish()


def sum_and_gather_acts(part):
    _, copies, rows, features = part.shape
    out = jax.ShapeDtypeStruct((copies, 16, rows, features), jnp.bfloat16)
    scratch = [pltpu.VMEM((3, copies, rows, features), jnp.bfloat16)]
    return remote_call(acts_kernel, out, 38, 2, 12, scratch)(part)


def rows_kernel(part, out, landed, send_sem, recv_sem):
    t = lax.axis_index("tensor")
    x, y = grid_place()
    m, d = lax.axis_index("mp"), lax.axis_index("dp")
    zh, core = d // 2, d % 2
    z = zh * 4 + m
    width = part.shape[3] // 2

    def column(index):
        return pl.ds(pl.multiple_of((index % 2) * width, 128), width)

    peers = [{"tensor": (t + k) % 16} for k in range(1, 16)]

    def at(chip):
        return {"mp": chip % 4, "dp": (chip // 4) * 2 + core}

    chips = [at((z + k) % 8) for k in range(1, 8)]
    sibling = {"dp": zh * 2 + 1 - core}
    greet(peers + chips + [sibling])
    send = Sender(send_sem, recv_sem)
    sums = []
    for k in range(1, 16):
        u = (t + k) % 16
        source = part.at[u // 4, (u % 4) // 2, :, column(u)]
        sums.append(send(source, landed.at[k - 1], peers[k - 1]))
    total = part[x, y // 2, :, column(y)]
    for k in range(15):
        sums[k].wait_recv()
        total += landed[k]
    out[z, core, x, y // 2, :, column(y)] = total
    own = out.at[z, core, x, y // 2, :, column(y)]
    spread = [send(own, own, chip) for chip in chips]
    for copy in spread:
        copy.wait_recv()

    low = pl.ds(0, 4), pl.ds(0, 2), pl.ds(2, 2)
    high = pl.ds(4, 4), pl.ds(4, 2), pl.ds(6, 2)

    def cell(members, i, j):
        return out.at[members, core, i, j // 2, :, column(j)]

    plan_a = (lambda i, j, p: cell(low[p], i, j), x, along_x(y), y, along_y(x))
    plan_b = (lambda i, j, p: cell(high[p], j, i), y, along_y(x), x, along_x(y))
    shared = []

    def share(shift):
        across_a = cell(low[0], slice(None), (y + shift) % 4)
        across_b = out.at[high[0], core, (x + shift) % 4]
        shared.append(send(across_a, across_a, sibling))
        shared.append(send(across_b, across_b, sibling))

    pending = crossed_rings(send, (plan_a, plan_b), lambda: share(0))
    share(3)
    share(1)
    for copy in pending:
        copy.wait_recv()
    share(2)
    for copy in shared:
        copy.wait_recv()
    send.finish()


def sum_and_gather_rows(part):
    rows, width = part.shape
    out = jax.ShapeDtypeStruct((8, 2, 4, 2, rows // 8, width), jnp.float32)
    scratch = [pltpu.VMEM((15, rows // 8, width // 2), jnp.float32)]
    full = remote_call(rows_kernel, out, 70, 3, 24, scratch)(part.reshape(4, 2, rows // 8, width))
    return full.reshape(16 * rows, width)


def products_kernel(acts, sketch, out):
    d = lax.axis_index("dp")
    core = d % 2
    z = (d // 2) * 4 + lax.axis_index("mp")
    rows = out.shape[0]
    for c in range(2):
        mine = acts[c, z, pl.ds(pl.multiple_of(core * rows, rows), rows)]
        for k in range(HALF + 1):
            other = acts[c, lax.rem(z + k, 8)]
            lanes = pl.ds((c * (HALF + 1) + k) * BLOCK, BLOCK)
            out[:, lanes] = lax.dot_general(
                mine, other, (((1,), (1,)), ((), ())), preferred_element_type=jnp.float32
            )
    lanes = pl.ds(2 * (HALF + 1) * BLOCK, sketch.shape[1])
    out[:, lanes] = jnp.dot(mine, sketch[...], preferred_element_type=jnp.float32)


def row_products(acts, sketch):
    rows = acts.shape[2] // 2
    width = 2 * (HALF + 1) * BLOCK + sketch.shape[1]
    return pl.pallas_call(
        products_kernel,
        out_shape=jax.ShapeDtypeStruct((rows, width), jnp.float32),
        in_specs=[VMEM, VMEM],
        out_specs=VMEM,
        compiler_params=pltpu.CompilerParams(vmem_limit_bytes=12 * 2**20),
    )(acts, sketch)


def against(left, right, dims):
    return lax.dot_general(left, right, (dims, ((), ())), preferred_element_type=jnp.float32)


def on_device(tokens, norm_gain, gate_weight, up_weight, down_weight, sketch):
    feature_count = tokens.shape[1]
    gathered = gather_tokens(tokens).reshape(-1, feature_count)
    count = gathered.shape[0]
    part, squares = project(gathered, norm_gain, gate_weight, up_weight)
    hidden = sum_and_gather_hidden(part, squares)
    hidden = hidden.reshape(2, -1, hidden.shape[-1])
    partial_out = jnp.stack(
        [
            against(hidden[c], down_weight[c], ((0,), (0,))).astype(jnp.bfloat16)
            for c in range(2)
        ],
        axis=1,
    )
    share_mp = lax.axis_size("mp")
    partial_out = partial_out.reshape(share_mp, -1, 2, partial_out.shape[-1]).swapaxes(1, 2)
    blocks = sum_and_gather_acts(partial_out)
    acts = blocks.reshape(2, count, -1)
    rows = row_products(blocks.reshape(2, 8, count // 8, -1), sketch)
    full = sum_and_gather_rows(rows)
    basis_share, projected = sketch_call(full, acts)
    return (basis_share.T, projected.T)


def solution(mesh):
    return jax.shard_map(
        on_device,
        mesh=mesh,
        in_specs=(
            P(("mp", "tensor"), "dp"),
            P(),
            P(None, "dp", ("mp", "tensor")),
            P(None, "dp", ("mp", "tensor")),
            P(None, "mp", "tensor"),
            P("tensor", None),
        ),
        out_specs=(P("tensor", ("mp", "dp")), P("tensor", ("mp", "dp"))),
        check_vma=False,
    )
```

```python
import functools

import jax
import jax.numpy as jnp
from jax import lax
from jax.experimental import pallas as pl
from jax.experimental.pallas import tpu as pltpu
from jax.sharding import PartitionSpec as P

D = 8192
EPSILON = 1e-05
BLOCK = 128
HALF = 4


def split(value):
    high = value.astype(jnp.bfloat16)
    return high, (value - high.astype(jnp.float32)).astype(jnp.bfloat16)


def mul(left, right, contract=((1,), (0,))):
    def dot(a, b):
        return lax.dot_general(a, b, (contract, ((), ())), preferred_element_type=jnp.float32)

    (a, a_low), (b, b_low) = left, right
    return dot(a, b) + (dot(a, b_low) + dot(a_low, b))


def reciprocal(value):
    return 1.0 / value


def inverse_factor(rows):
    lane = lax.broadcasted_iota(jnp.int32, (8, BLOCK), 1)
    sub = lax.broadcasted_iota(jnp.int32, (8, BLOCK), 0)
    rows = list(rows)
    groups = BLOCK // 8

    def spread(value):
        return jnp.broadcast_to(value, (8, BLOCK))

    out = []
    for g in range(groups):
        own = (lane >= 8 * g) & (lane < 8 * g + 8)
        cols = [[spread(rows[h][:, 8 * g + k : 8 * g + k + 1]) for k in range(8)] for h in range(g + 1, min(g + 2, groups))]
        plain = [spread(rows[g][k : k + 1, :]) for k in range(8)]
        s = [
            [spread(plain[i][:, 8 * g + k : 8 * g + k + 1]) for k in range(i + 1)] for i in range(8)
        ]
        lines = [
            jnp.where(own, (lane == 8 * g + k).astype(jnp.float32), plain[k]) for k in range(8)
        ]
        factor = [[None] * 8 for _ in range(8)]
        inv = [None] * 8
        for k in range(8):
            inv[k] = reciprocal(s[k][k])
            for i in range(k + 1, 8):
                factor[i][k] = s[i][k] * inv[k]
            for i in range(k + 1, 8):
                for n in range(k + 1, i + 1):
                    s[i][n] = s[i][n] - factor[i][k] * s[n][k]
        for k in range(8):
            for i in range(k + 1, 8):
                lines[i] = lines[i] - factor[i][k] * lines[k]
        solved = [lines[k] * inv[k] for k in range(8)]
        for i in range(7, 0, -1):
            for k in range(i):
                solved[k] = solved[k] - factor[i][k] * solved[i]
        for h in range(g + 1, min(g + 2, groups)):
            value = jnp.where(own, 0.0, rows[h])
            c = cols[h - g - 1]
            first = (c[0] * solved[0] + c[1] * solved[1]) + (c[2] * solved[2] + c[3] * solved[3])
            second = (c[4] * solved[4] + c[5] * solved[5]) + (c[6] * solved[6] + c[7] * solved[7])
            rows[h] = value - (first + second)
        if g + 2 < groups:
            tight = solved[0]
            for k in range(1, 8):
                tight = jnp.where(sub == k, solved[k], tight)
            zero = jnp.zeros_like(tight)
            wide = jnp.concatenate([tight if n == g else zero for n in range(groups)], axis=0)
            tall = jnp.concatenate(rows[g + 2 :], axis=0)
            change = mul(split(tall), split(wide))
            for h in range(g + 2, groups):
                n = 8 * (h - g - 2)
                rows[h] = jnp.where(own, 0.0, rows[h]) - change[n : n + 8, :]
        row = lines[0] * jnp.sqrt(inv[0])
        for k in range(1, 8):
            row = jnp.where(sub == k, lines[k] * jnp.sqrt(inv[k]), row)
        out.append(jnp.where(lane <= sub + 8 * g, row, 0.0))
    return jnp.concatenate(out, axis=0)


def orth_factor(gram, low_inv):
    n = gram.shape[0]
    blocks = n // BLOCK
    low_inv[...] = jnp.zeros_like(low_inv)
    at = [pl.ds(k * BLOCK, BLOCK) for k in range(blocks)]

    def diagonal(k):
        return [gram[pl.ds(k * BLOCK + 8 * g, 8), at[k]] for g in range(BLOCK // 8)]

    inv = inverse_factor(diagonal(0))
    for k in range(blocks):
        inv_s = split(inv)
        low_inv[at[k], at[k]] = inv
        panel = {}
        if k + 1 < blocks:
            panel[k + 1] = split(mul(inv_s, split(gram[at[k], at[k + 1]])))
            gram[at[k + 1], at[k + 1]] -= mul(panel[k + 1], panel[k + 1], ((0,), (0,)))
            following = inverse_factor(diagonal(k + 1))
        if k:
            before = pl.ds(0, k * BLOCK)
            low_inv[at[k], before] = mul(inv_s, split(low_inv[at[k], before]))
        so_far = pl.ds(0, (k + 1) * BLOCK)
        mine = split(low_inv[at[k], so_far])
        for i in range(k + 1, blocks):
            if i not in panel:
                panel[i] = split(mul(inv_s, split(gram[at[k], at[i]])))
            low_inv[at[i], so_far] -= mul(panel[i], mine, ((0,), (0,)))
            for j in range(i, blocks):
                if j not in panel:
                    panel[j] = split(mul(inv_s, split(gram[at[k], at[j]])))
                if (i, j) != (k + 1, k + 1):
                    gram[at[i], at[j]] -= mul(panel[i], panel[j], ((0,), (0,)))
        if k + 1 < blocks:
            inv = following


def fill_grams(full, g_high, g_low):
    @pl.loop(0, 2 * HALF)
    def _(z):
        here = pl.ds(pl.multiple_of(z * BLOCK, BLOCK), BLOCK)
        for c in range(2):
            for k in range(HALF + 1):
                there = pl.ds(pl.multiple_of(((z + k) % 8) * BLOCK, BLOCK), BLOCK)
                value = full[here, pl.ds((c * (HALF + 1) + k) * BLOCK, BLOCK)]
                g_high[c, here, there], g_low[c, here, there] = split(value)
                if 0 < k < HALF:
                    g_high[c, there, here], g_low[c, there, here] = split(value.T)


def sketch_kernel(full, acts, basis_out, last_out, gram, low_inv, high_z, low_z, g_high, g_low):
    tokens = full.shape[0]
    rank = gram.shape[0]
    share = basis_out.shape[0]
    high, low = split(full[:, pl.ds(2 * (HALF + 1) * BLOCK, rank)])
    high_z[...] = high
    low_z[...] = low
    fill_grams(full, g_high, g_low)

    def step(n, carry):
        z_s = (high_z[...], low_z[...])
        h = mul((g_high[n % 2], g_low[n % 2]), z_s)
        gram[...] = mul(z_s, split(h), ((0,), (0,))) * (2.0**-33)
        orth_factor(gram, low_inv)

        @pl.when(n < 2)
        def _():
            high, low = split(mul(split(h * (1.0 / 1024)), split(low_inv[...]), ((1,), (1,))))
            high_z[...] = high
            low_z[...] = low

        return carry

    lax.fori_loop(0, 3, step, 0)
    index = lax.axis_index("mp") * 4 + lax.axis_index("dp")
    rows = low_inv[pl.ds(pl.multiple_of(index * share, share), share), :]
    coeff = split(mul(split(rows), (high_z[...], low_z[...]), ((1,), (1,))) * (1.0 / 1024))
    last = split(mul(coeff, (g_high[0], g_low[0])) * (1.0 / 1024))

    def apply(pair, c):
        def dot(a):
            return jnp.dot(a, acts[c], preferred_element_type=jnp.float32)

        return dot(pair[0]) + dot(pair[1])

    basis_out[...] = apply(coeff, 0)
    last_out[...] = apply(last, 1)


def sketch_call(full, acts):
    tokens = full.shape[0]
    rank = full.shape[1] - 2 * (HALF + 1) * BLOCK
    features = acts.shape[2]
    shape = jax.ShapeDtypeStruct((rank // 16, features), jnp.float32)
    return pl.pallas_call(
        sketch_kernel,
        out_shape=(shape, shape),
        in_specs=[pl.BlockSpec(memory_space=pltpu.VMEM)] * 2,
        out_specs=(pl.BlockSpec(memory_space=pltpu.VMEM),) * 2,
        scratch_shapes=[
            pltpu.VMEM((rank, rank), jnp.float32),
            pltpu.VMEM((rank, rank), jnp.float32),
            pltpu.VMEM((tokens, rank), jnp.bfloat16),
            pltpu.VMEM((tokens, rank), jnp.bfloat16),
            pltpu.VMEM((2, tokens, tokens), jnp.bfloat16),
            pltpu.VMEM((2, tokens, tokens), jnp.bfloat16),
        ],
        compiler_params=pltpu.CompilerParams(vmem_limit_bytes=36 * 2**20),
    )(full, acts)


MESH = pl.DeviceIdType.MESH
VMEM = pl.BlockSpec(memory_space=pltpu.VMEM)


class Sender:
    def __init__(self, send, recv):
        self.send, self.recv, self.all = send, recv, []

    def __call__(self, source, target, device):
        n = len(self.all)
        copy = pltpu.make_async_remote_copy(
            src_ref=source,
            dst_ref=target,
            send_sem=self.send.at[n],
            recv_sem=self.recv.at[n],
            device_id=device,
            device_id_type=MESH,
        )
        copy.start()
        self.all.append(copy)
        return copy

    def finish(self):
        for copy in self.all:
            copy.wait_send()


def greet(peers):
    barrier = pltpu.get_barrier_semaphore()
    for peer in peers:
        pl.semaphore_signal(barrier, inc=1, device_id=peer, device_id_type=MESH)
    pl.semaphore_wait(barrier, len(peers))


def grid_place():
    t = lax.axis_index("tensor")
    return t // 4, t % 4


def ring(send, block, upper, lower, me, toward):
    right, left = (me + 1) % 4, (me + 3) % 4
    from_left = send(block(me), block(me), toward(right))
    from_right = send(block(me), block(me), toward(left))

    def forward():
        from_left.wait_recv()
        first = send(upper(left), upper(left), toward(right))
        from_right.wait_recv()
        second = send(lower(right), lower(right), toward(left))
        return first, second

    return forward


def crossed_rings(send, plans, middle=None):
    def along_first(plan):
        cell, me, toward, me_next, _ = plan
        return ring(send, *(lambda i, p=p: cell(i, me_next, p) for p in range(3)), me, toward)

    def along_second(plan, shift):
        cell, me, _, me_next, toward_next = plan
        i = (me + shift) % 4
        return ring(send, *(lambda j, p=p: cell(i, j, p) for p in range(3)), me_next, toward_next)

    first = [along_first(plan) for plan in plans]
    own = [along_second(plan, 0) for plan in plans]
    last = [copy for forward in first for copy in forward()]
    sides = [along_second(plan, shift) for shift in (3, 1) for plan in plans]
    pending = [copy for forward in own for copy in forward()]
    for copy in last:
        copy.wait_recv()
    opposite = [along_second(plan, 2) for plan in plans]
    if middle is not None:
        middle()
    for forward in sides + opposite:
        pending += forward()
    return pending


def along_x(y):
    return lambda i: {"tensor": i * 4 + y}


def along_y(x):
    return lambda i: {"tensor": x * 4 + i}


def xy_neighbours(x, y):
    return [
        {"tensor": ((x + 1) % 4) * 4 + y},
        {"tensor": ((x + 3) % 4) * 4 + y},
        {"tensor": x * 4 + (y + 1) % 4},
        {"tensor": x * 4 + (y + 3) % 4},
    ]


def tokens_kernel(x_ref, out, send_sem, recv_sem):
    x, y = grid_place()
    m = lax.axis_index("mp")
    mates = [{"mp": (m + d) % 4} for d in range(1, 4)]
    greet(mates + xy_neighbours(x, y))
    send = Sender(send_sem, recv_sem)
    rows = x_ref.shape[0]
    half = x_ref.shape[1] // 2
    mine = pl.ds(pl.multiple_of(m * rows, rows), rows)
    first = [send(x_ref, out.at[x, y, mine], mate) for mate in mates]
    out[x, y, mine] = x_ref[...]
    for copy in first:
        copy.wait_recv()
    count = 4 * rows
    a, b = pl.ds(0, half), pl.ds(half, half)
    up, down = pl.ds(0, count // 2), pl.ds(count // 2, count // 2)
    part = slice(None), up, down
    plan_a = (lambda i, j, p: out.at[i, j, part[p], a], x, along_x(y), y, along_y(x))
    plan_b = (lambda i, j, p: out.at[j, i, part[p], b], y, along_y(x), x, along_x(y))
    for copy in crossed_rings(send, (plan_a, plan_b)):
        copy.wait_recv()
    send.finish()


def remote_call(kernel, out_shape, copies, number, limit, scratch=()):
    return pl.pallas_call(
        kernel,
        out_shape=out_shape,
        out_specs=VMEM,
        scratch_shapes=[
            *scratch,
            pltpu.SemaphoreType.DMA((copies,)),
            pltpu.SemaphoreType.DMA((copies,)),
        ],
        compiler_params=pltpu.CompilerParams(
            collective_id=number, has_side_effects=True, vmem_limit_bytes=limit * 2**20
        ),
    )


def gather_tokens(tokens):
    rows, features = tokens.shape
    out = jax.ShapeDtypeStruct((4, 4, 4 * rows, features), tokens.dtype)
    return remote_call(tokens_kernel, out, 43, 0, 12)(tokens)


def project_kernel(x_ref, gain_ref, gate_ref, up_ref, part, squares):
    def dot(a, b):
        return lax.dot_general(a, b, (((1,), (1,)), ((), ())), preferred_element_type=jnp.float32)

    features = x_ref.shape[1]
    units = gate_ref.shape[1]
    values = x_ref[...].astype(jnp.float32)
    high, low = split(values * values)
    ones = jnp.ones((8, features), jnp.bfloat16)
    squares[...] = dot(ones, high) + dot(ones, low)
    lanes = pl.ds(pl.multiple_of(lax.axis_index("dp") * features, 128), features)
    for c in range(2):
        scaled = (values * gain_ref[c : c + 1, lanes]).astype(jnp.bfloat16)
        row = 2 * c * units
        part[pl.ds(row, units), :] = dot(gate_ref[c], scaled).astype(jnp.bfloat16)
        part[pl.ds(row + units, units), :] = dot(up_ref[c], scaled).astype(jnp.bfloat16)


def project(tokens, norm_gain, gate_weight, up_weight):
    count, features = tokens.shape
    units = gate_weight.shape[2]
    step = 256
    whole = pl.BlockSpec((2, units, features), lambda i: (0, 0, 0))
    return pl.pallas_call(
        project_kernel,
        grid=(count // step,),
        out_shape=(
            jax.ShapeDtypeStruct((4 * units, count), jnp.bfloat16),
            jax.ShapeDtypeStruct((8, count), jnp.float32),
        ),
        in_specs=[
            pl.BlockSpec((step, features), lambda i: (i, 0)),
            pl.BlockSpec(norm_gain.shape, lambda i: (0, 0)),
            whole,
            whole,
        ],
        out_specs=(
            pl.BlockSpec((4 * units, step), lambda i: (0, i)),
            pl.BlockSpec((8, step), lambda i: (0, i)),
        ),
        compiler_params=pltpu.CompilerParams(vmem_limit_bytes=40 * 2**20),
    )(tokens, norm_gain, gate_weight.swapaxes(1, 2), up_weight.swapaxes(1, 2))


def hidden_kernel(part, squares, out, near, near_sq, pair, pair_sq, far, far_sq, send_sem, recv_sem):
    x, y = grid_place()
    d = lax.axis_index("dp")
    z, core = d // 2, d % 2
    sibling, partner = {"dp": z * 2 + 1 - core}, {"dp": (1 - z) * 2 + core}
    greet([sibling, partner] + xy_neighbours(x, y))
    send = Sender(send_sem, recv_sem)
    units, tokens = out.shape[3], out.shape[4]
    chunk = tokens // 2
    step = 32

    def share(zh, side, h=None):
        start = (zh * 2 + side) * tokens
        if h is None:
            return pl.ds(pl.multiple_of(start, 128), tokens)
        return pl.ds(pl.multiple_of(start + h * chunk, 128), chunk)

    first_sq = send(squares.at[:, share(1 - z, 1 - core)], near_sq.at[1], sibling)
    first = [
        send(part.at[:, share(1 - z, 1 - core, h)], near.at[1, h], sibling) for h in range(2)
    ]
    second_sq = send(squares.at[:, share(z, 1 - core)], near_sq.at[0], sibling)
    second = [send(part.at[:, share(z, 1 - core, h)], near.at[0, h], sibling) for h in range(2)]

    first_sq.wait_recv()
    pair_sq[...] = squares[:, share(1 - z, core)] + near_sq[1]
    across_sq = send(pair_sq, far_sq, partner)
    across = []
    for h in range(2):
        first[h].wait_recv()

        @pl.loop(0, 4 * units // step)
        def _(i):
            rows = pl.ds(pl.multiple_of(i * step, step), step)
            total = part[rows, share(1 - z, core, h)].astype(jnp.float32) + near[
                1, h, rows, :
            ].astype(jnp.float32)
            pair[h, rows, :] = total.astype(jnp.bfloat16)

        across.append(send(pair.at[h], far.at[h], partner))

    second_sq.wait_recv()
    across_sq.wait_recv()
    square_total = squares[:, share(z, core)] + near_sq[0] + far_sq[...]
    root = lax.rsqrt(square_total[0:1, :] / D + EPSILON)

    def activate(h):
        second[h].wait_recv()
        across[h].wait_recv()
        lanes = pl.ds(h * chunk, chunk)
        scale = root[:, h * chunk : (h + 1) * chunk]
        for c in range(2):

            @pl.loop(0, units // step)
            def _(i):
                def total(row):
                    rows = pl.ds(pl.multiple_of(row + i * step, step), step)
                    return (
                        part[rows, share(z, core, h)].astype(jnp.float32)
                        + near[0, h, rows, :].astype(jnp.float32)
                        + far[h, rows, :].astype(jnp.float32)
                    ) * scale

                gate = total(c * 2 * units)
                up = total(c * 2 * units + units)
                value = gate / (1.0 + jnp.exp(-gate)) * up
                rows = pl.ds(pl.multiple_of(i * step, step), step)
                out[c, x, y, rows, lanes] = value.astype(jnp.bfloat16)

    part_rows = slice(None), pl.ds(0, units // 2), pl.ds(units // 2, units // 2)
    pending = []
    for h in range(2):
        activate(h)
        lanes = pl.ds(h * chunk, chunk)

        def base(i, j, p, lanes=lanes):
            return out.at[0, i, j, part_rows[p], lanes]

        def instruct(i, j, p, lanes=lanes):
            return out.at[1, j, i, part_rows[p], lanes]

        plan_a = (base, x, along_x(y), y, along_y(x))
        plan_b = (instruct, y, along_y(x), x, along_x(y))
        pending += crossed_rings(send, (plan_a, plan_b))
    for copy in pending:
        copy.wait_recv()
    send.finish()


def sum_and_gather_hidden(part, squares):
    rows, tokens = part.shape[0], part.shape[1] // lax.axis_size("dp")
    out = jax.ShapeDtypeStruct((2, 4, 4, rows // 4, tokens), jnp.bfloat16)
    scratch = [
        pltpu.VMEM((2, 2, rows, tokens // 2), jnp.bfloat16),
        pltpu.VMEM((2, 8, tokens), jnp.float32),
        pltpu.VMEM((2, rows, tokens // 2), jnp.bfloat16),
        pltpu.VMEM((8, tokens), jnp.float32),
        pltpu.VMEM((2, rows, tokens // 2), jnp.bfloat16),
        pltpu.VMEM((8, tokens), jnp.float32),
    ]
    return remote_call(hidden_kernel, out, 89, 1, 24, scratch)(part, squares)


def acts_kernel(part, out, landed, send_sem, recv_sem):
    m, d = lax.axis_index("mp"), lax.axis_index("dp")
    zh, core = d // 2, d % 2
    z = zh * 4 + m
    mates = [{"mp": (m + k) % 4} for k in range(1, 4)]

    def at(chip):
        return {"mp": chip % 4, "dp": (chip // 4) * 2 + core}

    right, left = at((z + 1) % 8), at((z + 7) % 8)
    sibling = {"dp": zh * 2 + 1 - core}
    greet(mates + [right, left, sibling])
    send = Sender(send_sem, recv_sem)
    sums = [
        [
            send(part.at[(m + k) % 4, c], landed.at[k - 1, c], mates[k - 1])
            for k in (2, 1, 3)
        ]
        for c in range(2)
    ]
    half = part.shape[2] // 2
    halves = pl.ds(0, half), pl.ds(half, half)

    def block(c, chip):
        return out.at[c, chip * 2 + core]

    shared = []
    waiting = []
    for c in range(2):
        for copy in sums[c]:
            copy.wait_recv()
        total = part[m, c].astype(jnp.float32)
        for k in range(3):
            total += landed[k, c].astype(jnp.float32)
        out[c, z * 2 + core] = total.astype(jnp.bfloat16)
        here = block(c, z)
        waiting.append((send(here, here, right), send(here, here, left)))
        shared.append(send(here, here, sibling))
    for k in range(1, 4):
        before, after = (z + 8 - k) % 8, (z + k) % 8
        for c in range(2):
            from_left, from_right = waiting[c]
            near, next_near = block(c, before), block(c, after)
            on, back = near, next_near
            if k == 3:
                on = out.at[c, before * 2 + core, halves[0]]
                back = out.at[c, after * 2 + core, halves[1]]
            from_left.wait_recv()
            next_left = send(on, on, right)
            from_right.wait_recv()
            next_right = send(back, back, left)
            shared.append(send(near, near, sibling))
            shared.append(send(next_near, next_near, sibling))
            waiting[c] = (next_left, next_right)
    far = (z + 4) % 8
    for c in range(2):
        for copy in waiting[c]:
            copy.wait_recv()
        shared.append(send(block(c, far), block(c, far), sibling))
    for copy in shared:
        copy.wait_recv()
    send.finish()


def sum_and_gather_acts(part):
    _, copies, rows, features = part.shape
    out = jax.ShapeDtypeStruct((copies, 16, rows, features), jnp.bfloat16)
    scratch = [pltpu.VMEM((3, copies, rows, features), jnp.bfloat16)]
    return remote_call(acts_kernel, out, 38, 2, 12, scratch)(part)


def rows_kernel(part, out, landed, send_sem, recv_sem):
    t = lax.axis_index("tensor")
    x, y = grid_place()
    m, d = lax.axis_index("mp"), lax.axis_index("dp")
    zh, core = d // 2, d % 2
    z = zh * 4 + m
    width = part.shape[3] // 2

    def column(index):
        return pl.ds(pl.multiple_of((index % 2) * width, 128), width)

    peers = [{"tensor": (t + k) % 16} for k in range(1, 16)]

    def at(chip):
        return {"mp": chip % 4, "dp": (chip // 4) * 2 + core}

    chips = [at((z + k) % 8) for k in (4, 3, 5, 2, 6, 1, 7)]
    sibling = {"dp": zh * 2 + 1 - core}
    greet(peers + chips + [sibling])
    send = Sender(send_sem, recv_sem)
    sums = []
    for k in range(1, 16):
        u = (t + k) % 16
        source = part.at[u // 4, (u % 4) // 2, :, column(u)]
        sums.append(send(source, landed.at[k - 1], peers[k - 1]))
    total = part[x, y // 2, :, column(y)]
    for k in range(15):
        sums[k].wait_recv()
        total += landed[k]
    out[z, core, x, y // 2, :, column(y)] = total
    own = out.at[z, core, x, y // 2, :, column(y)]
    spread = [send(own, own, chip) for chip in chips]
    for copy in spread:
        copy.wait_recv()

    low = pl.ds(0, 4), pl.ds(0, 2), pl.ds(2, 2)
    high = pl.ds(4, 4), pl.ds(4, 2), pl.ds(6, 2)

    def cell(members, i, j):
        return out.at[members, core, i, j // 2, :, column(j)]

    plan_a = (lambda i, j, p: cell(low[p], i, j), x, along_x(y), y, along_y(x))
    plan_b = (lambda i, j, p: cell(high[p], j, i), y, along_y(x), x, along_x(y))
    shared = []

    def share(shift):
        across_a = cell(low[0], slice(None), (y + shift) % 4)
        across_b = out.at[high[0], core, (x + shift) % 4]
        shared.append(send(across_a, across_a, sibling))
        shared.append(send(across_b, across_b, sibling))

    pending = crossed_rings(send, (plan_a, plan_b), lambda: share(0))
    share(3)
    share(1)
    for copy in pending:
        copy.wait_recv()
    share(2)
    for copy in shared:
        copy.wait_recv()
    send.finish()


def sum_and_gather_rows(part):
    rows, width = part.shape
    out = jax.ShapeDtypeStruct((8, 2, 4, 2, rows // 8, width), jnp.float32)
    scratch = [pltpu.VMEM((15, rows // 8, width // 2), jnp.float32)]
    full = remote_call(rows_kernel, out, 70, 3, 24, scratch)(part.reshape(4, 2, rows // 8, width))
    return full.reshape(16 * rows, width)


def products_kernel(acts, sketch, out):
    d = lax.axis_index("dp")
    core = d % 2
    z = (d // 2) * 4 + lax.axis_index("mp")
    rows = out.shape[0]
    for c in range(2):
        mine = acts[c, z, pl.ds(pl.multiple_of(core * rows, rows), rows)]
        for k in range(HALF + 1):
            other = acts[c, lax.rem(z + k, 8)]
            lanes = pl.ds((c * (HALF + 1) + k) * BLOCK, BLOCK)
            out[:, lanes] = lax.dot_general(
                mine, other, (((1,), (1,)), ((), ())), preferred_element_type=jnp.float32
            )
    lanes = pl.ds(2 * (HALF + 1) * BLOCK, sketch.shape[1])
    out[:, lanes] = jnp.dot(mine, sketch[...], preferred_element_type=jnp.float32)


def row_products(acts, sketch):
    rows = acts.shape[2] // 2
    width = 2 * (HALF + 1) * BLOCK + sketch.shape[1]
    return pl.pallas_call(
        products_kernel,
        out_shape=jax.ShapeDtypeStruct((rows, width), jnp.float32),
        in_specs=[VMEM, VMEM],
        out_specs=VMEM,
        compiler_params=pltpu.CompilerParams(vmem_limit_bytes=12 * 2**20),
    )(acts, sketch)


def against(left, right, dims):
    return lax.dot_general(left, right, (dims, ((), ())), preferred_element_type=jnp.float32)


def on_device(tokens, norm_gain, gate_weight, up_weight, down_weight, sketch):
    feature_count = tokens.shape[1]
    gathered = gather_tokens(tokens).reshape(-1, feature_count)
    count = gathered.shape[0]
    part, squares = project(gathered, norm_gain, gate_weight, up_weight)
    hidden = sum_and_gather_hidden(part, squares)
    hidden = hidden.reshape(2, -1, hidden.shape[-1])
    partial_out = jnp.stack(
        [
            against(hidden[c], down_weight[c], ((0,), (0,))).astype(jnp.bfloat16)
            for c in range(2)
        ],
        axis=1,
    )
    share_mp = lax.axis_size("mp")
    partial_out = partial_out.reshape(share_mp, -1, 2, partial_out.shape[-1]).swapaxes(1, 2)
    blocks = sum_and_gather_acts(partial_out)
    acts = blocks.reshape(2, count, -1)
    rows = row_products(blocks.reshape(2, 8, count // 8, -1), sketch)
    full = sum_and_gather_rows(rows)
    basis_share, projected = sketch_call(full, acts)
    return (basis_share.T, projected.T)


def solution(mesh):
    return jax.shard_map(
        on_device,
        mesh=mesh,
        in_specs=(
            P(("mp", "tensor"), "dp"),
            P(),
            P(None, "dp", ("mp", "tensor")),
            P(None, "dp", ("mp", "tensor")),
            P(None, "mp", "tensor"),
            P("tensor", None),
        ),
        out_specs=(P("tensor", ("mp", "dp")), P("tensor", ("mp", "dp"))),
        check_vma=False,
    )
```
